32 devices in a mesh: gx: 8 (over y, x, core), gy: 4 (over z).
Axes of the slice: x: 2, y: 2, z: 4, core: 2. Of those that a mesh axis runs over, the one named last changes fastest.
Arguments:
- start: float32 [16, 4, 1024], P('gx', 'gy'), may hold values from -6 to 6
- source: float32 [16, 4, 1024], P('gx', 'gy'), may hold values from -4 to 4
- diag_inverse: bfloat16 [16, 4, 16, 4096], P('gx', 'gy'), may hold values from -0.75 to 0.75
- x_lower: bfloat16 [16, 4, 16, 4096], P('gx', 'gy'), may hold values from -1 to 1
- x_upper: bfloat16 [16, 4, 16, 4096], P('gx', 'gy'), may hold values from -1 to 1
- side_blocks: bfloat16 [4, 16, 4, 16, 4096], P(None, 'gx', 'gy'), may hold values from -0.25 to 0.25
Outputs:
- forward: float32 [16, 4, 1024], P('gx', 'gy')
- result: float32 [16, 4, 1024], P('gx', 'gy')
The draws below stay inside these ranges and needn't reach their ends.
All inputs are finite; a program needn't handle non-finite values.
Results may differ from the reference program's by a relative error of at most 0.0003.
Values sent between devices are 32-bit elements; how exact they have to be, the bound alone decides.
No kernel may reach another device: no remote copies, remote signals or barrier semaphores. Data moves between devices by JAX's collectives and lax.ppermute only.
A program may use at most 64 MiB of HBM per device.

```python
import math
import jax
import jax.numpy as jnp
from jax import lax

S = 64
NZ = 16
CELLS_FIRST_AXIS = 16
NY = 4


def coupling(key, salt):
    key = jax.random.fold_in(key, salt)
    random_keys = jax.random.split(key, 6)
    order = jax.random.permutation(random_keys[0], S)
    share = S // 2
    slow = order < share
    decay = jnp.exp(jax.random.uniform(random_keys[1], (CELLS_FIRST_AXIS, NY, NZ, S), jnp.float32, math.log(0.7), math.log(2.3)))
    gentle_reaction_rate = jnp.exp(-decay / CELLS_FIRST_AXIS)
    sudden_pulse = jax.random.bernoulli(random_keys[2], 3.0 / CELLS_FIRST_AXIS, (CELLS_FIRST_AXIS, 1, 1, 1))
    residual_error = jax.random.uniform(random_keys[3], (CELLS_FIRST_AXIS, 1, 1, 1), jnp.float32, 0.5, 0.8)
    gentle_reaction_rate = gentle_reaction_rate * jnp.where(sudden_pulse, residual_error, 1.0)
    fast_rate = jax.random.uniform(random_keys[4], (CELLS_FIRST_AXIS, NY, NZ, S), jnp.float32, 0.1, 0.5)
    rate = jnp.where(slow, gentle_reaction_rate, fast_rate)
    noise = jnp.clip(jax.random.normal(random_keys[5], (CELLS_FIRST_AXIS, NY, NZ, S, S), jnp.float32), -4.0, 4.0)
    spread = jnp.where(slow, 0.003, 0.06)[:, None]
    unit_matrix = jnp.eye(S, dtype=jnp.float32)
    matrix = noise * spread * (1.0 - unit_matrix) + rate[..., None] * unit_matrix
    return (-matrix).reshape(CELLS_FIRST_AXIS, NY, NZ, S * S).astype(jnp.bfloat16)


def draw_x_lower(key, part):
    return coupling(key, 11)


def draw_x_upper(key, part):
    return coupling(key, 23)


def steps_of(stream_key, dims, pieces, smallest, largest):
    loudness, own = 1.0, jax.random.fold_in(stream_key, 6)
    for dim, blocks in pieces:
        heights = jnp.exp(jax.random.uniform(jax.random.fold_in(own, dim), (blocks,), jnp.float32, smallest / len(pieces), largest / len(pieces)))
        loudness = loudness * jnp.repeat(heights, dims[dim] // blocks).reshape([-1 if axis == dim else 1 for axis in range(len(dims))])
    return loudness


def centred(stream_key, dims, scale, bound, pieces=(), kind=jnp.bfloat16):
    gain = steps_of(stream_key, dims, pieces, -0.22, 0.18) if pieces else 1.0
    values = jax.random.normal(stream_key, dims, jnp.float32) * scale * gain
    return jnp.minimum(jnp.maximum(values, -bound), bound).astype(kind)


def setup_inputs(seed: int = 0) -> dict:
    splits = jax.random.split(jax.random.key(seed), 7)
    start = centred(splits[0], (CELLS_FIRST_AXIS, NY, NZ * S), 0.5, 6.0, ((0, 8), (1, 4)), jnp.float32)
    source = centred(splits[1], (CELLS_FIRST_AXIS, NY, NZ * S), 0.25, 4.0, ((0, 8), (1, 4)), jnp.float32)
    diag_inverse = centred(splits[2], (CELLS_FIRST_AXIS, NY, NZ, S * S), S ** -0.5, 0.75, ((0, 8), (1, 4)))
    x_lower = draw_x_lower(jax.random.fold_in(splits[6], 71), 0)
    x_upper = draw_x_upper(jax.random.fold_in(splits[6], 71), 0)
    side_blocks = centred(splits[5], (4, CELLS_FIRST_AXIS, NY, NZ, S * S), (8 * S) ** -0.5, 0.25, ((1, 8), (2, 4)))
    return dict(start=start, source=source, diag_inverse=diag_inverse, x_lower=x_lower, x_upper=x_upper, side_blocks=side_blocks)


def apply_block(block, column_values):
    lead = column_values.shape[:-1]
    depth = block.shape[-2]
    width = column_values.shape[-1] // depth
    matrix = block.astype(jnp.float32).reshape(lead + (depth, width, width))
    column = column_values.reshape(lead + (depth, width))
    product = jnp.einsum("...zab,...zb->...za", matrix, column, precision=lax.Precision.HIGHEST)
    return product.reshape(lead + (depth * width,))


def z_terms(side_blocks, column_values, depth):
    width = column_values.shape[-1] // depth
    cells = column_values.reshape(column_values.shape[:-1] + (depth, width))
    zero = jnp.zeros_like(cells[..., :1, :])
    below = jnp.concatenate([zero, cells[..., :-1, :]], -2).reshape(column_values.shape)
    above = jnp.concatenate([cells[..., 1:, :], zero], -2).reshape(column_values.shape)
    return apply_block(side_blocks[2], below) + apply_block(side_blocks[3], above)


def reference(start, source, diag_inverse, x_lower, x_upper, side_blocks):
    depth = NZ
    rhs = apply_block(diag_inverse, source)

    def sideways_coupling(column_values):
        padded = jnp.pad(column_values, ((0, 0), (1, 1), (0, 0)))
        total = apply_block(side_blocks[0], padded[:, :-2]) + apply_block(side_blocks[1], padded[:, 2:])
        return total + z_terms(side_blocks, column_values, depth)

    ahead = jnp.concatenate([start[1:], jnp.zeros_like(start[:1])], 0)
    drive_f = rhs - sideways_coupling(start) - apply_block(x_upper, ahead)

    def advance(previous, inputs):
        drive, block = inputs
        fresh = drive - apply_block(block, previous)
        return fresh, fresh

    initial = jnp.zeros(start.shape[1:], jnp.float32)
    _, forward = lax.scan(advance, initial, (drive_f, x_lower))
    behind = jnp.concatenate([jnp.zeros_like(forward[:1]), forward[:-1]], 0)
    drive_b = rhs - sideways_coupling(forward) - apply_block(x_lower, behind)
    _, reverse_out = lax.scan(advance, initial, (drive_b[::-1], x_upper[::-1]))
    result = reverse_out[::-1]
    return forward, result
```

```python
import functools

import jax
import jax.numpy as jnp
from jax import lax
from jax.experimental import pallas as pl
from jax.experimental.pallas import tpu as pltpu
from jax.sharding import PartitionSpec as P

LANES = 128
F32 = jnp.float32
BF16 = jnp.bfloat16


def lane_bit(shape, shift):
    return (lax.broadcasted_iota(jnp.int32, shape, len(shape) - 1) & shift) != 0


def segment_sums(leaf, tiles, rows):
    shape = (rows, LANES)

    def node(base, stride, shift):
        if stride == tiles:
            return leaf(base)
        low = node(base, stride * 2, shift * 2)
        high = node(base + stride, stride * 2, shift * 2)
        low = low + pltpu.roll(low, LANES - shift, 1)
        high = high + pltpu.roll(high, shift, 1)
        return jnp.where(lane_bit(shape, shift), high, low)

    part = node(0, 1, 2)
    odd = lane_bit(shape, 1)
    part = part + jnp.where(odd, pltpu.roll(part, 1, 1), pltpu.roll(part, LANES - 1, 1))
    upper = lane_bit(shape, LANES // 2)
    return jnp.where(upper == odd, part, pltpu.roll(part, LANES // 2, 1))


def apply(terms):
    rows = terms[0][1].shape[0]
    tiles = LANES // 4

    def leaf(t):
        return sum(read(t).astype(F32) * vector for read, vector in terms)

    return segment_sums(leaf, tiles, rows)


def reader(ref, *index):
    return lambda t: ref[(*index, slice(None), slice(t * LANES, (t + 1) * LANES))]


def spread(scratch, raw):
    upper = lane_bit(raw.shape, LANES // 2)
    other = pltpu.roll(raw, LANES // 2, 1)
    half = raw.shape[0]
    scratch[pl.ds(0, half, stride=2), :] = jnp.where(upper, other, raw)
    scratch[pl.ds(1, half, stride=2), :] = jnp.where(upper, raw, other)
    return scratch[...]


def gather_pairs(scratch, vector):
    scratch[...] = vector
    half = vector.shape[0] // 2
    even = scratch[pl.ds(0, half, stride=2), :]
    odd = scratch[pl.ds(1, half, stride=2), :]
    return jnp.where(lane_bit(even.shape, LANES // 2), odd, even)


def shifted(vector, down):
    rows = vector.shape[0]
    row = lax.broadcasted_iota(jnp.int32, vector.shape, 0)
    if down:
        return jnp.where(row == 0, 0.0, pltpu.roll(vector, 1, 0))
    return jnp.where(row == rows - 1, 0.0, pltpu.roll(vector, rows - 1, 0))


def to_rows(scratch, read, rows, species):
    for a in range(species):
        tile = read(a // 2).astype(F32)
        if a % 2:
            tile = pltpu.roll(tile, LANES // 2, 1)
        scratch[pl.ds(a, rows, stride=species), :] = tile


def from_rows(scratch, out, index, rows, species):
    upper = lane_bit((rows, LANES), LANES // 2)
    for t in range(species // 2):
        even = scratch[pl.ds(2 * t, rows, stride=species), :]
        odd = scratch[pl.ds(2 * t + 1, rows, stride=species), :]
        out[(*index, slice(None), slice(t * LANES, (t + 1) * LANES))] = jnp.where(upper, odd, even)


def twice(a):
    return jnp.concatenate([a, a], 1)


def halves(a):
    high = a.astype(BF16)
    return high, (a - high.astype(F32)).astype(BF16)


def dot(a, b):
    return jnp.dot(a, b, preferred_element_type=F32)


def prep_kernel(lower, upper, out, first, second):
    planes, _, rows, width = lower.shape
    species = LANES // 2
    for side, blocks, order in ((0, lower, range(planes)), (1, upper, range(planes)[::-1])):
        order = list(order)
        to_rows(first, reader(blocks, order[0], 0), rows, species)
        for plane in order[1:]:
            to_rows(second, reader(blocks, plane, 0), rows, species)
            for z in range(rows):
                at = pl.ds(z * species, species)
                left = second[at, : LANES // 2].astype(BF16)
                high, low = halves(first[at, : LANES // 2])
                if plane == order[1]:
                    product = dot(left, twice(high))
                else:
                    product = dot(left, twice(high)) + dot(left, twice(low))
                first[at, :] = product
        if planes % 2:
            first[...] = -first[...]
        from_rows(first, out, (side,), rows, species)


def join_kernel(level, axis, own, partner, out, first, second):
    rows, width = own.shape[1:]
    species = LANES // 2
    here = (lax.axis_index(axis) >> level) & 1
    for side in (0, 1):
        later = here == (1 if side == 0 else 0)
        a, b = reader(own, side), reader(partner, side)
        to_rows(first, lambda t: jnp.where(later, a(t), b(t)), rows, species)
        to_rows(second, lambda t: jnp.where(later, b(t), a(t)), rows, species)
        for z in range(rows):
            at = pl.ds(z * species, species)
            left_high, left_low = halves(first[at, : LANES // 2])
            high, low = halves(twice(second[at, : LANES // 2]))
            first[at, :] = dot(
                jnp.concatenate([left_high, left_low, left_high], 1),
                jnp.concatenate([high, high, low], 0),
            )
        from_rows(first, out, (side,), rows, species)


def base_kernel(start, source, diag, upper, side, rhs, base, scratch):
    planes = start.shape[0]
    vectors = [spread(scratch, start[p]) for p in range(planes)]
    for p in range(planes):
        own = apply([(reader(diag, p, 0), spread(scratch, source[p]))])
        rhs[p] = own
        terms = [
            (reader(side, 0, p, 0), shifted(vectors[p], True)),
            (reader(side, 1, p, 0), shifted(vectors[p], False)),
        ]
        if p + 1 < planes:
            terms.append((reader(upper, p, 0), vectors[p + 1]))
        base[p] = own - apply(terms)


def outgoing(offset, partners, here, sent):
    vector = offset
    for level in range(sent.shape[0]):
        sent[level] = vector
        if level + 1 < sent.shape[0]:
            passed = apply([(partners[level], vector)])
            vector = jnp.where((here >> level) & 1 == 0, passed, vector)


def incoming(gathered, partners, here, count, reverse):
    levels = gathered.shape[1]
    entering = None
    for level in range(levels)[::-1]:
        total = jnp.zeros(gathered.shape[2:], F32)
        for e in range(count):
            place = count - 1 - e if reverse else e
            total = total + jnp.where((place >> level) == (here >> level) - 1, gathered[e, level], 0.0)
        if entering is not None:
            total = total + apply([(partners[level], entering)])
        else:
            entering = jnp.zeros_like(total)
        entering = jnp.where((here >> level) & 1 == 1, total, entering)
    return entering


def forward_offset_kernel(axis, count, base, low, high, ahead, side, upper, lower, *rest):
    *partners, drive, sent, scratch = rest
    planes = base.shape[0]
    here = lax.axis_index(axis)
    previous = None
    for p in range(planes):
        terms = [
            (reader(side, 0, p, 0), spread(scratch, low[p])),
            (reader(side, 1, p, 0), spread(scratch, high[p])),
        ]
        if p + 1 == planes:
            terms.append((reader(upper, p, 0), spread(scratch, ahead[0])))
        fresh = base[p] - apply(terms)
        drive[p] = fresh
        if previous is not None:
            fresh = fresh - apply([(reader(lower, p, 0), previous)])
        previous = fresh
    outgoing(previous, [reader(ref, 0) for ref in partners], here, sent)


def forward_kernel(axis, count, gathered, drive, lower, rhs, *rest):
    *partners, out, vectors, base, scratch = rest
    planes = drive.shape[0]
    here = lax.axis_index(axis)
    previous = incoming(gathered, [reader(ref, 0) for ref in partners], here, count, False)
    for p in range(planes):
        term = apply([(reader(lower, p, 0), previous)])
        previous = drive[p] - term
        base[p] = rhs[p] - term
        vectors[p] = previous
        out[p] = gather_pairs(scratch, previous)


def side_kernel(base, vectors, side, out):
    for p in range(base.shape[0]):
        vector = vectors[p]
        out[p] = base[p] - apply(
            [
                (reader(side, 0, p, 0), shifted(vector, True)),
                (reader(side, 1, p, 0), shifted(vector, False)),
            ]
        )


def backward_offset_kernel(axis, count, base, low, high, side, upper, *rest):
    *partners, drive, sent, scratch = rest
    planes = base.shape[0]
    here = count - 1 - lax.axis_index(axis)
    previous = None
    for p in range(planes)[::-1]:
        fresh = base[p] - apply(
            [
                (reader(side, 0, p, 0), spread(scratch, low[p])),
                (reader(side, 1, p, 0), spread(scratch, high[p])),
            ]
        )
        drive[p] = fresh
        if previous is not None:
            fresh = fresh - apply([(reader(upper, p, 0), previous)])
        previous = fresh
    outgoing(previous, [reader(ref, 0) for ref in partners], here, sent)


def backward_kernel(axis, count, gathered, drive, upper, *rest):
    *partners, out, scratch = rest
    planes = drive.shape[0]
    here = count - 1 - lax.axis_index(axis)
    previous = incoming(gathered, [reader(ref, 0) for ref in partners], here, count, True)
    for p in range(planes)[::-1]:
        previous = drive[p] - apply([(reader(upper, p, 0), previous)])
        out[p] = gather_pairs(scratch, previous)


def call(kernel, operands, outs, scratch, flops=1 << 20):
    arrays = [o[0] if isinstance(o, tuple) else o for o in operands]
    parts = [(i, o[1], o[2]) for i, o in enumerate(operands) if isinstance(o, tuple)]
    buffers = [pltpu.VMEM((size,) + arrays[i].shape[1:], arrays[i].dtype) for i, _, size in parts]
    outs = [jax.ShapeDtypeStruct(shape, F32) for shape in outs]
    moved = sum(a.size * a.dtype.itemsize for a in arrays)

    def body(*refs):
        refs = list(refs)
        if parts:
            held, semaphores = refs[-len(parts) - 1 : -1], refs[-1]
            refs = refs[: -len(parts) - 1]
            copies = []
            for k, (i, first, size) in enumerate(parts):
                copies.append(
                    pltpu.make_async_copy(refs[i].at[pl.ds(first, size)], held[k], semaphores.at[k])
                )
                copies[-1].start()
                refs[i] = held[k]
            for copy in copies:
                copy.wait()
        kernel(*refs)

    inside = [pltpu.VMEM(shape, F32) for shape in scratch] + buffers
    if parts:
        inside.append(pltpu.SemaphoreType.DMA((len(parts),)))
    held = [i for i, _, _ in parts]
    return pl.pallas_call(
        body,
        out_shape=outs,
        in_specs=[
            pl.BlockSpec(memory_space=pl.ANY if i in held else pltpu.VMEM) for i in range(len(arrays))
        ],
        out_specs=[pl.BlockSpec(memory_space=pltpu.VMEM) for _ in outs],
        scratch_shapes=inside,
        compiler_params=pltpu.CompilerParams(vmem_limit_bytes=24 << 20),
        cost_estimate=pl.CostEstimate(flops=flops, bytes_accessed=moved, transcendentals=0),
    )(*arrays)


def neighbours(block, axis):
    count = lax.axis_size(axis)
    up = [(i, i + 1) for i in range(count - 1)]
    down = [(target, source) for source, target in up]
    return lax.ppermute(block, axis, up), lax.ppermute(block, axis, down)


def local(start, source, diag_inverse, x_lower, x_upper, side_blocks):
    planes, _, depth, width = x_lower.shape
    species = start.shape[2] // depth
    count = lax.axis_size("gx")
    levels = count.bit_length() - 1
    raw = (planes, depth * species // LANES, LANES)
    vec = (planes, depth, LANES)
    mat = (2, depth, width)
    rows = (depth * species, LANES)
    one = (depth, LANES)
    start = start.reshape(raw)
    source = source.reshape(raw)

    low, high = neighbours(start, "gy")
    ahead = lax.ppermute(start[:1], "gx", [(i + 1, i) for i in range(count - 1)])

    (maps,) = call(prep_kernel, [x_lower, x_upper], [mat], [rows, rows], 1 << 24)
    partners = []
    for level in range(levels - 1):
        got = lax.ppermute(maps, "gx", [(i, i ^ (1 << level)) for i in range(count)])
        partners.append(got)
        if level + 2 < levels:
            (maps,) = call(
                functools.partial(join_kernel, level, "gx"), [maps, got], [mat], [rows, rows], 1 << 25
            )
    forward_maps = [(a, 0, 1) for a in partners]
    backward_maps = [(a, 1, 1) for a in partners]

    near = (side_blocks, 0, 2)
    vertical = (side_blocks, 2, 2)
    rhs, base = call(base_kernel, [start, source, diag_inverse, x_upper, vertical], [vec, vec], [one])
    drive, sent = call(
        functools.partial(forward_offset_kernel, "gx", count),
        [base, low, high, ahead, near, x_upper, x_lower] + forward_maps,
        [vec, (levels,) + one],
        [one],
    )
    gathered = lax.all_gather(sent, "gx")
    forward, vectors, base = call(
        functools.partial(forward_kernel, "gx", count),
        [gathered, drive, x_lower, rhs] + forward_maps,
        [raw, vec, vec],
        [one],
    )
    low, high = neighbours(forward, "gy")
    (base,) = call(side_kernel, [base, vectors, vertical], [vec], [])
    drive, sent = call(
        functools.partial(backward_offset_kernel, "gx", count),
        [base, low, high, near, x_upper] + backward_maps,
        [vec, (levels,) + one],
        [one],
    )
    gathered = lax.all_gather(sent, "gx")
    (result,) = call(
        functools.partial(backward_kernel, "gx", count),
        [gathered, drive, x_upper] + backward_maps,
        [raw],
        [one],
    )
    shape = (planes, 1, depth * species)
    return forward.reshape(shape), result.reshape(shape)


def solution(mesh):
    return jax.shard_map(
        local,
        mesh=mesh,
        in_specs=(
            P("gx", "gy", None),
            P("gx", "gy", None),
            P("gx", "gy", None, None),
            P("gx", "gy", None, None),
            P("gx", "gy", None, None),
            P(None, "gx", "gy", None, None),
        ),
        out_specs=(P("gx", "gy", None), P("gx", "gy", None)),
        check_vma=False,
    )
```

```python
import functools

import jax
import jax.numpy as jnp
from jax import lax
from jax.experimental import pallas as pl
from jax.experimental.pallas import tpu as pltpu
from jax.sharding import PartitionSpec as P

LANES = 128
F32 = jnp.float32
BF16 = jnp.bfloat16


def lane_bit(shape, shift):
    return (lax.broadcasted_iota(jnp.int32, shape, len(shape) - 1) & shift) != 0


def segment_sums(leaf, tiles, rows):
    shape = (rows, LANES)

    def node(base, stride, shift):
        if stride == tiles:
            return leaf(base)
        low = node(base, stride * 2, shift * 2)
        high = node(base + stride, stride * 2, shift * 2)
        low = low + pltpu.roll(low, LANES - shift, 1)
        high = high + pltpu.roll(high, shift, 1)
        return jnp.where(lane_bit(shape, shift), high, low)

    part = node(0, 1, 2)
    odd = lane_bit(shape, 1)
    part = part + jnp.where(odd, pltpu.roll(part, 1, 1), pltpu.roll(part, LANES - 1, 1))
    upper = lane_bit(shape, LANES // 2)
    return jnp.where(upper == odd, part, pltpu.roll(part, LANES // 2, 1))


def apply(terms):
    rows = terms[0][1].shape[0]
    tiles = LANES // 4

    def leaf(t):
        return sum(read(t).astype(F32) * vector for read, vector in terms)

    return segment_sums(leaf, tiles, rows)


def reader(ref, *index):
    return lambda t: ref[(*index, slice(None), slice(t * LANES, (t + 1) * LANES))]


def spread(scratch, raw):
    upper = lane_bit(raw.shape, LANES // 2)
    other = pltpu.roll(raw, LANES // 2, 1)
    half = raw.shape[0]
    scratch[pl.ds(0, half, stride=2), :] = jnp.where(upper, other, raw)
    scratch[pl.ds(1, half, stride=2), :] = jnp.where(upper, raw, other)
    return scratch[...]


def gather_pairs(scratch, vector):
    scratch[...] = vector
    half = vector.shape[0] // 2
    even = scratch[pl.ds(0, half, stride=2), :]
    odd = scratch[pl.ds(1, half, stride=2), :]
    return jnp.where(lane_bit(even.shape, LANES // 2), odd, even)


def shifted(vector, down):
    rows = vector.shape[0]
    row = lax.broadcasted_iota(jnp.int32, vector.shape, 0)
    if down:
        return jnp.where(row == 0, 0.0, pltpu.roll(vector, 1, 0))
    return jnp.where(row == rows - 1, 0.0, pltpu.roll(vector, rows - 1, 0))


def to_rows(scratch, read, rows, species):
    for a in range(species):
        tile = read(a // 2).astype(F32)
        if a % 2:
            tile = pltpu.roll(tile, LANES // 2, 1)
        scratch[pl.ds(a, rows, stride=species), :] = tile


def from_rows(scratch, out, index, rows, species):
    upper = lane_bit((rows, LANES), LANES // 2)
    for t in range(species // 2):
        even = scratch[pl.ds(2 * t, rows, stride=species), :]
        odd = scratch[pl.ds(2 * t + 1, rows, stride=species), :]
        out[(*index, slice(None), slice(t * LANES, (t + 1) * LANES))] = jnp.where(upper, odd, even)


def twice(a):
    return jnp.concatenate([a, a], 1)


def halves(a):
    high = a.astype(BF16)
    return high, (a - high.astype(F32)).astype(BF16)


def dot(a, b):
    return jnp.dot(a, b, preferred_element_type=F32)


def prep_kernel(lower, upper, lower_map, upper_map, first, second):
    planes, _, rows, width = lower.shape
    species = LANES // 2
    for out, blocks, order in ((lower_map, lower, range(planes)), (upper_map, upper, range(planes)[::-1])):
        order = list(order)
        to_rows(first, reader(blocks, order[0], 0), rows, species)
        for plane in order[1:]:
            to_rows(second, reader(blocks, plane, 0), rows, species)
            for z in range(rows):
                at = pl.ds(z * species, species)
                left = second[at, : LANES // 2].astype(BF16)
                high, low = halves(first[at, : LANES // 2])
                if plane == order[1]:
                    product = dot(left, twice(high))
                else:
                    product = dot(left, twice(high)) + dot(left, twice(low))
                first[at, :] = product
        if planes % 2:
            first[...] = -first[...]
        from_rows(first, out, (), rows, species)


def join_kernel(level, axis, *refs):
    *refs, first, second = refs
    rows = refs[0].shape[0]
    species = LANES // 2
    here = (lax.axis_index(axis) >> level) & 1
    for side in (0, 1):
        later = here == (1 if side == 0 else 0)
        own, partner, out = refs[side::2]
        a, b = reader(own), reader(partner)
        to_rows(first, lambda t: jnp.where(later, a(t), b(t)), rows, species)
        to_rows(second, lambda t: jnp.where(later, b(t), a(t)), rows, species)
        for z in range(rows):
            at = pl.ds(z * species, species)
            left_high, left_low = halves(first[at, : LANES // 2])
            high, low = halves(twice(second[at, : LANES // 2]))
            first[at, :] = dot(
                jnp.concatenate([left_high, left_low, left_high], 1),
                jnp.concatenate([high, high, low], 0),
            )
        from_rows(first, out, (), rows, species)


def base_kernel(start, source, diag, upper, side, rhs, base, scratch):
    planes = start.shape[0]
    vectors = [spread(scratch, start[p]) for p in range(planes)]
    for p in range(planes):
        own = apply([(reader(diag, p, 0), spread(scratch, source[p]))])
        rhs[p] = own
        terms = [
            (reader(side, 0, p, 0), shifted(vectors[p], True)),
            (reader(side, 1, p, 0), shifted(vectors[p], False)),
        ]
        if p + 1 < planes:
            terms.append((reader(upper, p, 0), vectors[p + 1]))
        base[p] = own - apply(terms)


def outgoing(offset, partners, here, sent):
    vector = offset
    for level, out in enumerate(sent):
        out[...] = vector
        if level + 1 < len(sent):
            passed = apply([(partners[level], vector)])
            vector = jnp.where((here >> level) & 1 == 0, passed, vector)


def incoming(received, partners, here):
    entering = None
    for level in range(len(partners) + 1)[::-1]:
        total = sum(ref[...] for ref in received[(1 << level) - 1 : (2 << level) - 1])
        if entering is not None:
            total = total + apply([(partners[level], entering)])
        else:
            entering = jnp.zeros_like(total)
        entering = jnp.where((here >> level) & 1 == 1, total, entering)
    return entering


def beside(axis, paired, other):
    place, count = lax.axis_index(axis), lax.axis_size(axis)
    odd = place & 1 == 1
    low = jnp.where(odd, paired, other)
    high = jnp.where(odd, other, paired)
    return jnp.where(place == 0, 0.0, low), jnp.where(place == count - 1, 0.0, high)


def forward_offset_kernel(levels, base, paired, other, ahead, side, upper, lower, *rest):
    partners, drive = rest[: levels - 1], rest[levels - 1]
    sent, scratch = rest[levels:-1], rest[-1]
    planes = base.shape[0]
    here = lax.axis_index("gx")
    last = here == lax.axis_size("gx") - 1
    previous = None
    for p in range(planes):
        low, high = beside("gy", paired[p], other[p])
        terms = [
            (reader(side, 0, p, 0), spread(scratch, low)),
            (reader(side, 1, p, 0), spread(scratch, high)),
        ]
        if p + 1 == planes:
            beyond = jnp.where(last, 0.0, ahead[0])
            terms.append((reader(upper, p, 0), spread(scratch, beyond)))
        fresh = base[p] - apply(terms)
        drive[p] = fresh
        if previous is not None:
            fresh = fresh - apply([(reader(lower, p, 0), previous)])
        previous = fresh
    outgoing(previous, [reader(ref) for ref in partners], here, sent)


def forward_kernel(drive, lower, rhs, *rest):
    *rest, out, vectors, base, scratch = rest
    planes = drive.shape[0]
    here, count = lax.axis_index("gx"), lax.axis_size("gx")
    received, partners = rest[: count - 1], rest[count - 1 :]
    previous = incoming(received, [reader(ref) for ref in partners], here)
    for p in range(planes):
        term = apply([(reader(lower, p, 0), previous)])
        previous = drive[p] - term
        base[p] = rhs[p] - term
        vectors[p] = previous
        out[p] = gather_pairs(scratch, previous)


def side_kernel(base, vectors, side, out):
    for p in range(base.shape[0]):
        vector = vectors[p]
        out[p] = base[p] - apply(
            [
                (reader(side, 0, p, 0), shifted(vector, True)),
                (reader(side, 1, p, 0), shifted(vector, False)),
            ]
        )


def backward_offset_kernel(levels, base, paired, other, side, upper, *rest):
    partners, drive = rest[: levels - 1], rest[levels - 1]
    sent, scratch = rest[levels:-1], rest[-1]
    planes = base.shape[0]
    here = lax.axis_size("gx") - 1 - lax.axis_index("gx")
    previous = None
    for p in range(planes)[::-1]:
        low, high = beside("gy", paired[p], other[p])
        fresh = base[p] - apply(
            [
                (reader(side, 0, p, 0), spread(scratch, low)),
                (reader(side, 1, p, 0), spread(scratch, high)),
            ]
        )
        drive[p] = fresh
        if previous is not None:
            fresh = fresh - apply([(reader(upper, p, 0), previous)])
        previous = fresh
    outgoing(previous, [reader(ref) for ref in partners], here, sent)


def backward_kernel(drive, upper, *rest):
    *rest, out, scratch = rest
    planes = drive.shape[0]
    count = lax.axis_size("gx")
    here = count - 1 - lax.axis_index("gx")
    received, partners = rest[: count - 1], rest[count - 1 :]
    previous = incoming(received, [reader(ref) for ref in partners], here)
    for p in range(planes)[::-1]:
        previous = drive[p] - apply([(reader(upper, p, 0), previous)])
        out[p] = gather_pairs(scratch, previous)


def call(kernel, operands, outs, scratch, flops=1 << 20):
    arrays = [o[0] if isinstance(o, tuple) else o for o in operands]
    parts = [(i, o[1], o[2]) for i, o in enumerate(operands) if isinstance(o, tuple)]
    buffers = [pltpu.VMEM((size,) + arrays[i].shape[1:], arrays[i].dtype) for i, _, size in parts]
    outs = [jax.ShapeDtypeStruct(shape, F32) for shape in outs]
    moved = sum(a.size * a.dtype.itemsize for a in arrays)

    def body(*refs):
        refs = list(refs)
        if parts:
            held, semaphores = refs[-len(parts) - 1 : -1], refs[-1]
            refs = refs[: -len(parts) - 1]
            copies = []
            for k, (i, first, size) in enumerate(parts):
                copies.append(
                    pltpu.make_async_copy(refs[i].at[pl.ds(first, size)], held[k], semaphores.at[k])
                )
                copies[-1].start()
                refs[i] = held[k]
            for copy in copies:
                copy.wait()
        kernel(*refs)

    inside = [pltpu.VMEM(shape, F32) for shape in scratch] + buffers
    if parts:
        inside.append(pltpu.SemaphoreType.DMA((len(parts),)))
    held = [i for i, _, _ in parts]
    return pl.pallas_call(
        body,
        out_shape=outs,
        in_specs=[
            pl.BlockSpec(memory_space=pl.ANY if i in held else pltpu.VMEM) for i in range(len(arrays))
        ],
        out_specs=[pl.BlockSpec(memory_space=pltpu.VMEM) for _ in outs],
        scratch_shapes=inside,
        compiler_params=pltpu.CompilerParams(vmem_limit_bytes=24 << 20),
        cost_estimate=pl.CostEstimate(flops=flops, bytes_accessed=moved, transcendentals=0),
    )(*arrays)


def swaps(block, axis):
    count = lax.axis_size(axis)
    other = [(i, (i + 1 if i & 1 else i - 1)) for i in range(1, count - 1)]
    other += [(0, 0), (count - 1, count - 1)]
    paired = lax.ppermute(block, axis, [(i, i ^ 1) for i in range(count)])
    return paired, lax.ppermute(block, axis, other)


def crossed(block, axis, distance):
    return lax.ppermute(block, axis, [(i, i ^ distance) for i in range(lax.axis_size(axis))])


def local(start, source, diag_inverse, x_lower, x_upper, side_blocks):
    planes, _, depth, width = x_lower.shape
    species = start.shape[2] // depth
    count = lax.axis_size("gx")
    levels = count.bit_length() - 1
    raw = (planes, depth * species // LANES, LANES)
    vec = (planes, depth, LANES)
    mat = (depth, width)
    rows = (depth * species, LANES)
    one = (depth, LANES)
    start = start.reshape(raw)
    source = source.reshape(raw)

    paired, other = swaps(start, "gy")
    ahead = lax.ppermute(start[:1], "gx", [(i, (i - 1) % count) for i in range(count)])

    maps = call(prep_kernel, [x_lower, x_upper], [mat, mat], [rows, rows], 1 << 24)
    partners = []
    for level in range(levels - 1):
        partners.append([crossed(a, "gx", 1 << level) for a in maps])
        if level + 2 < levels:
            maps = call(
                functools.partial(join_kernel, level, "gx"),
                [*maps, *partners[-1]],
                [mat, mat],
                [rows, rows],
                1 << 25,
            )
    forward_maps = [a for a, _ in partners]
    backward_maps = [a for _, a in partners]
    pack = [one] * levels

    def exchange(sent):
        return [crossed(sent[m.bit_length() - 1], "gx", m) for m in range(1, count)]

    near = (side_blocks, 0, 2)
    vertical = (side_blocks, 2, 2)
    rhs, base = call(base_kernel, [start, source, diag_inverse, x_upper, vertical], [vec, vec], [one])
    drive, *sent = call(
        functools.partial(forward_offset_kernel, levels),
        [base, paired, other, ahead, near, x_upper, x_lower] + forward_maps,
        [vec] + pack,
        [one],
    )
    forward, vectors, base = call(
        forward_kernel,
        [drive, x_lower, rhs] + exchange(sent) + forward_maps,
        [raw, vec, vec],
        [one],
    )
    paired, other = swaps(forward, "gy")
    (base,) = call(side_kernel, [base, vectors, vertical], [vec], [])
    drive, *sent = call(
        functools.partial(backward_offset_kernel, levels),
        [base, paired, other, near, x_upper] + backward_maps,
        [vec] + pack,
        [one],
    )
    (result,) = call(
        backward_kernel,
        [drive, x_upper] + exchange(sent) + backward_maps,
        [raw],
        [one],
    )
    shape = (planes, 1, depth * species)
    return forward.reshape(shape), result.reshape(shape)


def solution(mesh):
    return jax.shard_map(
        local,
        mesh=mesh,
        in_specs=(
            P("gx", "gy", None),
            P("gx", "gy", None),
            P("gx", "gy", None, None),
            P("gx", "gy", None, None),
            P("gx", "gy", None, None),
            P(None, "gx", "gy", None, None),
        ),
        out_specs=(P("gx", "gy", None), P("gx", "gy", None)),
        check_vma=False,
    )
```

```python
import functools

import jax
import jax.numpy as jnp
from jax import lax
from jax.experimental import pallas as pl
from jax.experimental.pallas import tpu as pltpu
from jax.sharding import PartitionSpec as P

LANES = 128
F32 = jnp.float32
BF16 = jnp.bfloat16


def lane_bit(shape, shift):
    return (lax.broadcasted_iota(jnp.int32, shape, len(shape) - 1) & shift) != 0


def segment_sums(leaf, tiles, rows):
    shape = (rows, LANES)

    def node(base, stride, shift):
        if stride == tiles:
            return leaf(base)
        low = node(base, stride * 2, shift * 2)
        high = node(base + stride, stride * 2, shift * 2)
        low = low + pltpu.roll(low, LANES - shift, 1)
        high = high + pltpu.roll(high, shift, 1)
        return jnp.where(lane_bit(shape, shift), high, low)

    part = node(0, 1, 2)
    odd = lane_bit(shape, 1)
    part = part + jnp.where(odd, pltpu.roll(part, 1, 1), pltpu.roll(part, LANES - 1, 1))
    upper = lane_bit(shape, LANES // 2)
    return jnp.where(upper == odd, part, pltpu.roll(part, LANES // 2, 1))


def apply(terms):
    rows = terms[0][1].shape[0]
    tiles = LANES // 4

    def leaf(t):
        return sum(read(t).astype(F32) * vector for read, vector in terms)

    return segment_sums(leaf, tiles, rows)


def reader(ref, *index):
    return lambda t: ref[(*index, slice(None), slice(t * LANES, (t + 1) * LANES))]


def spread(scratch, raw):
    upper = lane_bit(raw.shape, LANES // 2)
    other = pltpu.roll(raw, LANES // 2, 1)
    half = raw.shape[0]
    scratch[pl.ds(0, half, stride=2), :] = jnp.where(upper, other, raw)
    scratch[pl.ds(1, half, stride=2), :] = jnp.where(upper, raw, other)
    return scratch[...]


def gather_pairs(scratch, vector):
    scratch[...] = vector
    half = vector.shape[0] // 2
    even = scratch[pl.ds(0, half, stride=2), :]
    odd = scratch[pl.ds(1, half, stride=2), :]
    return jnp.where(lane_bit(even.shape, LANES // 2), odd, even)


def shifted(vector, down):
    rows = vector.shape[0]
    row = lax.broadcasted_iota(jnp.int32, vector.shape, 0)
    if down:
        return jnp.where(row == 0, 0.0, pltpu.roll(vector, 1, 0))
    return jnp.where(row == rows - 1, 0.0, pltpu.roll(vector, rows - 1, 0))


def to_rows(scratch, read, rows, species):
    for a in range(species):
        tile = read(a // 2).astype(F32)
        if a % 2:
            tile = pltpu.roll(tile, LANES // 2, 1)
        scratch[pl.ds(a, rows, stride=species), :] = tile


def halves(a):
    high = a.astype(BF16)
    return high, (a - high.astype(F32)).astype(BF16)


def dot(a, b, dims=((1,), (0,))):
    return lax.dot_general(a, b, (dims, ((), ())), preferred_element_type=F32)


def turn(scratch, out, first, pairs, species):
    unit = (
        lax.broadcasted_iota(jnp.int32, (species, species), 0)
        == lax.broadcasted_iota(jnp.int32, (species, species), 1)
    ).astype(F32).astype(BF16)
    for pair in range(pairs):
        block = scratch[pair * LANES : (pair + 1) * LANES, :species].astype(BF16)
        out[pl.ds(first + pair, species, stride=pairs), :] = dot(unit, block, ((1,), (1,)))


def both(block):
    upper = lane_bit(block.shape, LANES // 2)
    zero = jnp.zeros_like(block)
    return jnp.concatenate([jnp.where(upper, zero, block), jnp.where(upper, block, zero)], 0)


def multiply(earlier, later, exact):
    if exact:
        return dot(earlier.astype(BF16), both(later).astype(BF16))
    earlier_high, earlier_low = halves(earlier)
    high, low = halves(both(later))
    return dot(earlier_high, high) + (dot(earlier_low, high) + dot(earlier_high, low))


def turned(ref, vector, first=0, swapped=None):
    pairs = vector.shape[0]
    lane = lax.broadcasted_iota(jnp.int32, vector.shape, 1)
    side = lane & (LANES // 2)
    refs = [(ref, first)] if swapped is None else [(ref, 0), (swapped, 0)]
    sums = [None] * 4
    total = LANES // 2
    share = total // len(refs)
    for b in range(total):
        held, at = refs[b // share]
        row = at + (b % share) * pairs
        term = held[row : row + pairs, :] * jnp.take_along_axis(vector, side + b, 1)
        sums[b % 4] = term if sums[b % 4] is None else sums[b % 4] + term
    return (sums[0] + sums[1]) + (sums[2] + sums[3])


def prep_kernel(lower, upper, lower_turned, upper_turned, lower_products, upper_products, rows_scratch):
    planes, _, rows, width = lower.shape
    species = LANES // 2
    pairs = rows // 2
    size = species * pairs
    for blocks, maps, products, order in (
        (lower, lower_turned, lower_products, list(range(planes))),
        (upper, upper_turned, upper_products, list(range(planes))[::-1]),
    ):
        for plane in order:
            to_rows(rows_scratch, reader(blocks, plane, 0), rows, species)
            turn(rows_scratch, maps, plane * size, pairs, species)
        for step, plane in enumerate(order):
            at = pl.ds(plane * size, size)
            if step == 0:
                products[at, :] = -maps[at, :]
                continue
            for pair in range(pairs):
                here = pl.ds(plane * size + pair, species, stride=pairs)
                before = pl.ds(order[step - 1] * size + pair, species, stride=pairs)
                later = -maps[here, :]
                if step == 1:
                    products[here, :] = multiply(products[before, :], later, True)
                else:
                    products[here, :] = multiply(products[before, :], later, False)


def join_kernel(level, full, pairs, own_planes, *refs):
    here = (lax.axis_index("gx") >> level) & 1
    core = lax.axis_index("gx") & 1
    species = LANES // 2
    size = species * pairs
    half = size // 2
    inputs, outputs = refs[: len(own_planes)], refs[len(own_planes) :]
    each = len(inputs) // 2
    for side in (0, 1):
        later_is_own = here == (1 if side == 0 else 0)
        own, *partner = inputs[side * each : (side + 1) * each]
        first = own_planes[side * each] * size
        outs = outputs[side * (len(outputs) // 2) : (side + 1) * (len(outputs) // 2)]
        for pair in range(pairs):
            mine = own[pl.ds(first + pair, species, stride=pairs), :]
            if len(partner) == 1:
                theirs = partner[0][pl.ds(pair, species, stride=pairs), :]
            else:
                near = partner[0][pl.ds(pair, species // 2, stride=pairs), :]
                far = partner[1][pl.ds(pair, species // 2, stride=pairs), :]
                theirs = jnp.where(
                    core == 0, jnp.concatenate([near, far], 0), jnp.concatenate([far, near], 0)
                )
            earlier = jnp.where(later_is_own, theirs, mine)
            later = jnp.where(later_is_own, mine, theirs)
            kept = jnp.where(core == 0, earlier[: species // 2], earlier[species // 2 :])
            if full:
                product = multiply(earlier, later, False)
                outs[0][pl.ds(pair, species, stride=pairs), :] = product
                kept = jnp.where(core == 0, product[: species // 2], product[species // 2 :])
            else:
                kept = multiply(kept, later, False)
            outs[-1][pl.ds(pair, species // 2, stride=pairs), :] = kept


def base_kernel(start, source, diag, upper, side, rhs, base, scratch):
    planes = start.shape[0]
    vectors = [spread(scratch, start[p]) for p in range(planes)]
    for p in range(planes):
        own = apply([(reader(diag, p, 0), spread(scratch, source[p]))])
        terms = [
            (reader(side, 0, p, 0), shifted(vectors[p], True)),
            (reader(side, 1, p, 0), shifted(vectors[p], False)),
        ]
        if p + 1 < planes:
            terms.append((reader(upper, p, 0), vectors[p + 1]))
        around = apply(terms)
        rhs[p] = gather_pairs(scratch, own)
        base[p] = gather_pairs(scratch, own - around)


def partner_map(refs, vector):
    if len(refs) == 1:
        return turned(refs[0], vector)
    core = lax.axis_index("gx") & 1
    quarter = LANES // 4
    inner = lane_bit(vector.shape, quarter)
    crossed_over = jnp.where(
        inner, pltpu.roll(vector, quarter, 1), pltpu.roll(vector, LANES - quarter, 1)
    )
    return turned(refs[0], jnp.where(core == 0, vector, crossed_over), 0, refs[1])


def outgoing(offset, partners, here, slots):
    vectors = [offset]
    for level, refs in enumerate(partners):
        passed = partner_map(refs, vectors[-1])
        vectors.append(jnp.where((here >> level) & 1 == 0, passed, vectors[-1]))
    place = lax.axis_index("gx")
    for target in range(slots.shape[0]):
        apart = place ^ target
        value = vectors[0]
        for level in range(1, len(vectors)):
            value = jnp.where(apart >= 1 << level, vectors[level], value)
        slots[target] = value


def incoming(got, partners, here, reverse):
    count = got.shape[0]
    entering = None
    for level in range(len(partners) + 1)[::-1]:
        total = None
        for source in range(count):
            place = count - 1 - source if reverse else source
            term = jnp.where((place >> level) == (here >> level) - 1, got[source], 0.0)
            total = term if total is None else total + term
        if entering is not None:
            total = total + partner_map(partners[level], entering)
        before = jnp.zeros_like(total) if entering is None else entering
        entering = jnp.where((here >> level) & 1 == 1, total, before)
    return entering


def grouped(refs, levels):
    return [list(refs[:1])] + [list(refs[i : i + 2]) for i in range(1, 2 * levels - 3, 2)]


def beside(axis, paired, other):
    place, count = lax.axis_index(axis), lax.axis_size(axis)
    odd = place & 1 == 1
    low = jnp.where(odd, paired, other)
    high = jnp.where(odd, other, paired)
    return jnp.where(place == 0, 0.0, low), jnp.where(place == count - 1, 0.0, high)


def forward_offset_kernel(levels, base, paired, other, ahead, side, upper, lower, *rest):
    *partners, drive, offsets, slots, scratch = rest
    planes = base.shape[0]
    size = base.shape[1] * LANES // 2
    here = lax.axis_index("gx")
    last = here == lax.axis_size("gx") - 1
    previous = None
    for p in range(planes):
        low, high = beside("gy", paired[p], other[p])
        terms = [
            (reader(side, 0, p, 0), spread(scratch, low)),
            (reader(side, 1, p, 0), spread(scratch, high)),
        ]
        if p + 1 == planes:
            beyond = jnp.where(last, 0.0, ahead[0])
            terms.append((reader(upper, p, 0), spread(scratch, beyond)))
        fresh = base[p] - gather_pairs(scratch, apply(terms))
        drive[p] = fresh
        if previous is not None:
            fresh = fresh - turned(lower, previous, p * size)
        offsets[p] = fresh
        previous = fresh
    outgoing(previous, grouped(partners, levels), here, slots)


def forward_kernel(levels, got, drive, offsets, rhs, products, *rest):
    *partners, out, copies, base = rest
    planes = drive.shape[0]
    size = drive.shape[1] * LANES // 2
    entering = incoming(got, grouped(partners, levels), lax.axis_index("gx"), False)
    for p in range(planes):
        value = offsets[p] + turned(products, entering, p * size)
        base[p] = rhs[p] - (drive[p] - value)
        out[p] = value
        for target in range(copies.shape[0]):
            copies[target, p] = value


def side_kernel(base, vectors, side, out, scratch):
    for p in range(base.shape[0]):
        vector = spread(scratch, vectors[p])
        around = apply(
            [
                (reader(side, 0, p, 0), shifted(vector, True)),
                (reader(side, 1, p, 0), shifted(vector, False)),
            ]
        )
        out[p] = base[p] - gather_pairs(scratch, around)


def backward_offset_kernel(levels, base, got, side, upper, *rest):
    *partners, offsets, slots, scratch = rest
    planes = base.shape[0]
    size = base.shape[1] * LANES // 2
    row, rows = lax.axis_index("gy"), lax.axis_size("gy")
    here = lax.axis_size("gx") - 1 - lax.axis_index("gx")
    previous = None
    for p in range(planes)[::-1]:
        low = jnp.where(row == 0, 0.0, got[jnp.maximum(row - 1, 0), p])
        high = jnp.where(row == rows - 1, 0.0, got[jnp.minimum(row + 1, rows - 1), p])
        around = apply(
            [
                (reader(side, 0, p, 0), spread(scratch, low)),
                (reader(side, 1, p, 0), spread(scratch, high)),
            ]
        )
        fresh = base[p] - gather_pairs(scratch, around)
        if previous is not None:
            fresh = fresh - turned(upper, previous, p * size)
        offsets[p] = fresh
        previous = fresh
    outgoing(previous, grouped(partners, levels), here, slots)


def backward_kernel(levels, got, offsets, products, *rest):
    *partners, out = rest
    size = offsets.shape[1] * LANES // 2
    here = lax.axis_size("gx") - 1 - lax.axis_index("gx")
    entering = incoming(got, grouped(partners, levels), here, True)
    for p in range(offsets.shape[0]):
        out[p] = offsets[p] + turned(products, entering, p * size)


def call(kernel, operands, outs, scratch, micros):
    arrays = [o[0] if isinstance(o, tuple) else o for o in operands]
    parts = [(i, o[1], o[2]) for i, o in enumerate(operands) if isinstance(o, tuple)]
    buffers = [pltpu.VMEM((size,) + arrays[i].shape[1:], arrays[i].dtype) for i, _, size in parts]
    outs = [jax.ShapeDtypeStruct(shape, F32) for shape in outs]
    moved = sum(a.size * a.dtype.itemsize for a in arrays)

    def body(*refs):
        refs = list(refs)
        if parts:
            held, semaphores = refs[-len(parts) - 1 : -1], refs[-1]
            refs = refs[: -len(parts) - 1]
            copies = []
            for k, (i, first, size) in enumerate(parts):
                copies.append(
                    pltpu.make_async_copy(refs[i].at[pl.ds(first, size)], held[k], semaphores.at[k])
                )
                copies[-1].start()
                refs[i] = held[k]
            for copy in copies:
                copy.wait()
        kernel(*refs)

    inside = [pltpu.VMEM(shape, F32) for shape in scratch] + buffers
    if parts:
        inside.append(pltpu.SemaphoreType.DMA((len(parts),)))
    held = [i for i, _, _ in parts]
    return pl.pallas_call(
        body,
        out_shape=outs,
        in_specs=[
            pl.BlockSpec(memory_space=pl.ANY if i in held else pltpu.VMEM) for i in range(len(arrays))
        ],
        out_specs=[pl.BlockSpec(memory_space=pltpu.VMEM) for _ in outs],
        scratch_shapes=inside,
        compiler_params=pltpu.CompilerParams(vmem_limit_bytes=24 << 20),
        cost_estimate=pl.CostEstimate(flops=int(micros * 1.15e9), bytes_accessed=moved, transcendentals=0),
    )(*arrays)


def swaps(block, axis):
    count = lax.axis_size(axis)
    other = [(i, (i + 1 if i & 1 else i - 1)) for i in range(1, count - 1)]
    other += [(0, 0), (count - 1, count - 1)]
    paired = lax.ppermute(block, axis, [(i, i ^ 1) for i in range(count)])
    return paired, lax.ppermute(block, axis, other)


def crossed(block, axis, distance):
    return lax.ppermute(block, axis, [(i, i ^ distance) for i in range(lax.axis_size(axis))])


def exchange(slots, axis):
    return lax.all_to_all(slots, axis, 0, 0)


def local(start, source, diag_inverse, x_lower, x_upper, side_blocks):
    planes, _, depth, width = x_lower.shape
    species = start.shape[2] // depth
    pairs = depth // 2
    count, rows = lax.axis_size("gx"), lax.axis_size("gy")
    levels = count.bit_length() - 1
    size = species * pairs
    one = (pairs, LANES)
    vec = (planes,) + one
    maps = (planes * size, LANES)
    whole, half = (size, LANES), (size // 2, LANES)
    dup = (depth, LANES)
    slots = (count,) + one
    start = start.reshape(vec)
    source = source.reshape(vec)

    paired, other = swaps(start, "gy")
    ahead = lax.ppermute(start[:1], "gx", [(i, (i - 1) % count) for i in range(count)])

    lower, upper, lower_products, upper_products = call(
        prep_kernel, [x_lower, x_upper], [maps] * 4, [(depth * species, LANES)], 2.0
    )
    owns = [(lower_products, planes - 1), (upper_products, 0)]
    partners = [[], []]
    for level in range(levels - 1):
        got = []
        for side, (own, plane) in enumerate(owns):
            if level == 0:
                got.append([crossed(own[plane * size : (plane + 1) * size], "gx", 1)])
            else:
                mine = crossed(kept[side], "gx", 1 << level)
                got.append([mine, crossed(mine, "gx", 1)])
            partners[side] += got[side]
        if level + 2 < levels:
            full = level + 3 < levels
            operands, places = [], []
            for (own, plane), parts in zip(owns, got):
                operands += [own] + parts
                places += [plane] + [0] * len(parts)
            outs = call(
                functools.partial(join_kernel, level, full, pairs, places),
                operands,
                ([whole, half] if full else [half]) * 2,
                [],
                1.5,
            )
            kept = [outs[1], outs[3]] if full else outs
            owns = [(outs[0], 0), (outs[2 if full else 1], 0)]

    near = (side_blocks, 0, 2)
    vertical = (side_blocks, 2, 2)
    rhs, base = call(
        base_kernel, [start, source, diag_inverse, x_upper, vertical], [vec, vec], [dup], 1.5
    )
    drive, offsets, sent = call(
        functools.partial(forward_offset_kernel, levels),
        [base, paired, other, ahead, near, x_upper, lower] + partners[0],
        [vec, vec, slots],
        [dup],
        1.5,
    )
    forward, copies, base = call(
        functools.partial(forward_kernel, levels),
        [exchange(sent, "gx"), drive, offsets, rhs, lower_products] + partners[0],
        [vec, (rows,) + vec, vec],
        [],
        1.0,
    )
    beyond = exchange(copies, "gy")
    (base,) = call(side_kernel, [base, forward, vertical], [vec], [dup], 0.7)
    offsets, sent = call(
        functools.partial(backward_offset_kernel, levels),
        [base, beyond, near, upper] + partners[1],
        [vec, slots],
        [dup],
        1.5,
    )
    (result,) = call(
        functools.partial(backward_kernel, levels),
        [exchange(sent, "gx"), offsets, upper_products] + partners[1],
        [vec],
        [],
        1.0,
    )
    shape = (planes, 1, depth * species)
    return forward.reshape(shape), result.reshape(shape)


def solution(mesh):
    return jax.shard_map(
        local,
        mesh=mesh,
        in_specs=(
            P("gx", "gy", None),
            P("gx", "gy", None),
            P("gx", "gy", None, None),
            P("gx", "gy", None, None),
            P("gx", "gy", None, None),
            P(None, "gx", "gy", None, None),
        ),
        out_specs=(P("gx", "gy", None), P("gx", "gy", None)),
        check_vma=False,
    )
```

```python
import functools

import jax
import jax.numpy as jnp
from jax import lax
from jax.experimental import pallas as pl
from jax.experimental.pallas import tpu as pltpu
from jax.sharding import PartitionSpec as P

LANES = 128
F32 = jnp.float32
BF16 = jnp.bfloat16


def lane_bit(shape, shift):
    return (lax.broadcasted_iota(jnp.int32, shape, len(shape) - 1) & shift) != 0


def segment_sums(leaf, tiles, rows):
    shape = (rows, LANES)

    def node(base, stride, shift):
        if stride == tiles:
            return leaf(base)
        low = node(base, stride * 2, shift * 2)
        high = node(base + stride, stride * 2, shift * 2)
        low = low + pltpu.roll(low, LANES - shift, 1)
        high = high + pltpu.roll(high, shift, 1)
        return jnp.where(lane_bit(shape, shift), high, low)

    part = node(0, 1, 2)
    odd = lane_bit(shape, 1)
    part = part + jnp.where(odd, pltpu.roll(part, 1, 1), pltpu.roll(part, LANES - 1, 1))
    upper = lane_bit(shape, LANES // 2)
    return jnp.where(upper == odd, part, pltpu.roll(part, LANES // 2, 1))


def apply(terms):
    rows = terms[0][1].shape[0]
    tiles = LANES // 4

    def leaf(t):
        return sum(read(t).astype(F32) * vector for read, vector in terms)

    return segment_sums(leaf, tiles, rows)


def reader(ref, *index):
    return lambda t: ref[(*index, slice(None), slice(t * LANES, (t + 1) * LANES))]


def spread(scratch, raw):
    upper = lane_bit(raw.shape, LANES // 2)
    other = pltpu.roll(raw, LANES // 2, 1)
    half = raw.shape[0]
    scratch[pl.ds(0, half, stride=2), :] = jnp.where(upper, other, raw)
    scratch[pl.ds(1, half, stride=2), :] = jnp.where(upper, raw, other)
    return scratch[...]


def gather_pairs(scratch, vector):
    scratch[...] = vector
    half = vector.shape[0] // 2
    even = scratch[pl.ds(0, half, stride=2), :]
    odd = scratch[pl.ds(1, half, stride=2), :]
    return jnp.where(lane_bit(even.shape, LANES // 2), odd, even)


def shifted(vector, down):
    rows = vector.shape[0]
    row = lax.broadcasted_iota(jnp.int32, vector.shape, 0)
    if down:
        return jnp.where(row == 0, 0.0, pltpu.roll(vector, 1, 0))
    return jnp.where(row == rows - 1, 0.0, pltpu.roll(vector, rows - 1, 0))


def to_rows(scratch, read, rows, species):
    for a in range(species):
        tile = read(a // 2).astype(F32)
        if a % 2:
            tile = pltpu.roll(tile, LANES // 2, 1)
        scratch[pl.ds(a, rows, stride=species), :] = tile


def halves(a):
    high = a.astype(BF16)
    return high, (a - high.astype(F32)).astype(BF16)


def dot(a, b, dims=((1,), (0,))):
    return lax.dot_general(a, b, (dims, ((), ())), preferred_element_type=F32)


def turn(scratch, out, first, pairs, species):
    unit = (
        lax.broadcasted_iota(jnp.int32, (species, species), 0)
        == lax.broadcasted_iota(jnp.int32, (species, species), 1)
    ).astype(F32).astype(BF16)
    for pair in range(pairs):
        block = scratch[pair * LANES : (pair + 1) * LANES, :species].astype(BF16)
        out[pl.ds(first + pair, species, stride=pairs), :] = dot(unit, block, ((1,), (1,)))


def both(block):
    upper = lane_bit(block.shape, LANES // 2)
    zero = jnp.zeros_like(block)
    return jnp.concatenate([jnp.where(upper, zero, block), jnp.where(upper, block, zero)], 0)


def multiply(earlier, later, exact):
    if exact:
        return dot(earlier.astype(BF16), both(later).astype(BF16))
    earlier_high, earlier_low = halves(earlier)
    high, low = halves(both(later))
    return dot(earlier_high, high) + (dot(earlier_low, high) + dot(earlier_high, low))


def turned(ref, vector, first=0, swapped=None):
    pairs = vector.shape[0]
    lane = lax.broadcasted_iota(jnp.int32, vector.shape, 1)
    side = lane & (LANES // 2)
    refs = [(ref, first)] if swapped is None else [(ref, 0), (swapped, 0)]
    sums = [None] * 4
    total = LANES // 2
    share = total // len(refs)
    for b in range(total):
        held, at = refs[b // share]
        row = at + (b % share) * pairs
        term = held[row : row + pairs, :] * jnp.take_along_axis(vector, side + b, 1)
        sums[b % 4] = term if sums[b % 4] is None else sums[b % 4] + term
    return (sums[0] + sums[1]) + (sums[2] + sums[3])


def prep_kernel(reverse, blocks, *refs):
    maps, products, own, rows_scratch = refs[-4:]
    planes, _, rows, width = blocks.shape
    species = LANES // 2
    pairs = rows // 2
    size = species * pairs
    order = list(range(planes))[::-1] if reverse else list(range(planes))
    for plane in order:
        to_rows(rows_scratch, reader(blocks, plane, 0), rows, species)
        turn(rows_scratch, maps, plane * size, pairs, species)
    for step, plane in enumerate(order):
        at = pl.ds(plane * size, size)
        if step == 0:
            products[at, :] = -maps[at, :]
            continue
        for pair in range(pairs):
            here = pl.ds(plane * size + pair, species, stride=pairs)
            before = pl.ds(order[step - 1] * size + pair, species, stride=pairs)
            products[here, :] = multiply(products[before, :], -maps[here, :], step == 1)
    own[...] = products[pl.ds(order[-1] * size, size), :]


def join_kernel(level, reverse, full, pairs, own, *refs):
    here = (lax.axis_index("gx") >> level) & 1
    core = lax.axis_index("gx") & 1
    species = LANES // 2
    outs = refs[-2:] if full else refs[-1:]
    partner = refs[: len(refs) - len(outs)]
    later_is_own = here == (0 if reverse else 1)
    for pair in range(pairs):
        mine = own[pl.ds(pair, species, stride=pairs), :]
        if len(partner) == 1:
            theirs = partner[0][pl.ds(pair, species, stride=pairs), :]
        else:
            close = partner[0][pl.ds(pair, species // 2, stride=pairs), :]
            far = partner[1][pl.ds(pair, species // 2, stride=pairs), :]
            theirs = jnp.where(
                core == 0, jnp.concatenate([close, far], 0), jnp.concatenate([far, close], 0)
            )
        earlier = jnp.where(later_is_own, theirs, mine)
        later = jnp.where(later_is_own, mine, theirs)
        if full:
            kept = multiply(earlier, later, False)
            outs[0][pl.ds(pair, species, stride=pairs), :] = kept
            kept = jnp.where(core == 0, kept[: species // 2], kept[species // 2 :])
        else:
            kept = jnp.where(core == 0, earlier[: species // 2], earlier[species // 2 :])
            kept = multiply(kept, later, False)
        outs[-1][pl.ds(pair, species // 2, stride=pairs), :] = kept


def base_kernel(start, source, diag, upper, side, rhs, base, scratch):
    planes = start.shape[0]
    vectors = [spread(scratch, start[p]) for p in range(planes)]
    for p in range(planes):
        own = apply([(reader(diag, p, 0), spread(scratch, source[p]))])
        terms = [
            (reader(side, 2, p, 0), shifted(vectors[p], True)),
            (reader(side, 3, p, 0), shifted(vectors[p], False)),
        ]
        if p + 1 < planes:
            terms.append((reader(upper, p, 0), vectors[p + 1]))
        around = apply(terms)
        rhs[p] = gather_pairs(scratch, own)
        base[p] = gather_pairs(scratch, own - around)


def partner_map(refs, vector):
    if len(refs) == 1:
        return turned(refs[0], vector)
    core = lax.axis_index("gx") & 1
    quarter = LANES // 4
    inner = lane_bit(vector.shape, quarter)
    crossed_over = jnp.where(
        inner, pltpu.roll(vector, quarter, 1), pltpu.roll(vector, LANES - quarter, 1)
    )
    return turned(refs[0], jnp.where(core == 0, vector, crossed_over), 0, refs[1])


def outgoing(offset, partners, here, slots):
    vectors = [offset]
    for level, refs in enumerate(partners):
        passed = partner_map(refs, vectors[-1])
        vectors.append(jnp.where((here >> level) & 1 == 0, passed, vectors[-1]))
    place = lax.axis_index("gx")
    for target in range(slots.shape[0]):
        apart = place ^ target
        value = vectors[0]
        for level in range(1, len(vectors)):
            value = jnp.where(apart >= 1 << level, vectors[level], value)
        slots[target] = value


def incoming(got, partners, here, reverse):
    count = got.shape[0]
    entering = None
    for level in range(len(partners) + 1)[::-1]:
        total = None
        for source in range(count):
            place = count - 1 - source if reverse else source
            term = jnp.where((place >> level) == (here >> level) - 1, got[source], 0.0)
            total = term if total is None else total + term
        if entering is not None:
            total = total + partner_map(partners[level], entering)
        before = jnp.zeros_like(total) if entering is None else entering
        entering = jnp.where((here >> level) & 1 == 1, total, before)
    return entering


def grouped(refs, levels):
    return [list(refs[:1])] + [list(refs[i : i + 2]) for i in range(1, 2 * levels - 3, 2)]


def beside(axis, paired, other):
    place, count = lax.axis_index(axis), lax.axis_size(axis)
    odd = place & 1 == 1
    low = jnp.where(odd, paired, other)
    high = jnp.where(odd, other, paired)
    return jnp.where(place == 0, 0.0, low), jnp.where(place == count - 1, 0.0, high)


def forward_offset_kernel(levels, base, paired, other, ahead, side, upper, lower, *rest):
    *partners, drive, offsets, slots, scratch = rest
    planes = base.shape[0]
    size = base.shape[1] * LANES // 2
    here = lax.axis_index("gx")
    last = here == lax.axis_size("gx") - 1
    previous = None
    for p in range(planes):
        low, high = beside("gy", paired[p], other[p])
        terms = [
            (reader(side, 0, p, 0), spread(scratch, low)),
            (reader(side, 1, p, 0), spread(scratch, high)),
        ]
        if p + 1 == planes:
            beyond = jnp.where(last, 0.0, ahead[0])
            terms.append((reader(upper, p, 0), spread(scratch, beyond)))
        fresh = base[p] - gather_pairs(scratch, apply(terms))
        drive[p] = fresh
        if previous is not None:
            fresh = fresh - turned(lower, previous, p * size)
        offsets[p] = fresh
        previous = fresh
    outgoing(previous, grouped(partners, levels), here, slots)


def forward_kernel(levels, got, drive, offsets, rhs, products, *rest):
    *partners, out, copy, base = rest
    planes = drive.shape[0]
    size = drive.shape[1] * LANES // 2
    entering = incoming(got, grouped(partners, levels), lax.axis_index("gx"), False)
    for p in range(planes):
        value = offsets[p] + turned(products, entering, p * size)
        base[p] = rhs[p] - (drive[p] - value)
        out[p] = value
        copy[p] = value


def side_kernel(base, vectors, side, out, scratch):
    for p in range(base.shape[0]):
        vector = spread(scratch, vectors[p])
        around = apply(
            [
                (reader(side, 2, p, 0), shifted(vector, True)),
                (reader(side, 3, p, 0), shifted(vector, False)),
            ]
        )
        out[p] = base[p] - gather_pairs(scratch, around)


def backward_offset_kernel(levels, base, paired, other, side, upper, *rest):
    *partners, offsets, slots, scratch = rest
    planes = base.shape[0]
    size = base.shape[1] * LANES // 2
    here = lax.axis_size("gx") - 1 - lax.axis_index("gx")
    previous = None
    for p in range(planes)[::-1]:
        low, high = beside("gy", paired[p], other[p])
        around = apply(
            [
                (reader(side, 0, p, 0), spread(scratch, low)),
                (reader(side, 1, p, 0), spread(scratch, high)),
            ]
        )
        fresh = base[p] - gather_pairs(scratch, around)
        if previous is not None:
            fresh = fresh - turned(upper, previous, p * size)
        offsets[p] = fresh
        previous = fresh
    outgoing(previous, grouped(partners, levels), here, slots)


def backward_kernel(levels, got, offsets, products, *rest):
    *partners, out = rest
    size = offsets.shape[1] * LANES // 2
    here = lax.axis_size("gx") - 1 - lax.axis_index("gx")
    entering = incoming(got, grouped(partners, levels), here, True)
    for p in range(offsets.shape[0]):
        out[p] = offsets[p] + turned(products, entering, p * size)


def call(kernel, operands, outs, scratch, micros):
    arrays = [o[0] if isinstance(o, tuple) else o for o in operands]
    held = [i for i, o in enumerate(operands) if isinstance(o, tuple)]
    outs = [jax.ShapeDtypeStruct(shape, F32) for shape in outs]
    moved = sum(a.size * a.dtype.itemsize for a in arrays)

    return pl.pallas_call(
        kernel,
        out_shape=outs,
        in_specs=[
            pl.BlockSpec(memory_space=pl.ANY if i in held else pltpu.VMEM) for i in range(len(arrays))
        ],
        out_specs=[pl.BlockSpec(memory_space=pltpu.VMEM) for _ in outs],
        scratch_shapes=[pltpu.VMEM(shape, F32) for shape in scratch],
        compiler_params=pltpu.CompilerParams(vmem_limit_bytes=24 << 20),
        cost_estimate=pl.CostEstimate(flops=int(micros * 1.15e9), bytes_accessed=moved, transcendentals=0),
    )(*arrays)


def swaps(block, axis):
    count = lax.axis_size(axis)
    other = [(i, (i + 1 if i & 1 else i - 1) % count) for i in range(count)]
    return crossed(block, axis, 1), lax.ppermute(block, axis, other)


def crossed(block, axis, distance):
    return lax.ppermute(block, axis, [(i, i ^ distance) for i in range(lax.axis_size(axis))])


def exchange(slots, axis):
    return lax.all_to_all(slots, axis, 0, 0)


def local(start, source, diag_inverse, x_lower, x_upper, side_blocks):
    planes, _, depth, width = x_lower.shape
    species = start.shape[2] // depth
    pairs = depth // 2
    count = lax.axis_size("gx")
    levels = count.bit_length() - 1
    size = species * pairs
    one = (pairs, LANES)
    vec = (planes,) + one
    maps = (planes * size, LANES)
    whole, half = (size, LANES), (size // 2, LANES)
    dup = (depth, LANES)
    slots = (count,) + one
    start = start.reshape(vec)
    source = source.reshape(vec)

    paired, other = swaps(start, "gy")
    ahead = lax.ppermute(start[:1], "gx", [(i, (i - 1) % count) for i in range(count)])

    def prepare(reverse, blocks, after):
        turned_blocks, products, own = call(
            functools.partial(prep_kernel, reverse),
            [blocks] + [(a, None) for a in after],
            [maps, maps, whole],
            [(depth * species, LANES)],
            1.0,
        )
        partners, kept = [], None
        for level in range(levels - 1):
            if level == 0:
                got = [crossed(own, "gx", 1)]
            else:
                mine = crossed(kept, "gx", 1 << level)
                got = [mine, crossed(mine, "gx", 1)]
            partners += got
            if level + 2 < levels:
                full = level + 3 < levels
                outs = call(
                    functools.partial(join_kernel, level, reverse, full, pairs),
                    [own] + got,
                    [whole, half] if full else [half],
                    [],
                    0.4,
                )
                own, kept = outs[0], outs[-1]
        return turned_blocks, products, partners

    lower, lower_products, lower_partners = prepare(False, x_lower, [])
    upper, upper_products, upper_partners = prepare(True, x_upper, [lower_products])
    rhs, base = call(
        base_kernel, [start, source, diag_inverse, x_upper, side_blocks], [vec, vec], [dup], 1.5
    )
    drive, offsets, sent = call(
        functools.partial(forward_offset_kernel, levels),
        [base, paired, other, ahead, side_blocks, x_upper, lower] + lower_partners,
        [vec, vec, slots],
        [dup],
        1.5,
    )
    forward, copy, base = call(
        functools.partial(forward_kernel, levels),
        [exchange(sent, "gx"), drive, offsets, rhs, lower_products] + lower_partners,
        [vec, vec, vec],
        [],
        1.0,
    )
    paired, other = swaps(copy, "gy")
    (base,) = call(side_kernel, [base, copy, side_blocks], [vec], [dup], 0.7)
    offsets, sent = call(
        functools.partial(backward_offset_kernel, levels),
        [base, paired, other, side_blocks, upper] + upper_partners,
        [vec, slots],
        [dup],
        1.5,
    )
    (result,) = call(
        functools.partial(backward_kernel, levels),
        [exchange(sent, "gx"), offsets, upper_products] + upper_partners,
        [vec],
        [],
        1.0,
    )
    shape = (planes, 1, depth * species)
    return forward.reshape(shape), result.reshape(shape)


def solution(mesh):
    return jax.shard_map(
        local,
        mesh=mesh,
        in_specs=(
            P("gx", "gy", None),
            P("gx", "gy", None),
            P("gx", "gy", None, None),
            P("gx", "gy", None, None),
            P("gx", "gy", None, None),
            P(None, "gx", "gy", None, None),
        ),
        out_specs=(P("gx", "gy", None), P("gx", "gy", None)),
        check_vma=False,
    )
```

```python
import functools

import jax
import jax.numpy as jnp
from jax import lax
from jax.experimental import pallas as pl
from jax.experimental.pallas import tpu as pltpu
from jax.sharding import PartitionSpec as P

LANES = 128
F32 = jnp.float32
BF16 = jnp.bfloat16


def lane_bit(shape, shift):
    return (lax.broadcasted_iota(jnp.int32, shape, len(shape) - 1) & shift) != 0


def segment_sums(leaf, tiles, rows):
    shape = (rows, LANES)

    def node(base, stride, shift):
        if stride == tiles:
            return leaf(base)
        low = node(base, stride * 2, shift * 2)
        high = node(base + stride, stride * 2, shift * 2)
        low = low + pltpu.roll(low, LANES - shift, 1)
        high = high + pltpu.roll(high, shift, 1)
        return jnp.where(lane_bit(shape, shift), high, low)

    part = node(0, 1, 2)
    odd = lane_bit(shape, 1)
    part = part + jnp.where(odd, pltpu.roll(part, 1, 1), pltpu.roll(part, LANES - 1, 1))
    upper = lane_bit(shape, LANES // 2)
    return jnp.where(upper == odd, part, pltpu.roll(part, LANES // 2, 1))


def apply(terms):
    rows = terms[0][1].shape[0]
    tiles = LANES // 4

    def leaf(t):
        return sum(read(t).astype(F32) * vector for read, vector in terms)

    return segment_sums(leaf, tiles, rows)


def reader(ref, *index):
    return lambda t: ref[(*index, slice(None), slice(t * LANES, (t + 1) * LANES))]


def spread(raw):
    half = raw.shape[0]
    row = lax.broadcasted_iota(jnp.int32, raw.shape, 0)
    same = (row & 1 == 1) == lane_bit(raw.shape, LANES // 2)
    parts = []
    for first in (0, half // 2):
        block = jnp.take_along_axis(raw, first + row // 2, 0)
        parts.append(jnp.where(same, block, pltpu.roll(block, LANES // 2, 1)))
    return jnp.concatenate(parts, 0)


def gather_pairs(vector):
    half = vector.shape[0] // 2
    shape = (half, LANES)
    row = lax.broadcasted_iota(jnp.int32, shape, 0)
    upper = lane_bit(shape, LANES // 2)
    parts = []
    for block in (vector[:half], vector[half:]):
        block = jnp.where(upper, pltpu.roll(block, half - 1, 0), block)
        parts.append(jnp.take_along_axis(block, 2 * row & half - 1, 0))
    return jnp.where(row < half // 2, parts[0], parts[1])


def shifted(vector, down):
    rows = vector.shape[0]
    row = lax.broadcasted_iota(jnp.int32, vector.shape, 0)
    if down:
        return jnp.where(row == 0, 0.0, pltpu.roll(vector, 1, 0))
    return jnp.where(row == rows - 1, 0.0, pltpu.roll(vector, rows - 1, 0))


def to_rows(scratch, read, rows, species):
    for a in range(species):
        tile = read(a // 2).astype(F32)
        if a % 2:
            tile = pltpu.roll(tile, LANES // 2, 1)
        scratch[pl.ds(a, rows, stride=species), :] = tile


def halves(a):
    high = a.astype(BF16)
    return high, (a - high.astype(F32)).astype(BF16)


def dot(a, b, dims=((1,), (0,))):
    return lax.dot_general(a, b, (dims, ((), ())), preferred_element_type=F32)


def turn(scratch, out, first, pairs, species):
    unit = (
        lax.broadcasted_iota(jnp.int32, (species, species), 0)
        == lax.broadcasted_iota(jnp.int32, (species, species), 1)
    ).astype(F32).astype(BF16)
    for pair in range(pairs):
        block = scratch[pair * LANES : (pair + 1) * LANES, :species].astype(BF16)
        out[pl.ds(first + pair, species, stride=pairs), :] = dot(unit, block, ((1,), (1,)))


def both(block):
    upper = lane_bit(block.shape, LANES // 2)
    zero = jnp.zeros_like(block)
    return jnp.concatenate([jnp.where(upper, zero, block), jnp.where(upper, block, zero)], 0)


def multiply(earlier, later, exact):
    if exact:
        return dot(earlier.astype(BF16), both(later).astype(BF16))
    earlier_high, earlier_low = halves(earlier)
    high, low = halves(both(later))
    return dot(earlier_high, high) + (dot(earlier_low, high) + dot(earlier_high, low))


def turned(ref, vector, first=0, swapped=None):
    pairs = vector.shape[0]
    lane = lax.broadcasted_iota(jnp.int32, vector.shape, 1)
    side = lane & (LANES // 2)
    refs = [(ref, first)] if swapped is None else [(ref, 0), (swapped, 0)]
    sums = [None] * 4
    total = LANES // 2
    share = total // len(refs)
    for b in range(total):
        held, at = refs[b // share]
        row = at + (b % share) * pairs
        term = held[row : row + pairs, :] * jnp.take_along_axis(vector, side + b, 1)
        sums[b % 4] = term if sums[b % 4] is None else sums[b % 4] + term
    return (sums[0] + sums[1]) + (sums[2] + sums[3])


def prep_kernel(reverse, blocks, beside_it, *refs):
    if not reverse:
        refs[0][...] = beside_it[...]
    maps, products, own, rows_scratch = refs[-4:]
    planes, _, rows, width = blocks.shape
    species = LANES // 2
    pairs = rows // 2
    size = species * pairs
    order = list(range(planes))[::-1] if reverse else list(range(planes))
    for plane in order:
        to_rows(rows_scratch, reader(blocks, plane, 0), rows, species)
        turn(rows_scratch, maps, plane * size, pairs, species)
    for step, plane in enumerate(order):
        at = pl.ds(plane * size, size)
        if step == 0:
            products[at, :] = -maps[at, :]
            continue
        for pair in range(pairs):
            here = pl.ds(plane * size + pair, species, stride=pairs)
            before = pl.ds(order[step - 1] * size + pair, species, stride=pairs)
            products[here, :] = multiply(products[before, :], -maps[here, :], step == 1)
    own[...] = products[pl.ds(order[-1] * size, size), :]


def join_kernel(level, reverse, full, pairs, own, *refs):
    here = (lax.axis_index("gx") >> level) & 1
    core = lax.axis_index("gx") & 1
    species = LANES // 2
    outs = refs[-2:] if full else refs[-1:]
    partner = refs[: len(refs) - len(outs)]
    later_is_own = here == (0 if reverse else 1)
    for pair in range(pairs):
        mine = own[pl.ds(pair, species, stride=pairs), :]
        if len(partner) == 1:
            theirs = partner[0][pl.ds(pair, species, stride=pairs), :]
        else:
            close = partner[0][pl.ds(pair, species // 2, stride=pairs), :]
            far = partner[1][pl.ds(pair, species // 2, stride=pairs), :]
            theirs = jnp.where(
                core == 0, jnp.concatenate([close, far], 0), jnp.concatenate([far, close], 0)
            )
        earlier = jnp.where(later_is_own, theirs, mine)
        later = jnp.where(later_is_own, mine, theirs)
        if full:
            kept = multiply(earlier, later, False)
            outs[0][pl.ds(pair, species, stride=pairs), :] = kept
            kept = jnp.where(core == 0, kept[: species // 2], kept[species // 2 :])
        else:
            kept = jnp.where(core == 0, earlier[: species // 2], earlier[species // 2 :])
            kept = multiply(kept, later, False)
        outs[-1][pl.ds(pair, species // 2, stride=pairs), :] = kept


def base_kernel(start, source, diag, upper, side, rhs, base):
    planes = start.shape[0]
    vectors = [spread(start[p]) for p in range(planes)]
    for p in range(planes):
        own = apply([(reader(diag, p, 0), spread(source[p]))])
        terms = [
            (reader(side, 2, p, 0), shifted(vectors[p], True)),
            (reader(side, 3, p, 0), shifted(vectors[p], False)),
        ]
        if p + 1 < planes:
            terms.append((reader(upper, p, 0), vectors[p + 1]))
        around = apply(terms)
        rhs[p] = gather_pairs(own)
        base[p] = gather_pairs(own - around)


def partner_map(refs, vector):
    if len(refs) == 1:
        return turned(refs[0], vector)
    core = lax.axis_index("gx") & 1
    quarter = LANES // 4
    inner = lane_bit(vector.shape, quarter)
    crossed_over = jnp.where(
        inner, pltpu.roll(vector, quarter, 1), pltpu.roll(vector, LANES - quarter, 1)
    )
    return turned(refs[0], jnp.where(core == 0, vector, crossed_over), 0, refs[1])


def outgoing(offset, partners, here, slots):
    vectors = [offset]
    for level, refs in enumerate(partners):
        passed = partner_map(refs, vectors[-1])
        vectors.append(jnp.where((here >> level) & 1 == 0, passed, vectors[-1]))
    place = lax.axis_index("gx")
    for target in range(slots.shape[0]):
        apart = place ^ target
        value = vectors[0]
        for level in range(1, len(vectors)):
            value = jnp.where(apart >= 1 << level, vectors[level], value)
        slots[target] = value


def incoming(got, partners, here, reverse):
    count = got.shape[0]
    entering = None
    for level in range(len(partners) + 1)[::-1]:
        total = None
        for source in range(count):
            place = count - 1 - source if reverse else source
            term = jnp.where((place >> level) == (here >> level) - 1, got[source], 0.0)
            total = term if total is None else total + term
        if entering is not None:
            total = total + partner_map(partners[level], entering)
        before = jnp.zeros_like(total) if entering is None else entering
        entering = jnp.where((here >> level) & 1 == 1, total, before)
    return entering


def grouped(refs, levels):
    return [list(refs[:1])] + [list(refs[i : i + 2]) for i in range(1, 2 * levels - 3, 2)]


def beside(axis, paired, other):
    place, count = lax.axis_index(axis), lax.axis_size(axis)
    odd = place & 1 == 1
    low = jnp.where(odd, paired, other)
    high = jnp.where(odd, other, paired)
    return jnp.where(place == 0, 0.0, low), jnp.where(place == count - 1, 0.0, high)


def forward_offset_kernel(levels, base, paired, other, ahead, side, upper, lower, *rest):
    *partners, drive, offsets, slots = rest
    planes = base.shape[0]
    size = base.shape[1] * LANES // 2
    here = lax.axis_index("gx")
    last = here == lax.axis_size("gx") - 1
    previous = None
    for p in range(planes):
        low, high = beside("gy", paired[p], other[p])
        terms = [
            (reader(side, 0, p, 0), spread(low)),
            (reader(side, 1, p, 0), spread(high)),
        ]
        if p + 1 == planes:
            beyond = jnp.where(last, 0.0, ahead[0])
            terms.append((reader(upper, p, 0), spread(beyond)))
        fresh = base[p] - gather_pairs(apply(terms))
        drive[p] = fresh
        if previous is not None:
            fresh = fresh - turned(lower, previous, p * size)
        offsets[p] = fresh
        previous = fresh
    outgoing(previous, grouped(partners, levels), here, slots)


def forward_kernel(levels, got, drive, offsets, rhs, products, *rest):
    *partners, out, copy, base = rest
    planes = drive.shape[0]
    size = drive.shape[1] * LANES // 2
    entering = incoming(got, grouped(partners, levels), lax.axis_index("gx"), False)
    for p in range(planes):
        value = offsets[p] + turned(products, entering, p * size)
        base[p] = rhs[p] - (drive[p] - value)
        out[p] = value
        copy[p] = value


def side_kernel(base, vectors, side, out):
    for p in range(base.shape[0]):
        vector = spread(vectors[p])
        around = apply(
            [
                (reader(side, 2, p, 0), shifted(vector, True)),
                (reader(side, 3, p, 0), shifted(vector, False)),
            ]
        )
        out[p] = base[p] - gather_pairs(around)


def backward_offset_kernel(levels, base, paired, other, side, upper, *rest):
    *partners, offsets, slots = rest
    planes = base.shape[0]
    size = base.shape[1] * LANES // 2
    here = lax.axis_size("gx") - 1 - lax.axis_index("gx")
    previous = None
    for p in range(planes)[::-1]:
        low, high = beside("gy", paired[p], other[p])
        around = apply(
            [
                (reader(side, 0, p, 0), spread(low)),
                (reader(side, 1, p, 0), spread(high)),
            ]
        )
        fresh = base[p] - gather_pairs(around)
        if previous is not None:
            fresh = fresh - turned(upper, previous, p * size)
        offsets[p] = fresh
        previous = fresh
    outgoing(previous, grouped(partners, levels), here, slots)


def backward_kernel(levels, got, offsets, products, *rest):
    *partners, out = rest
    size = offsets.shape[1] * LANES // 2
    here = lax.axis_size("gx") - 1 - lax.axis_index("gx")
    entering = incoming(got, grouped(partners, levels), here, True)
    for p in range(offsets.shape[0]):
        out[p] = offsets[p] + turned(products, entering, p * size)


def call(kernel, operands, outs, scratch, micros):
    arrays = [o[0] if isinstance(o, tuple) else o for o in operands]
    held = [i for i, o in enumerate(operands) if isinstance(o, tuple)]
    outs = [jax.ShapeDtypeStruct(shape, F32) for shape in outs]
    moved = sum(a.size * a.dtype.itemsize for a in arrays)

    return pl.pallas_call(
        kernel,
        out_shape=outs,
        in_specs=[
            pl.BlockSpec(memory_space=pl.ANY if i in held else pltpu.VMEM) for i in range(len(arrays))
        ],
        out_specs=[pl.BlockSpec(memory_space=pltpu.VMEM) for _ in outs],
        scratch_shapes=[pltpu.VMEM(shape, F32) for shape in scratch],
        compiler_params=pltpu.CompilerParams(vmem_limit_bytes=24 << 20),
        cost_estimate=pl.CostEstimate(flops=int(micros * 1.15e9), bytes_accessed=moved, transcendentals=0),
    )(*arrays)


def swaps(block):
    count, rows = lax.axis_size("gx"), lax.axis_size("gy")
    route = []
    for place in range(count):
        for row in range(rows):
            target = row + 1 if row & 1 else row - 1
            to = place * rows + target if 0 <= target < rows else (place ^ 1) * rows + row
            route.append((place * rows + row, to))
    return crossed(block, "gy", 1), lax.ppermute(block, ("gx", "gy"), route)


def crossed(block, axis, distance):
    return lax.ppermute(block, axis, [(i, i ^ distance) for i in range(lax.axis_size(axis))])


def exchange(slots, axis):
    return lax.all_to_all(slots, axis, 0, 0)


def local(start, source, diag_inverse, x_lower, x_upper, side_blocks):
    planes, _, depth, width = x_lower.shape
    species = start.shape[2] // depth
    pairs = depth // 2
    count = lax.axis_size("gx")
    levels = count.bit_length() - 1
    size = species * pairs
    one = (pairs, LANES)
    vec = (planes,) + one
    maps = (planes * size, LANES)
    whole, half = (size, LANES), (size // 2, LANES)
    slots = (count,) + one
    start = start.reshape(vec)
    source = source.reshape(vec)

    def prepare(reverse, blocks, other):
        *passed, turned_blocks, products, own = call(
            functools.partial(prep_kernel, reverse),
            [blocks, (other, None) if reverse else other],
            ([] if reverse else [vec]) + [maps, maps, whole],
            [(depth * species, LANES)],
            1.0,
        )
        partners, kept = [], None
        for level in range(levels - 1):
            if level == 0:
                got = [crossed(own, "gx", 1)]
            else:
                mine = crossed(kept, "gx", 1 << level)
                got = [mine, crossed(mine, "gx", 1)]
            partners += got
            if level + 2 < levels:
                full = level + 3 < levels
                outs = call(
                    functools.partial(join_kernel, level, reverse, full, pairs),
                    [own] + got,
                    [whole, half] if full else [half],
                    [],
                    0.4,
                )
                own, kept = outs[0], outs[-1]
        return turned_blocks, products, partners, passed

    lower, lower_products, lower_partners, (start,) = prepare(False, x_lower, start)
    paired, other = swaps(start)
    ahead = lax.ppermute(start[:1], "gx", [(i, (i - 1) % count) for i in range(count)])
    rhs, base = call(
        base_kernel, [start, source, diag_inverse, x_upper, side_blocks], [vec, vec], [], 1.0
    )
    drive, offsets, sent = call(
        functools.partial(forward_offset_kernel, levels),
        [base, paired, other, ahead, side_blocks, x_upper, lower] + lower_partners,
        [vec, vec, slots],
        [],
        1.5,
    )
    upper, upper_products, upper_partners, _ = prepare(True, x_upper, offsets)
    forward, copy, base = call(
        functools.partial(forward_kernel, levels),
        [exchange(sent, "gx"), drive, offsets, rhs, lower_products] + lower_partners,
        [vec, vec, vec],
        [],
        1.0,
    )
    paired, other = swaps(copy)
    (base,) = call(side_kernel, [base, copy, side_blocks], [vec], [], 0.7)
    offsets, sent = call(
        functools.partial(backward_offset_kernel, levels),
        [base, paired, other, side_blocks, upper] + upper_partners,
        [vec, slots],
        [],
        1.5,
    )
    (result,) = call(
        functools.partial(backward_kernel, levels),
        [exchange(sent, "gx"), offsets, upper_products] + upper_partners,
        [vec],
        [],
        1.0,
    )
    shape = (planes, 1, depth * species)
    return forward.reshape(shape), result.reshape(shape)


def solution(mesh):
    return jax.shard_map(
        local,
        mesh=mesh,
        in_specs=(
            P("gx", "gy", None),
            P("gx", "gy", None),
            P("gx", "gy", None, None),
            P("gx", "gy", None, None),
            P("gx", "gy", None, None),
            P(None, "gx", "gy", None, None),
        ),
        out_specs=(P("gx", "gy", None), P("gx", "gy", None)),
        check_vma=False,
    )
```

```python
import functools

import jax
import jax.numpy as jnp
from jax import lax
from jax.experimental import pallas as pl
from jax.experimental.pallas import tpu as pltpu
from jax.sharding import PartitionSpec as P

LANES = 128
F32 = jnp.float32
BF16 = jnp.bfloat16


def lane_bit(shape, shift):
    return (lax.broadcasted_iota(jnp.int32, shape, len(shape) - 1) & shift) != 0


def segment_sums(leaf, tiles, rows):
    shape = (rows, LANES)

    def node(base, stride, shift):
        if stride == tiles:
            return leaf(base)
        low = node(base, stride * 2, shift * 2)
        high = node(base + stride, stride * 2, shift * 2)
        low = low + pltpu.roll(low, LANES - shift, 1)
        high = high + pltpu.roll(high, shift, 1)
        return jnp.where(lane_bit(shape, shift), high, low)

    part = node(0, 1, 2)
    odd = lane_bit(shape, 1)
    part = part + jnp.where(odd, pltpu.roll(part, 1, 1), pltpu.roll(part, LANES - 1, 1))
    upper = lane_bit(shape, LANES // 2)
    return jnp.where(upper == odd, part, pltpu.roll(part, LANES // 2, 1))


def apply(terms):
    rows = terms[0][1].shape[0]
    tiles = LANES // 4

    def leaf(t):
        return sum(read(t).astype(F32) * vector for read, vector in terms)

    return segment_sums(leaf, tiles, rows)


def reader(ref, *index):
    return lambda t: ref[(*index, slice(None), slice(t * LANES, (t + 1) * LANES))]


def spread(raw):
    half = raw.shape[0]
    row = lax.broadcasted_iota(jnp.int32, raw.shape, 0)
    same = (row & 1 == 1) == lane_bit(raw.shape, LANES // 2)
    parts = []
    for first in (0, half // 2):
        block = jnp.take_along_axis(raw, first + row // 2, 0)
        parts.append(jnp.where(same, block, pltpu.roll(block, LANES // 2, 1)))
    return jnp.concatenate(parts, 0)


def gather_pairs(vector):
    half = vector.shape[0] // 2
    shape = (half, LANES)
    row = lax.broadcasted_iota(jnp.int32, shape, 0)
    upper = lane_bit(shape, LANES // 2)
    parts = []
    for block in (vector[:half], vector[half:]):
        block = jnp.where(upper, pltpu.roll(block, half - 1, 0), block)
        parts.append(jnp.take_along_axis(block, 2 * row & half - 1, 0))
    return jnp.where(row < half // 2, parts[0], parts[1])


def shifted(vector, down):
    rows = vector.shape[0]
    row = lax.broadcasted_iota(jnp.int32, vector.shape, 0)
    if down:
        return jnp.where(row == 0, 0.0, pltpu.roll(vector, 1, 0))
    return jnp.where(row == rows - 1, 0.0, pltpu.roll(vector, rows - 1, 0))


def to_rows(scratch, read, rows, species):
    for a in range(species):
        tile = read(a // 2).astype(F32)
        if a % 2:
            tile = pltpu.roll(tile, LANES // 2, 1)
        scratch[pl.ds(a, rows, stride=species), :] = tile


def halves(a):
    high = a.astype(BF16)
    return high, (a - high.astype(F32)).astype(BF16)


def dot(a, b, dims=((1,), (0,))):
    return lax.dot_general(a, b, (dims, ((), ())), preferred_element_type=F32)


def turn(scratch, out, first, pairs, species):
    unit = (
        lax.broadcasted_iota(jnp.int32, (species, species), 0)
        == lax.broadcasted_iota(jnp.int32, (species, species), 1)
    ).astype(F32).astype(BF16)
    for pair in range(pairs):
        block = scratch[pair * LANES : (pair + 1) * LANES, :species].astype(BF16)
        out[pl.ds(first + pair, species, stride=pairs), :] = dot(unit, block, ((1,), (1,)))


def both(block):
    upper = lane_bit(block.shape, LANES // 2)
    zero = jnp.zeros_like(block)
    return jnp.concatenate([jnp.where(upper, zero, block), jnp.where(upper, block, zero)], 0)


def multiply(earlier, later, exact):
    if exact:
        return dot(earlier.astype(BF16), both(later).astype(BF16))
    earlier_high, earlier_low = halves(earlier)
    high, low = halves(both(later))
    return dot(earlier_high, high) + (dot(earlier_low, high) + dot(earlier_high, low))


def turned(ref, vector, first=0, swapped=None):
    pairs = vector.shape[0]
    lane = lax.broadcasted_iota(jnp.int32, vector.shape, 1)
    side = lane & (LANES // 2)
    refs = [(ref, first)] if swapped is None else [(ref, 0), (swapped, 0)]
    sums = [None] * 4
    total = LANES // 2
    share = total // len(refs)
    for b in range(total):
        held, at = refs[b // share]
        row = at + (b % share) * pairs
        term = held[row : row + pairs, :] * jnp.take_along_axis(vector, side + b, 1)
        sums[b % 4] = term if sums[b % 4] is None else sums[b % 4] + term
    return (sums[0] + sums[1]) + (sums[2] + sums[3])


def prep_kernel(reverse, blocks, beside_it, *refs):
    if not reverse:
        refs[0][...] = beside_it[...]
    maps, products, own, rows_scratch = refs[-4:]
    planes, _, rows, width = blocks.shape
    species = LANES // 2
    pairs = rows // 2
    size = species * pairs
    order = list(range(planes))[::-1] if reverse else list(range(planes))
    for plane in order:
        to_rows(rows_scratch, reader(blocks, plane, 0), rows, species)
        turn(rows_scratch, maps, plane * size, pairs, species)
    for step, plane in enumerate(order):
        at = pl.ds(plane * size, size)
        if step == 0:
            products[at, :] = -maps[at, :]
            continue
        for pair in range(pairs):
            here = pl.ds(plane * size + pair, species, stride=pairs)
            before = pl.ds(order[step - 1] * size + pair, species, stride=pairs)
            products[here, :] = multiply(products[before, :], -maps[here, :], step == 1)
    own[...] = products[pl.ds(order[-1] * size, size), :]


def join_kernel(level, reverse, full, pairs, own, *refs):
    here = (lax.axis_index("gx") >> level) & 1
    core = lax.axis_index("gx") & 1
    species = LANES // 2
    outs = refs[-2:] if full else refs[-1:]
    partner = refs[: len(refs) - len(outs)]
    later_is_own = here == (0 if reverse else 1)
    for pair in range(pairs):
        mine = own[pl.ds(pair, species, stride=pairs), :]
        if len(partner) == 1:
            theirs = partner[0][pl.ds(pair, species, stride=pairs), :]
        else:
            close = partner[0][pl.ds(pair, species // 2, stride=pairs), :]
            far = partner[1][pl.ds(pair, species // 2, stride=pairs), :]
            theirs = jnp.where(
                core == 0, jnp.concatenate([close, far], 0), jnp.concatenate([far, close], 0)
            )
        earlier = jnp.where(later_is_own, theirs, mine)
        later = jnp.where(later_is_own, mine, theirs)
        if full:
            kept = multiply(earlier, later, False)
            outs[0][pl.ds(pair, species, stride=pairs), :] = kept
            kept = jnp.where(core == 0, kept[: species // 2], kept[species // 2 :])
        else:
            kept = jnp.where(core == 0, earlier[: species // 2], earlier[species // 2 :])
            kept = multiply(kept, later, False)
        outs[-1][pl.ds(pair, species // 2, stride=pairs), :] = kept


def base_kernel(start, source, diag, upper, side, rhs, base):
    planes = start.shape[0]
    vectors = [spread(start[p]) for p in range(planes)]
    for p in range(planes):
        own = apply([(reader(diag, p, 0), spread(source[p]))])
        terms = [
            (reader(side, 2, p, 0), shifted(vectors[p], True)),
            (reader(side, 3, p, 0), shifted(vectors[p], False)),
        ]
        if p + 1 < planes:
            terms.append((reader(upper, p, 0), vectors[p + 1]))
        around = apply(terms)
        rhs[p] = gather_pairs(own)
        base[p] = gather_pairs(own - around)


def partner_map(refs, vector):
    if len(refs) == 1:
        return turned(refs[0], vector)
    core = lax.axis_index("gx") & 1
    quarter = LANES // 4
    inner = lane_bit(vector.shape, quarter)
    crossed_over = jnp.where(
        inner, pltpu.roll(vector, quarter, 1), pltpu.roll(vector, LANES - quarter, 1)
    )
    return turned(refs[0], jnp.where(core == 0, vector, crossed_over), 0, refs[1])


def outgoing(offset, partners, here, slots):
    vectors = [offset]
    for level, refs in enumerate(partners):
        passed = partner_map(refs, vectors[-1])
        vectors.append(jnp.where((here >> level) & 1 == 0, passed, vectors[-1]))
    place = lax.axis_index("gx")
    for target in range(slots.shape[0]):
        apart = place ^ target
        value = vectors[0]
        for level in range(1, len(vectors)):
            value = jnp.where(apart >= 1 << level, vectors[level], value)
        slots[target] = value


def incoming(got, partners, here, reverse):
    count = got.shape[0]
    entering = None
    for level in range(len(partners) + 1)[::-1]:
        total = None
        for source in range(count):
            place = count - 1 - source if reverse else source
            term = jnp.where((place >> level) == (here >> level) - 1, got[source], 0.0)
            total = term if total is None else total + term
        if entering is not None:
            total = total + partner_map(partners[level], entering)
        before = jnp.zeros_like(total) if entering is None else entering
        entering = jnp.where((here >> level) & 1 == 1, total, before)
    return entering


def grouped(refs, levels):
    return [list(refs[:1])] + [list(refs[i : i + 2]) for i in range(1, 2 * levels - 3, 2)]


def beside(axis, paired, other):
    place, count = lax.axis_index(axis), lax.axis_size(axis)
    odd = place & 1 == 1
    low = jnp.where(odd, paired, other)
    high = jnp.where(odd, other, paired)
    return jnp.where(place == 0, 0.0, low), jnp.where(place == count - 1, 0.0, high)


def forward_offset_kernel(levels, base, paired, other, ahead, side, upper, lower, *rest):
    *partners, drive, offsets, slots = rest
    planes = base.shape[0]
    size = base.shape[1] * LANES // 2
    here = lax.axis_index("gx")
    last = here == lax.axis_size("gx") - 1
    previous = None
    for p in range(planes):
        low, high = beside("gy", paired[p], other[p])
        terms = [
            (reader(side, 0, p, 0), spread(low)),
            (reader(side, 1, p, 0), spread(high)),
        ]
        if p + 1 == planes:
            beyond = jnp.where(last, 0.0, ahead[0])
            terms.append((reader(upper, p, 0), spread(beyond)))
        fresh = base[p] - gather_pairs(apply(terms))
        drive[p] = fresh
        if previous is not None:
            fresh = fresh - turned(lower, previous, p * size)
        offsets[p] = fresh
        previous = fresh
    outgoing(previous, grouped(partners, levels), here, slots)


def forward_kernel(levels, got, drive, offsets, rhs, products, *rest):
    *partners, out, copy, base = rest
    planes = drive.shape[0]
    size = drive.shape[1] * LANES // 2
    entering = incoming(got, grouped(partners, levels), lax.axis_index("gx"), False)
    for p in range(planes):
        value = offsets[p] + turned(products, entering, p * size)
        base[p] = rhs[p] - (drive[p] - value)
        out[p] = value
        copy[p] = value


def side_kernel(base, vectors, side, out):
    for p in range(base.shape[0]):
        vector = spread(vectors[p])
        around = apply(
            [
                (reader(side, 2, p, 0), shifted(vector, True)),
                (reader(side, 3, p, 0), shifted(vector, False)),
            ]
        )
        out[p] = base[p] - gather_pairs(around)


def backward_offset_kernel(levels, base, paired, other, side, upper, *rest):
    *partners, offsets, slots = rest
    planes = base.shape[0]
    size = base.shape[1] * LANES // 2
    here = lax.axis_size("gx") - 1 - lax.axis_index("gx")
    previous = None
    for p in range(planes)[::-1]:
        low, high = beside("gy", paired[p], other[p])
        around = apply(
            [
                (reader(side, 0, p, 0), spread(low)),
                (reader(side, 1, p, 0), spread(high)),
            ]
        )
        fresh = base[p] - gather_pairs(around)
        if previous is not None:
            fresh = fresh - turned(upper, previous, p * size)
        offsets[p] = fresh
        previous = fresh
    outgoing(previous, grouped(partners, levels), here, slots)


def backward_kernel(levels, got, offsets, products, *rest):
    *partners, out = rest
    size = offsets.shape[1] * LANES // 2
    here = lax.axis_size("gx") - 1 - lax.axis_index("gx")
    entering = incoming(got, grouped(partners, levels), here, True)
    for p in range(offsets.shape[0]):
        out[p] = offsets[p] + turned(products, entering, p * size)


def call(kernel, operands, outs, scratch, micros):
    arrays = [o[0] if isinstance(o, tuple) else o for o in operands]
    held = [i for i, o in enumerate(operands) if isinstance(o, tuple)]
    outs = [jax.ShapeDtypeStruct(shape, F32) for shape in outs]
    moved = sum(a.size * a.dtype.itemsize for a in arrays)

    return pl.pallas_call(
        kernel,
        out_shape=outs,
        in_specs=[
            pl.BlockSpec(memory_space=pl.ANY if i in held else pltpu.VMEM) for i in range(len(arrays))
        ],
        out_specs=[pl.BlockSpec(memory_space=pltpu.VMEM) for _ in outs],
        scratch_shapes=[pltpu.VMEM(shape, F32) for shape in scratch],
        compiler_params=pltpu.CompilerParams(vmem_limit_bytes=24 << 20),
        cost_estimate=pl.CostEstimate(flops=int(micros * 1.15e9), bytes_accessed=moved, transcendentals=0),
    )(*arrays)


def swaps(block):
    count, rows = lax.axis_size("gx"), lax.axis_size("gy")
    route = []
    for place in range(count):
        for row in range(rows):
            target = row + 1 if row & 1 else row - 1
            to = place * rows + target if 0 <= target < rows else (place ^ 1) * rows + row
            route.append((place * rows + row, to))
    return crossed(block, "gy", 1), lax.ppermute(block, ("gx", "gy"), route)


def crossed(block, axis, distance):
    return lax.ppermute(block, axis, [(i, i ^ distance) for i in range(lax.axis_size(axis))])


def exchange(slots, axis):
    return lax.all_to_all(slots, axis, 0, 0)


def local(start, source, diag_inverse, x_lower, x_upper, side_blocks):
    planes, _, depth, width = x_lower.shape
    species = start.shape[2] // depth
    pairs = depth // 2
    count = lax.axis_size("gx")
    levels = count.bit_length() - 1
    size = species * pairs
    one = (pairs, LANES)
    vec = (planes,) + one
    maps = (planes * size, LANES)
    whole, half = (size, LANES), (size // 2, LANES)
    slots = (count,) + one
    start = start.reshape(vec)
    source = source.reshape(vec)

    def prepare(reverse, blocks, other):
        *passed, turned_blocks, products, own = call(
            functools.partial(prep_kernel, reverse),
            [blocks, (other, None) if reverse else other],
            ([] if reverse else [vec]) + [maps, maps, whole],
            [(depth * species, LANES)],
            1.0,
        )
        partners, kept = [], None
        for level in range(levels - 1):
            if level == 0:
                got = [crossed(own, "gx", 1)]
            else:
                mine = crossed(kept, "gx", 1 << level)
                got = [mine, crossed(mine, "gx", 1)]
            partners += got
            if level + 2 < levels:
                full = level + 3 < levels
                outs = call(
                    functools.partial(join_kernel, level, reverse, full, pairs),
                    [own] + got,
                    [whole, half] if full else [half],
                    [],
                    0.4,
                )
                own, kept = outs[0], outs[-1]
        return turned_blocks, products, partners, passed

    lower, lower_products, lower_partners, (start,) = prepare(False, x_lower, start)
    upper, upper_products, upper_partners, _ = prepare(True, x_upper, lower_products)
    paired, other = swaps(start)
    ahead = lax.ppermute(start[:1], "gx", [(i, (i - 1) % count) for i in range(count)])
    rhs, base = call(
        base_kernel, [start, source, diag_inverse, x_upper, side_blocks], [vec, vec], [], 5.0
    )
    drive, offsets, sent = call(
        functools.partial(forward_offset_kernel, levels),
        [base, paired, other, ahead, side_blocks, x_upper, lower] + lower_partners,
        [vec, vec, slots],
        [],
        1.5,
    )
    forward, copy, base = call(
        functools.partial(forward_kernel, levels),
        [exchange(sent, "gx"), drive, offsets, rhs, lower_products] + lower_partners,
        [vec, vec, vec],
        [],
        1.0,
    )
    paired, other = swaps(copy)
    (base,) = call(side_kernel, [base, copy, side_blocks], [vec], [], 0.7)
    offsets, sent = call(
        functools.partial(backward_offset_kernel, levels),
        [base, paired, other, side_blocks, upper] + upper_partners,
        [vec, slots],
        [],
        1.5,
    )
    (result,) = call(
        functools.partial(backward_kernel, levels),
        [exchange(sent, "gx"), offsets, upper_products] + upper_partners,
        [vec],
        [],
        1.0,
    )
    shape = (planes, 1, depth * species)
    return forward.reshape(shape), result.reshape(shape)


def solution(mesh):
    return jax.shard_map(
        local,
        mesh=mesh,
        in_specs=(
            P("gx", "gy", None),
            P("gx", "gy", None),
            P("gx", "gy", None, None),
            P("gx", "gy", None, None),
            P("gx", "gy", None, None),
            P(None, "gx", "gy", None, None),
        ),
        out_specs=(P("gx", "gy", None), P("gx", "gy", None)),
        check_vma=False,
    )
```

```python
import functools

import jax
import jax.numpy as jnp
from jax import lax
from jax.experimental import pallas as pl
from jax.experimental.pallas import tpu as pltpu
from jax.sharding import PartitionSpec as P

LANES = 128
F32 = jnp.float32
BF16 = jnp.bfloat16


def lane_bit(shape, shift):
    return (lax.broadcasted_iota(jnp.int32, shape, len(shape) - 1) & shift) != 0


def segment_sums(leaf, tiles, rows):
    shape = (rows, LANES)

    def node(base, stride, shift):
        if stride == tiles:
            return leaf(base)
        low = node(base, stride * 2, shift * 2)
        high = node(base + stride, stride * 2, shift * 2)
        low = low + pltpu.roll(low, LANES - shift, 1)
        high = high + pltpu.roll(high, shift, 1)
        return jnp.where(lane_bit(shape, shift), high, low)

    part = node(0, 1, 2)
    odd = lane_bit(shape, 1)
    part = part + jnp.where(odd, pltpu.roll(part, 1, 1), pltpu.roll(part, LANES - 1, 1))
    upper = lane_bit(shape, LANES // 2)
    return jnp.where(upper == odd, part, pltpu.roll(part, LANES // 2, 1))


def apply(terms):
    rows = terms[0][1].shape[0]
    tiles = LANES // 4

    def leaf(t):
        return sum(read(t).astype(F32) * vector for read, vector in terms)

    return segment_sums(leaf, tiles, rows)


def reader(ref, *index):
    return lambda t: ref[(*index, slice(None), slice(t * LANES, (t + 1) * LANES))]


def lanes(shape):
    return lax.broadcasted_iota(jnp.int32, shape, 1)


def woven(raw):
    lane = lanes(raw.shape)
    return jnp.take_along_axis(raw, (lane >> 1) + (lane & 1) * (LANES // 2), 1)


def unwoven(vector):
    lane = lanes(vector.shape)
    return jnp.take_along_axis(vector, (lane & LANES // 2 - 1) * 2 + lane // (LANES // 2), 1)


def spread(vector):
    half = vector.shape[0]
    row = lax.broadcasted_iota(jnp.int32, vector.shape, 0)
    place = (lanes(vector.shape) & LANES // 2 - 1) * 2 + (row & 1)
    parts = []
    for first in (0, half // 2):
        block = jnp.take_along_axis(vector, first + row // 2, 0)
        parts.append(jnp.take_along_axis(block, place, 1))
    return jnp.concatenate(parts, 0)


def gather_pairs(vector):
    half = vector.shape[0] // 2
    shape = (half, LANES)
    row = lax.broadcasted_iota(jnp.int32, shape, 0)
    odd = lane_bit(shape, 1)
    parts = []
    for block in (vector[:half], vector[half:]):
        block = jnp.take_along_axis(block, lanes(shape) >> 1, 1)
        block = jnp.where(odd, pltpu.roll(block, half - 1, 0), block)
        parts.append(jnp.take_along_axis(block, 2 * row & half - 1, 0))
    return jnp.where(row < half // 2, parts[0], parts[1])


def shifted(vector, down):
    rows = vector.shape[0]
    row = lax.broadcasted_iota(jnp.int32, vector.shape, 0)
    if down:
        return jnp.where(row == 0, 0.0, pltpu.roll(vector, 1, 0))
    return jnp.where(row == rows - 1, 0.0, pltpu.roll(vector, rows - 1, 0))


def to_rows(scratch, native, read, rows, species):
    pairs = rows // 2
    for t in range(species // 2):
        native[t * rows : (t + 1) * rows, :] = read(t).astype(F32)
    for t in range(species // 2):
        for inner in (0, 1):
            tile = native[pl.ds(t * rows + inner, pairs, stride=2), :]
            other = pltpu.roll(tile, LANES // 2, 1)
            scratch[pl.ds(4 * t + inner, pairs, stride=LANES), :] = tile
            scratch[pl.ds(4 * t + 2 + inner, pairs, stride=LANES), :] = other


def halves(a):
    high = a.astype(BF16)
    return high, (a - high.astype(F32)).astype(BF16)


def dot(a, b, dims=((1,), (0,))):
    return lax.dot_general(a, b, (dims, ((), ())), preferred_element_type=F32)


def turn(scratch, out, first, pairs, species):
    unit = (
        lax.broadcasted_iota(jnp.int32, (species, species), 0)
        == lax.broadcasted_iota(jnp.int32, (species, species), 1)
    ).astype(F32).astype(BF16)
    for pair in range(pairs):
        block = scratch[pair * LANES : (pair + 1) * LANES, :species].astype(BF16)
        out[pl.ds(first + pair, species, stride=pairs), :] = dot(unit, block, ((1,), (1,)))


def both(scratch, pair, block):
    odd = lane_bit(block.shape, 1)
    zero = jnp.zeros_like(block)
    scratch[pl.ds(pair * LANES, block.shape[0], stride=2), :] = jnp.where(odd, zero, block)
    scratch[pl.ds(pair * LANES + 1, block.shape[0], stride=2), :] = jnp.where(odd, block, zero)
    return scratch[pair * LANES : (pair + 1) * LANES, :]


def multiply(scratch, pair, earlier, later, exact):
    later = both(scratch, pair, later)
    if exact:
        return dot(earlier.astype(BF16), later.astype(BF16))
    earlier_high, earlier_low = halves(earlier)
    high, low = halves(later)
    return dot(earlier_high, high) + (dot(earlier_low, high) + dot(earlier_high, low))


STEP = 8


def diagonals(tiles, out, first):
    count = len(tiles)
    shape = tiles[0].shape
    shift = 1
    while shift < count:
        here = lane_bit(shape, 2 * shift)
        tiles = [jnp.where(here, tiles[(j + shift) % count], tiles[j]) for j in range(count)]
        shift *= 2
    for j, tile in enumerate(tiles):
        turn_by = j // STEP * STEP * 2
        at = first + j * shape[0]
        out[at : at + shape[0], :] = pltpu.roll(tile, turn_by, 1) if turn_by else tile


def whole_tiles(ref, first, pairs, count=LANES // 2):
    return [ref[first + b * pairs : first + (b + 1) * pairs, :] for b in range(count)]


def part_tiles(mine, other, pairs):
    first_core = lax.axis_index("gx") & 1 == 0
    halves_of = [whole_tiles(ref, 0, pairs, LANES // 4) for ref in (mine, other)]
    low = [jnp.where(first_core, a, b) for a, b in zip(*halves_of)]
    high = [jnp.where(first_core, b, a) for a, b in zip(*halves_of)]
    return low + high


def mapped(ref, vector, first=0):
    pairs = vector.shape[0]
    turns = [vector] + [pltpu.roll(vector, LANES - 2 * j, 1) for j in range(1, STEP)]
    total = None
    for giant in range(LANES // 2 // STEP):
        terms = []
        for j in range(STEP):
            at = first + (giant * STEP + j) * pairs
            terms.append(ref[at : at + pairs, :] * turns[j])
        while len(terms) > 1:
            terms = [a + b for a, b in zip(terms[::2], terms[1::2])]
        part = pltpu.roll(terms[0], LANES - 2 * STEP * giant, 1) if giant else terms[0]
        total = part if total is None else total + part
    return total


def prep_kernel(reverse, blocks, beside_it, *refs):
    *passed, maps, products, own, held, held_start, native, rows_scratch, semaphores = refs
    planes, _, rows, width = blocks.shape
    species = LANES // 2
    pairs = rows // 2
    size = species * pairs
    order = list(range(planes))[::-1] if reverse else list(range(planes))
    copies = [
        pltpu.make_async_copy(blocks.at[p], held.at[p], semaphores.at[p]) for p in range(planes)
    ]
    for plane in order:
        copies[plane].start()
    if passed:
        copy = pltpu.make_async_copy(beside_it, held_start, semaphores.at[planes])
        copy.start()
        copy.wait()
        for p in range(planes):
            passed[0][p] = woven(held_start[p])
    for plane in order:
        copies[plane].wait()
        to_rows(rows_scratch, native, reader(held, plane, 0), rows, species)
        turn(rows_scratch, maps, plane * size, pairs, species)
    for step, plane in enumerate(order):
        at = pl.ds(plane * size, size)
        if step == 0:
            products[at, :] = -maps[at, :]
            continue
        for pair in range(pairs):
            here = pl.ds(plane * size + pair, species, stride=pairs)
            before = pl.ds(order[step - 1] * size + pair, species, stride=pairs)
            products[here, :] = multiply(
                rows_scratch, pair, products[before, :], -maps[here, :], step == 1
            )
    own[...] = products[pl.ds(order[-1] * size, size), :]


def join_kernel(level, reverse, full, pairs, own, *refs):
    here = (lax.axis_index("gx") >> level) & 1
    core = lax.axis_index("gx") & 1
    species = LANES // 2
    *refs, scratch = refs
    outs = refs[-2:] if full else refs[-1:]
    partner = refs[: len(refs) - len(outs)]
    later_is_own = here == (0 if reverse else 1)
    for pair in range(pairs):
        mine = own[pl.ds(pair, species, stride=pairs), :]
        if len(partner) == 1:
            theirs = partner[0][pl.ds(pair, species, stride=pairs), :]
        else:
            close = partner[0][pl.ds(pair, species // 2, stride=pairs), :]
            far = partner[1][pl.ds(pair, species // 2, stride=pairs), :]
            theirs = jnp.where(
                core == 0, jnp.concatenate([close, far], 0), jnp.concatenate([far, close], 0)
            )
        earlier = jnp.where(later_is_own, theirs, mine)
        later = jnp.where(later_is_own, mine, theirs)
        if full:
            kept = multiply(scratch, pair, earlier, later, False)
            outs[0][pl.ds(pair, species, stride=pairs), :] = kept
            kept = jnp.where(core == 0, kept[: species // 2], kept[species // 2 :])
        else:
            kept = jnp.where(core == 0, earlier[: species // 2], earlier[species // 2 :])
            kept = multiply(scratch, pair, kept, later, False)
        outs[-1][pl.ds(pair, species // 2, stride=pairs), :] = kept


def base_kernel(start, source, diag, upper, side, maps, products, partner, *outs):
    rhs, base, step_maps, entry_maps, near_map = outs
    planes, pairs = start.shape[:2]
    size = pairs * LANES // 2
    vectors = [spread(start[p]) for p in range(planes)]
    for p in range(planes):
        own = apply([(reader(diag, p, 0), spread(woven(source[p])))])
        terms = [
            (reader(side, 2, p, 0), shifted(vectors[p], True)),
            (reader(side, 3, p, 0), shifted(vectors[p], False)),
        ]
        if p + 1 < planes:
            terms.append((reader(upper, p, 0), vectors[p + 1]))
        around = apply(terms)
        rhs[p] = gather_pairs(own)
        base[p] = gather_pairs(own - around)
    for p in range(planes):
        if p:
            diagonals(whole_tiles(maps, p * size, pairs), step_maps, p * size)
        diagonals(whole_tiles(products, p * size, pairs), entry_maps, p * size)
    diagonals(whole_tiles(partner, 0, pairs), near_map, 0)


def outgoing(offset, partners, here, slots):
    vectors = [offset]
    for level, ref in enumerate(partners):
        passed = mapped(ref, vectors[-1])
        vectors.append(jnp.where((here >> level) & 1 == 0, passed, vectors[-1]))
    place = lax.axis_index("gx")
    for target in range(slots.shape[0]):
        apart = place ^ target
        value = vectors[0]
        for level in range(1, len(vectors)):
            value = jnp.where(apart >= 1 << level, vectors[level], value)
        slots[target] = value


def incoming(got, partners, here, reverse):
    count = got.shape[0]
    entering = None
    for level in range(len(partners) + 1)[::-1]:
        total = None
        for source in range(count):
            place = count - 1 - source if reverse else source
            term = jnp.where((place >> level) == (here >> level) - 1, got[source], 0.0)
            total = term if total is None else total + term
        if entering is not None:
            total = total + mapped(partners[level], entering)
        before = jnp.zeros_like(total) if entering is None else entering
        entering = jnp.where((here >> level) & 1 == 1, total, before)
    return entering


def beside(axis, paired, other):
    place, count = lax.axis_index(axis), lax.axis_size(axis)
    odd = place & 1 == 1
    low = jnp.where(odd, paired, other)
    high = jnp.where(odd, other, paired)
    return jnp.where(place == 0, 0.0, low), jnp.where(place == count - 1, 0.0, high)


def forward_offset_kernel(levels, base, paired, other, ahead, side, upper, step_maps, near, *rest):
    parts, (drive, offsets, slots, *far) = rest[: 2 * (levels - 2)], rest[2 * (levels - 2) :]
    planes, pairs = base.shape[:2]
    size = pairs * LANES // 2
    here = lax.axis_index("gx")
    last = here == lax.axis_size("gx") - 1
    for level, ref in enumerate(far):
        diagonals(part_tiles(*parts[2 * level : 2 * level + 2], pairs), ref, 0)
    previous = None
    for p in range(planes):
        low, high = beside("gy", paired[p], other[p])
        terms = [(reader(side, 0, p, 0), spread(low)), (reader(side, 1, p, 0), spread(high))]
        if p + 1 == planes:
            beyond = jnp.where(last, 0.0, ahead[0])
            terms.append((reader(upper, p, 0), spread(beyond)))
        fresh = base[p] - gather_pairs(apply(terms))
        drive[p] = fresh
        if previous is not None:
            fresh = fresh - mapped(step_maps, previous, p * size)
        offsets[p] = fresh
        previous = fresh
    outgoing(previous, [near, *far], here, slots)


def forward_kernel(got, drive, offsets, rhs, entry_maps, *rest):
    *partners, out, copy, base = rest
    planes = drive.shape[0]
    size = drive.shape[1] * LANES // 2
    entering = incoming(got, partners, lax.axis_index("gx"), False)
    for p in range(planes):
        value = offsets[p] + mapped(entry_maps, entering, p * size)
        base[p] = rhs[p] - (drive[p] - value)
        out[p] = unwoven(value)
        copy[p] = value


def side_kernel(levels, base, vectors, side, maps, products, partner, *rest):
    parts = rest[: 2 * (levels - 2)]
    out, step_maps, entry_maps, near, *far = rest[2 * (levels - 2) :]
    planes, pairs = base.shape[:2]
    size = pairs * LANES // 2
    for p in range(planes):
        vector = spread(vectors[p])
        around = apply(
            [
                (reader(side, 2, p, 0), shifted(vector, True)),
                (reader(side, 3, p, 0), shifted(vector, False)),
            ]
        )
        out[p] = base[p] - gather_pairs(around)
        if p + 1 < planes:
            diagonals(whole_tiles(maps, p * size, pairs), step_maps, p * size)
        diagonals(whole_tiles(products, p * size, pairs), entry_maps, p * size)
    diagonals(whole_tiles(partner, 0, pairs), near, 0)
    for level, ref in enumerate(far):
        diagonals(part_tiles(*parts[2 * level : 2 * level + 2], pairs), ref, 0)


def backward_offset_kernel(base, paired, other, side, step_maps, *rest):
    *partners, offsets, slots = rest
    planes = base.shape[0]
    size = base.shape[1] * LANES // 2
    here = lax.axis_size("gx") - 1 - lax.axis_index("gx")
    previous = None
    for p in range(planes)[::-1]:
        low, high = beside("gy", paired[p], other[p])
        around = apply([(reader(side, 0, p, 0), spread(low)), (reader(side, 1, p, 0), spread(high))])
        fresh = base[p] - gather_pairs(around)
        if previous is not None:
            fresh = fresh - mapped(step_maps, previous, p * size)
        offsets[p] = fresh
        previous = fresh
    outgoing(previous, partners, here, slots)


def backward_kernel(got, offsets, entry_maps, *rest):
    *partners, out = rest
    size = offsets.shape[1] * LANES // 2
    here = lax.axis_size("gx") - 1 - lax.axis_index("gx")
    entering = incoming(got, partners, here, True)
    for p in range(offsets.shape[0]):
        out[p] = unwoven(offsets[p] + mapped(entry_maps, entering, p * size))


def call(kernel, operands, outs, scratch, micros):
    arrays = [o[0] if isinstance(o, tuple) else o for o in operands]
    held = [i for i, o in enumerate(operands) if isinstance(o, tuple)]
    outs = [jax.ShapeDtypeStruct(shape, F32) for shape in outs]
    moved = sum(a.size * a.dtype.itemsize for a in arrays)
    return pl.pallas_call(
        kernel,
        out_shape=outs,
        in_specs=[
            pl.BlockSpec(memory_space=pltpu.HBM if i in held else pltpu.VMEM) for i in range(len(arrays))
        ],
        out_specs=[pl.BlockSpec(memory_space=pltpu.VMEM) for _ in outs],
        scratch_shapes=[pltpu.VMEM(s, F32) if isinstance(s, tuple) else s for s in scratch],
        compiler_params=pltpu.CompilerParams(vmem_limit_bytes=24 << 20),
        cost_estimate=pl.CostEstimate(
            flops=int(micros * 1.15e9), bytes_accessed=moved, transcendentals=0
        ),
    )(*arrays)


def swaps(block):
    count, rows = lax.axis_size("gx"), lax.axis_size("gy")
    route = []
    for place in range(count):
        for row in range(rows):
            target = row + 1 if row & 1 else row - 1
            to = place * rows + target if 0 <= target < rows else (place ^ 1) * rows + row
            route.append((place * rows + row, to))
    return crossed(block, "gy", 1), lax.ppermute(block, ("gx", "gy"), route)


def crossed(block, axis, distance):
    return lax.ppermute(block, axis, [(i, i ^ distance) for i in range(lax.axis_size(axis))])


def exchange(slots, axis):
    return lax.all_to_all(slots, axis, 0, 0)


def local(start, source, diag_inverse, x_lower, x_upper, side_blocks):
    planes, _, depth, width = x_lower.shape
    species = start.shape[2] // depth
    pairs = depth // 2
    count = lax.axis_size("gx")
    levels = count.bit_length() - 1
    size = species * pairs
    one = (pairs, LANES)
    vec = (planes,) + one
    maps = (planes * size, LANES)
    whole, half = (size, LANES), (size // 2, LANES)
    slots = (count,) + one
    start = start.reshape(vec)
    source = source.reshape(vec)

    def prepare(reverse, blocks, other):
        *passed, maps_of, products, own = call(
            functools.partial(prep_kernel, reverse),
            [(blocks, None), other if reverse else (other, None)],
            ([] if reverse else [vec]) + [maps, maps, whole],
            [
                pltpu.VMEM(blocks.shape, blocks.dtype),
                vec,
                (depth * species // 2, LANES),
                (depth * species, LANES),
                pltpu.SemaphoreType.DMA((planes + 1,)),
            ],
            1.0,
        )
        partners, kept = [], None
        for level in range(levels - 1):
            if level == 0:
                got = [crossed(own, "gx", 1)]
            else:
                mine = crossed(kept, "gx", 1 << level)
                got = [mine, crossed(mine, "gx", 1)]
            partners += got
            if level + 2 < levels:
                full = level + 3 < levels
                outs = call(
                    functools.partial(join_kernel, level, reverse, full, pairs),
                    [own] + got,
                    [whole, half] if full else [half],
                    [(depth * species, LANES)],
                    0.4,
                )
                own, kept = outs[0], outs[-1]
        return [maps_of, products, *partners], passed

    lower, (start,) = prepare(False, x_lower, start)
    upper, _ = prepare(True, x_upper, lower[1])
    paired, other = swaps(start)
    ahead = lax.ppermute(start[:1], "gx", [(i, (i - 1) % count) for i in range(count)])

    far = [whole] * (levels - 2)
    rhs, base, step_maps, entry_maps, near = call(
        base_kernel,
        [start, source, diag_inverse, x_upper, side_blocks] + lower[:3],
        [vec, vec, maps, maps, whole],
        [],
        5.0,
    )
    drive, offsets, sent, *partners = call(
        functools.partial(forward_offset_kernel, levels),
        [base, paired, other, ahead, side_blocks, x_upper, step_maps, near] + lower[3:],
        [vec, vec, slots] + far,
        [],
        1.5,
    )
    forward, copy, base = call(
        forward_kernel,
        [exchange(sent, "gx"), drive, offsets, rhs, entry_maps, near] + partners,
        [vec, vec, vec],
        [],
        1.0,
    )
    paired, other = swaps(copy)
    base, step_maps, entry_maps, *partners = call(
        functools.partial(side_kernel, levels),
        [base, copy, side_blocks] + upper,
        [vec, maps, maps, whole] + far,
        [],
        0.7,
    )
    offsets, sent = call(
        backward_offset_kernel,
        [base, paired, other, side_blocks, step_maps] + partners,
        [vec, slots],
        [],
        1.5,
    )
    (result,) = call(
        backward_kernel, [exchange(sent, "gx"), offsets, entry_maps] + partners, [vec], [], 1.0
    )
    shape = (planes, 1, depth * species)
    return forward.reshape(shape), result.reshape(shape)


def solution(mesh):
    return jax.shard_map(
        local,
        mesh=mesh,
        in_specs=(
            P("gx", "gy", None),
            P("gx", "gy", None),
            P("gx", "gy", None, None),
            P("gx", "gy", None, None),
            P("gx", "gy", None, None),
            P(None, "gx", "gy", None, None),
        ),
        out_specs=(P("gx", "gy", None), P("gx", "gy", None)),
        check_vma=False,
    )
```

```python
import functools

import jax
import jax.numpy as jnp
from jax import lax
from jax.experimental import pallas as pl
from jax.experimental.pallas import tpu as pltpu
from jax.sharding import PartitionSpec as P

LANES = 128
F32 = jnp.float32
BF16 = jnp.bfloat16


def lane_bit(shape, shift):
    return (lax.broadcasted_iota(jnp.int32, shape, len(shape) - 1) & shift) != 0


def segment_sums(leaf, tiles, rows):
    shape = (rows, LANES)

    def node(base, stride, shift):
        if stride == tiles:
            return leaf(base)
        low = node(base, stride * 2, shift * 2)
        high = node(base + stride, stride * 2, shift * 2)
        low = low + pltpu.roll(low, LANES - shift, 1)
        high = high + pltpu.roll(high, shift, 1)
        return jnp.where(lane_bit(shape, shift), high, low)

    part = node(0, 1, 2)
    odd = lane_bit(shape, 1)
    part = part + jnp.where(odd, pltpu.roll(part, 1, 1), pltpu.roll(part, LANES - 1, 1))
    upper = lane_bit(shape, LANES // 2)
    return jnp.where(upper == odd, part, pltpu.roll(part, LANES // 2, 1))


def apply(terms):
    rows = terms[0][1].shape[0]
    tiles = LANES // 4

    def leaf(t):
        return sum(read(t).astype(F32) * vector for read, vector in terms)

    return segment_sums(leaf, tiles, rows)


def reader(ref, *index):
    return lambda t: ref[(*index, slice(None), slice(t * LANES, (t + 1) * LANES))]


def lanes(shape):
    return lax.broadcasted_iota(jnp.int32, shape, 1)


def woven(raw):
    lane = lanes(raw.shape)
    return jnp.take_along_axis(raw, (lane >> 1) + (lane & 1) * (LANES // 2), 1)


def unwoven(vector):
    lane = lanes(vector.shape)
    return jnp.take_along_axis(vector, (lane & LANES // 2 - 1) * 2 + lane // (LANES // 2), 1)


def spread(vector):
    half = vector.shape[0]
    row = lax.broadcasted_iota(jnp.int32, vector.shape, 0)
    place = (lanes(vector.shape) & LANES // 2 - 1) * 2 + (row & 1)
    parts = []
    for first in (0, half // 2):
        block = jnp.take_along_axis(vector, first + row // 2, 0)
        parts.append(jnp.take_along_axis(block, place, 1))
    return jnp.concatenate(parts, 0)


def gather_pairs(vector):
    half = vector.shape[0] // 2
    shape = (half, LANES)
    row = lax.broadcasted_iota(jnp.int32, shape, 0)
    odd = lane_bit(shape, 1)
    parts = []
    for block in (vector[:half], vector[half:]):
        block = jnp.take_along_axis(block, lanes(shape) >> 1, 1)
        block = jnp.where(odd, pltpu.roll(block, half - 1, 0), block)
        parts.append(jnp.take_along_axis(block, 2 * row & half - 1, 0))
    return jnp.where(row < half // 2, parts[0], parts[1])


def shifted(vector, down):
    rows = vector.shape[0]
    row = lax.broadcasted_iota(jnp.int32, vector.shape, 0)
    if down:
        return jnp.where(row == 0, 0.0, pltpu.roll(vector, 1, 0))
    return jnp.where(row == rows - 1, 0.0, pltpu.roll(vector, rows - 1, 0))


def to_rows(scratch, native, read, rows, species):
    pairs = rows // 2
    for t in range(species // 2):
        native[t * rows : (t + 1) * rows, :] = read(t).astype(F32)
    for t in range(species // 2):
        for inner in (0, 1):
            tile = native[pl.ds(t * rows + inner, pairs, stride=2), :]
            other = pltpu.roll(tile, LANES // 2, 1)
            scratch[pl.ds(4 * t + inner, pairs, stride=LANES), :] = tile
            scratch[pl.ds(4 * t + 2 + inner, pairs, stride=LANES), :] = other


def halves(a):
    high = a.astype(BF16)
    return high, (a - high.astype(F32)).astype(BF16)


def dot(a, b, dims=((1,), (0,))):
    return lax.dot_general(a, b, (dims, ((), ())), preferred_element_type=F32)


def turn(scratch, out, first, pairs, species):
    unit = (
        lax.broadcasted_iota(jnp.int32, (species, species), 0)
        == lax.broadcasted_iota(jnp.int32, (species, species), 1)
    ).astype(F32).astype(BF16)
    for pair in range(pairs):
        block = scratch[pair * LANES : (pair + 1) * LANES, :species].astype(BF16)
        out[pl.ds(first + pair, species, stride=pairs), :] = dot(unit, block, ((1,), (1,)))


def both(scratch, pair, block):
    odd = lane_bit(block.shape, 1)
    zero = jnp.zeros_like(block)
    scratch[pl.ds(pair * LANES, block.shape[0], stride=2), :] = jnp.where(odd, zero, block)
    scratch[pl.ds(pair * LANES + 1, block.shape[0], stride=2), :] = jnp.where(odd, block, zero)
    return scratch[pair * LANES : (pair + 1) * LANES, :]


def multiply(scratch, pair, earlier, later, exact):
    later = both(scratch, pair, later)
    if exact:
        return dot(earlier.astype(BF16), later.astype(BF16))
    earlier_high, earlier_low = halves(earlier)
    high, low = halves(later)
    return dot(earlier_high, high) + (dot(earlier_low, high) + dot(earlier_high, low))


STEP = 8


def diagonals(load, out, first, scratch, pairs):
    count = LANES // 2
    shape = (pairs, LANES)
    giants = count // STEP

    def slid(tiles, shift, mask):
        here = lane_bit(shape, mask)
        return [jnp.where(here, b, a) for a, b in zip(tiles, tiles[shift:] + tiles[:shift])]

    for small in range(STEP):
        tiles = [load(small + STEP * giant) for giant in range(giants)]
        shift = 1
        while shift < giants:
            tiles = slid(tiles, shift, 2 * STEP * shift)
            shift *= 2
        for giant, tile in enumerate(tiles):
            at = (small + STEP * giant) * pairs
            scratch[at : at + pairs, :] = tile
    for giant in range(giants):
        tiles = []
        for j in range(2 * STEP - 1):
            at = (giant * STEP + j) % count * pairs
            tiles.append(scratch[at : at + pairs, :])
        shift = 1
        while shift < STEP:
            tiles = slid(tiles, shift, 2 * shift)[:-shift]
            shift *= 2
        for j, tile in enumerate(tiles):
            at = first + (giant * STEP + j) * pairs
            turn_by = 2 * STEP * giant
            out[at : at + pairs, :] = pltpu.roll(tile, turn_by, 1) if giant else tile


def whole_tiles(ref, first, pairs):
    return lambda b: ref[first + b * pairs : first + (b + 1) * pairs, :]


def part_tiles(mine, other, pairs):
    first_core = lax.axis_index("gx") & 1 == 0

    def load(b):
        low, at = b < LANES // 4, b % (LANES // 4) * pairs
        own, far = mine[at : at + pairs, :], other[at : at + pairs, :]
        return jnp.where(first_core, own if low else far, far if low else own)

    return load


def mapped(ref, vector, first=0):
    pairs = vector.shape[0]
    turns = [vector] + [pltpu.roll(vector, LANES - 2 * j, 1) for j in range(1, STEP)]
    total = None
    for giant in range(LANES // 2 // STEP):
        terms = []
        for j in range(STEP):
            at = first + (giant * STEP + j) * pairs
            terms.append(ref[at : at + pairs, :] * turns[j])
        while len(terms) > 1:
            terms = [a + b for a, b in zip(terms[::2], terms[1::2])]
        part = pltpu.roll(terms[0], LANES - 2 * STEP * giant, 1) if giant else terms[0]
        total = part if total is None else total + part
    return total


def prep_kernel(reverse, blocks, beside_it, *refs):
    *passed, maps, products, own, native, rows_scratch = refs
    planes, _, rows, width = blocks.shape
    species = LANES // 2
    pairs = rows // 2
    size = species * pairs
    order = list(range(planes))[::-1] if reverse else list(range(planes))
    if passed:
        for p in range(planes):
            passed[0][p] = woven(beside_it[p])
    for plane in order:
        to_rows(rows_scratch, native, reader(blocks, plane, 0), rows, species)
        turn(rows_scratch, maps, plane * size, pairs, species)
    for step, plane in enumerate(order):
        at = pl.ds(plane * size, size)
        if step == 0:
            products[at, :] = -maps[at, :]
            continue
        for pair in range(pairs):
            here = pl.ds(plane * size + pair, species, stride=pairs)
            before = pl.ds(order[step - 1] * size + pair, species, stride=pairs)
            products[here, :] = multiply(
                rows_scratch, pair, products[before, :], -maps[here, :], step == 1
            )
    own[...] = products[pl.ds(order[-1] * size, size), :]


def join_kernel(level, reverse, full, pairs, own, *refs):
    here = (lax.axis_index("gx") >> level) & 1
    core = lax.axis_index("gx") & 1
    species = LANES // 2
    *refs, scratch = refs
    outs = refs[-2:] if full else refs[-1:]
    partner = refs[: len(refs) - len(outs)]
    later_is_own = here == (0 if reverse else 1)
    for pair in range(pairs):
        mine = own[pl.ds(pair, species, stride=pairs), :]
        if len(partner) == 1:
            theirs = partner[0][pl.ds(pair, species, stride=pairs), :]
        else:
            close = partner[0][pl.ds(pair, species // 2, stride=pairs), :]
            far = partner[1][pl.ds(pair, species // 2, stride=pairs), :]
            theirs = jnp.where(
                core == 0, jnp.concatenate([close, far], 0), jnp.concatenate([far, close], 0)
            )
        earlier = jnp.where(later_is_own, theirs, mine)
        later = jnp.where(later_is_own, mine, theirs)
        if full:
            kept = multiply(scratch, pair, earlier, later, False)
            outs[0][pl.ds(pair, species, stride=pairs), :] = kept
            kept = jnp.where(core == 0, kept[: species // 2], kept[species // 2 :])
        else:
            kept = jnp.where(core == 0, earlier[: species // 2], earlier[species // 2 :])
            kept = multiply(scratch, pair, kept, later, False)
        outs[-1][pl.ds(pair, species // 2, stride=pairs), :] = kept


def base_kernel(start, source, diag, upper, side, maps, products, partner, *outs):
    rhs, base, step_maps, entry_maps, near_map, scratch = outs
    planes, pairs = start.shape[:2]
    size = pairs * LANES // 2
    vectors = [spread(start[p]) for p in range(planes)]
    for p in range(planes):
        own = apply([(reader(diag, p, 0), spread(woven(source[p])))])
        terms = [
            (reader(side, 2, p, 0), shifted(vectors[p], True)),
            (reader(side, 3, p, 0), shifted(vectors[p], False)),
        ]
        if p + 1 < planes:
            terms.append((reader(upper, p, 0), vectors[p + 1]))
        around = apply(terms)
        rhs[p] = gather_pairs(own)
        base[p] = gather_pairs(own - around)
    for p in range(planes):
        if p:
            diagonals(whole_tiles(maps, p * size, pairs), step_maps, p * size, scratch.at[0], pairs)
        diagonals(whole_tiles(products, p * size, pairs), entry_maps, p * size, scratch.at[1], pairs)
    diagonals(whole_tiles(partner, 0, pairs), near_map, 0, scratch.at[2], pairs)


def far_kernel(pairs, mine, other, out, scratch):
    diagonals(part_tiles(mine, other, pairs), out, 0, scratch, pairs)


def outgoing(offset, partners, here, slots):
    vectors = [offset]
    for level, ref in enumerate(partners):
        passed = mapped(ref, vectors[-1])
        vectors.append(jnp.where((here >> level) & 1 == 0, passed, vectors[-1]))
    place = lax.axis_index("gx")
    for target in range(slots.shape[0]):
        apart = place ^ target
        value = vectors[0]
        for level in range(1, len(vectors)):
            value = jnp.where(apart >= 1 << level, vectors[level], value)
        slots[target] = value


def incoming(got, partners, here, reverse):
    count = got.shape[0]
    entering = None
    for level in range(len(partners) + 1)[::-1]:
        total = None
        for source in range(count):
            place = count - 1 - source if reverse else source
            term = jnp.where((place >> level) == (here >> level) - 1, got[source], 0.0)
            total = term if total is None else total + term
        if entering is not None:
            total = total + mapped(partners[level], entering)
        before = jnp.zeros_like(total) if entering is None else entering
        entering = jnp.where((here >> level) & 1 == 1, total, before)
    return entering


def beside(axis, paired, other):
    place, count = lax.axis_index(axis), lax.axis_size(axis)
    odd = place & 1 == 1
    low = jnp.where(odd, paired, other)
    high = jnp.where(odd, other, paired)
    return jnp.where(place == 0, 0.0, low), jnp.where(place == count - 1, 0.0, high)


def forward_offset_kernel(base, other, paired, ahead, side, upper, step_maps, *rest):
    *partners, drive, offsets, slots = rest
    planes, pairs = base.shape[:2]
    size = pairs * LANES // 2
    here = lax.axis_index("gx")
    last = here == lax.axis_size("gx") - 1
    previous = None
    for p in range(planes):
        low, high = beside("gy", paired[p], other[p])
        terms = [(reader(side, 0, p, 0), spread(low)), (reader(side, 1, p, 0), spread(high))]
        if p + 1 == planes:
            beyond = jnp.where(last, 0.0, ahead[0])
            terms.append((reader(upper, p, 0), spread(beyond)))
        fresh = base[p] - gather_pairs(apply(terms))
        drive[p] = fresh
        if previous is not None:
            fresh = fresh - mapped(step_maps, previous, p * size)
        offsets[p] = fresh
        previous = fresh
    outgoing(previous, partners, here, slots)


def forward_kernel(got, drive, offsets, rhs, entry_maps, *rest):
    *partners, out, copy, base = rest
    planes = drive.shape[0]
    size = drive.shape[1] * LANES // 2
    entering = incoming(got, partners, lax.axis_index("gx"), False)
    for p in range(planes):
        value = offsets[p] + mapped(entry_maps, entering, p * size)
        base[p] = rhs[p] - (drive[p] - value)
        out[p] = unwoven(value)
        copy[p] = value


def side_kernel(levels, base, vectors, side, maps, products, partner, *rest):
    parts = rest[: 2 * (levels - 2)]
    out, step_maps, entry_maps, near, *far, scratch = rest[2 * (levels - 2) :]
    planes, pairs = base.shape[:2]
    size = pairs * LANES // 2
    for p in range(planes):
        vector = spread(vectors[p])
        around = apply(
            [
                (reader(side, 2, p, 0), shifted(vector, True)),
                (reader(side, 3, p, 0), shifted(vector, False)),
            ]
        )
        out[p] = base[p] - gather_pairs(around)
        if p + 1 < planes:
            diagonals(whole_tiles(maps, p * size, pairs), step_maps, p * size, scratch.at[0], pairs)
        diagonals(whole_tiles(products, p * size, pairs), entry_maps, p * size, scratch.at[1], pairs)
    diagonals(whole_tiles(partner, 0, pairs), near, 0, scratch.at[2], pairs)
    for level, ref in enumerate(far):
        diagonals(part_tiles(*parts[2 * level : 2 * level + 2], pairs), ref, 0, scratch.at[3], pairs)


def backward_offset_kernel(base, other, paired, side, step_maps, *rest):
    *partners, offsets, slots = rest
    planes = base.shape[0]
    size = base.shape[1] * LANES // 2
    here = lax.axis_size("gx") - 1 - lax.axis_index("gx")
    previous = None
    for p in range(planes)[::-1]:
        low, high = beside("gy", paired[p], other[p])
        around = apply([(reader(side, 0, p, 0), spread(low)), (reader(side, 1, p, 0), spread(high))])
        fresh = base[p] - gather_pairs(around)
        if previous is not None:
            fresh = fresh - mapped(step_maps, previous, p * size)
        offsets[p] = fresh
        previous = fresh
    outgoing(previous, partners, here, slots)


def backward_kernel(got, offsets, entry_maps, *rest):
    *partners, out = rest
    size = offsets.shape[1] * LANES // 2
    here = lax.axis_size("gx") - 1 - lax.axis_index("gx")
    entering = incoming(got, partners, here, True)
    for p in range(offsets.shape[0]):
        out[p] = unwoven(offsets[p] + mapped(entry_maps, entering, p * size))


def call(kernel, operands, outs, scratch, micros):
    arrays = [o[0] if isinstance(o, tuple) else o for o in operands]
    held = [i for i, o in enumerate(operands) if isinstance(o, tuple)]
    outs = [jax.ShapeDtypeStruct(shape, F32) for shape in outs]
    moved = sum(a.size * a.dtype.itemsize for a in arrays)
    return pl.pallas_call(
        kernel,
        out_shape=outs,
        in_specs=[
            pl.BlockSpec(memory_space=pl.ANY if i in held else pltpu.VMEM) for i in range(len(arrays))
        ],
        out_specs=[pl.BlockSpec(memory_space=pltpu.VMEM) for _ in outs],
        scratch_shapes=[pltpu.VMEM(shape, F32) for shape in scratch],
        compiler_params=pltpu.CompilerParams(vmem_limit_bytes=12 << 20),
        cost_estimate=pl.CostEstimate(
            flops=int(micros * 1.15e9), bytes_accessed=moved, transcendentals=0
        ),
    )(*arrays)


def swaps(block):
    count, rows = lax.axis_size("gx"), lax.axis_size("gy")
    route = []
    for place in range(count):
        for row in range(rows):
            target = row + 1 if row & 1 else row - 1
            to = place * rows + target if 0 <= target < rows else (place ^ 1) * rows + row
            route.append((place * rows + row, to))
    return crossed(block, "gy", 1), lax.ppermute(block, ("gx", "gy"), route)


def crossed(block, axis, distance):
    return lax.ppermute(block, axis, [(i, i ^ distance) for i in range(lax.axis_size(axis))])


def exchange(slots, axis):
    return lax.all_to_all(slots, axis, 0, 0)


def local(start, source, diag_inverse, x_lower, x_upper, side_blocks):
    planes, _, depth, width = x_lower.shape
    species = start.shape[2] // depth
    pairs = depth // 2
    count = lax.axis_size("gx")
    levels = count.bit_length() - 1
    size = species * pairs
    one = (pairs, LANES)
    vec = (planes,) + one
    maps = (planes * size, LANES)
    whole, half = (size, LANES), (size // 2, LANES)
    slots = (count,) + one
    start = start.reshape(vec)
    source = source.reshape(vec)

    def prepare(reverse, blocks, other):
        *passed, maps_of, products, own = call(
            functools.partial(prep_kernel, reverse),
            [blocks, (other, None) if reverse else other],
            ([] if reverse else [vec]) + [maps, maps, whole],
            [(depth * species // 2, LANES), (depth * species, LANES)],
            1.0,
        )
        partners, kept = [], None
        for level in range(levels - 1):
            if level == 0:
                got = [crossed(own, "gx", 1)]
            else:
                mine = crossed(kept, "gx", 1 << level)
                got = [mine, crossed(mine, "gx", 1)]
            partners += got
            if level + 2 < levels:
                full = level + 3 < levels
                outs = call(
                    functools.partial(join_kernel, level, reverse, full, pairs),
                    [own] + got,
                    [whole, half] if full else [half],
                    [(depth * species, LANES)],
                    0.4,
                )
                own, kept = outs[0], outs[-1]
        return [maps_of, products, *partners], passed

    lower, (start,) = prepare(False, x_lower, start)
    upper, _ = prepare(True, x_upper, lower[1])
    paired, other = swaps(start)
    ahead = lax.ppermute(start[:1], "gx", [(i, (i - 1) % count) for i in range(count)])

    rhs, base, step_maps, entry_maps, near = call(
        base_kernel,
        [start, source, diag_inverse, x_upper, side_blocks] + lower[:3],
        [vec, vec, maps, maps, whole],
        [(3,) + whole],
        5.0,
    )
    partners = [near]
    for level in range(levels - 2):
        partners += call(
            functools.partial(far_kernel, pairs),
            lower[3 + 2 * level : 5 + 2 * level],
            [whole],
            [whole],
            0.3,
        )
    drive, offsets, sent = call(
        forward_offset_kernel,
        [base, other, paired, ahead, side_blocks, x_upper, step_maps] + partners,
        [vec, vec, slots],
        [],
        1.5,
    )
    forward, copy, base = call(
        forward_kernel,
        [exchange(sent, "gx"), drive, offsets, rhs, entry_maps] + partners,
        [vec, vec, vec],
        [],
        1.0,
    )
    paired, other = swaps(copy)
    base, step_maps, entry_maps, *partners = call(
        functools.partial(side_kernel, levels),
        [base, copy, side_blocks] + upper,
        [vec, maps, maps, whole] + [whole] * (levels - 2),
        [(4,) + whole],
        0.7,
    )
    offsets, sent = call(
        backward_offset_kernel,
        [base, other, paired, side_blocks, step_maps] + partners,
        [vec, slots],
        [],
        1.5,
    )
    (result,) = call(
        backward_kernel, [exchange(sent, "gx"), offsets, entry_maps] + partners, [vec], [], 1.0
    )
    shape = (planes, 1, depth * species)
    return forward.reshape(shape), result.reshape(shape)


def solution(mesh):
    return jax.shard_map(
        local,
        mesh=mesh,
        in_specs=(
            P("gx", "gy", None),
            P("gx", "gy", None),
            P("gx", "gy", None, None),
            P("gx", "gy", None, None),
            P("gx", "gy", None, None),
            P(None, "gx", "gy", None, None),
        ),
        out_specs=(P("gx", "gy", None), P("gx", "gy", None)),
        check_vma=False,
    )
```

```python
import functools

import jax
import jax.numpy as jnp
from jax import lax
from jax.experimental import pallas as pl
from jax.experimental.pallas import tpu as pltpu
from jax.sharding import PartitionSpec as P

LANES = 128
F32 = jnp.float32
BF16 = jnp.bfloat16


def lane_bit(shape, shift):
    return (lax.broadcasted_iota(jnp.int32, shape, len(shape) - 1) & shift) != 0


def segment_sums(leaf, tiles, rows):
    shape = (rows, LANES)

    def node(base, stride, shift):
        if stride == tiles:
            return leaf(base)
        low = node(base, stride * 2, shift * 2)
        high = node(base + stride, stride * 2, shift * 2)
        low = low + pltpu.roll(low, LANES - shift, 1)
        high = high + pltpu.roll(high, shift, 1)
        return jnp.where(lane_bit(shape, shift), high, low)

    part = node(0, 1, 2)
    odd = lane_bit(shape, 1)
    part = part + jnp.where(odd, pltpu.roll(part, 1, 1), pltpu.roll(part, LANES - 1, 1))
    upper = lane_bit(shape, LANES // 2)
    return jnp.where(upper == odd, part, pltpu.roll(part, LANES // 2, 1))


def apply(terms):
    rows = terms[0][1].shape[0]
    tiles = LANES // 4

    def leaf(t):
        return sum(read(t).astype(F32) * vector for read, vector in terms)

    return segment_sums(leaf, tiles, rows)


def reader(ref, *index):
    return lambda t: ref[(*index, slice(None), slice(t * LANES, (t + 1) * LANES))]


def lanes(shape):
    return lax.broadcasted_iota(jnp.int32, shape, 1)


def woven(raw):
    lane = lanes(raw.shape)
    return jnp.take_along_axis(raw, (lane >> 1) + (lane & 1) * (LANES // 2), 1)


def unwoven(vector):
    lane = lanes(vector.shape)
    return jnp.take_along_axis(vector, (lane & LANES // 2 - 1) * 2 + lane // (LANES // 2), 1)


def spread(vector):
    half = vector.shape[0]
    row = lax.broadcasted_iota(jnp.int32, vector.shape, 0)
    place = (lanes(vector.shape) & LANES // 2 - 1) * 2 + (row & 1)
    parts = []
    for first in (0, half // 2):
        block = jnp.take_along_axis(vector, first + row // 2, 0)
        parts.append(jnp.take_along_axis(block, place, 1))
    return jnp.concatenate(parts, 0)


def spread_raw(raw):
    half = raw.shape[0]
    row = lax.broadcasted_iota(jnp.int32, raw.shape, 0)
    same = (row & 1 == 1) == lane_bit(raw.shape, LANES // 2)
    parts = []
    for first in (0, half // 2):
        block = jnp.take_along_axis(raw, first + row // 2, 0)
        parts.append(jnp.where(same, block, pltpu.roll(block, LANES // 2, 1)))
    return jnp.concatenate(parts, 0)


def gather_pairs(vector):
    half = vector.shape[0] // 2
    shape = (half, LANES)
    row = lax.broadcasted_iota(jnp.int32, shape, 0)
    odd = lane_bit(shape, 1)
    parts = []
    for block in (vector[:half], vector[half:]):
        block = jnp.take_along_axis(block, lanes(shape) >> 1, 1)
        block = jnp.where(odd, pltpu.roll(block, half - 1, 0), block)
        parts.append(jnp.take_along_axis(block, 2 * row & half - 1, 0))
    return jnp.where(row < half // 2, parts[0], parts[1])


def shifted(vector, down):
    rows = vector.shape[0]
    row = lax.broadcasted_iota(jnp.int32, vector.shape, 0)
    if down:
        return jnp.where(row == 0, 0.0, pltpu.roll(vector, 1, 0))
    return jnp.where(row == rows - 1, 0.0, pltpu.roll(vector, rows - 1, 0))


def to_rows(scratch, native, read, rows, species):
    pairs = rows // 2
    for t in range(species // 2):
        native[t * rows : (t + 1) * rows, :] = read(t).astype(F32)
    for t in range(species // 2):
        for inner in (0, 1):
            tile = native[pl.ds(t * rows + inner, pairs, stride=2), :]
            other = pltpu.roll(tile, LANES // 2, 1)
            scratch[pl.ds(4 * t + inner, pairs, stride=LANES), :] = tile
            scratch[pl.ds(4 * t + 2 + inner, pairs, stride=LANES), :] = other


def halves(a):
    high = a.astype(BF16)
    return high, (a - high.astype(F32)).astype(BF16)


def dot(a, b, dims=((1,), (0,))):
    return lax.dot_general(a, b, (dims, ((), ())), preferred_element_type=F32)


def turn(scratch, out, first, pairs, species):
    unit = (
        lax.broadcasted_iota(jnp.int32, (species, species), 0)
        == lax.broadcasted_iota(jnp.int32, (species, species), 1)
    ).astype(F32).astype(BF16)
    for pair in range(pairs):
        block = scratch[pair * LANES : (pair + 1) * LANES, :species].astype(BF16)
        out[pl.ds(first + pair, species, stride=pairs), :] = dot(unit, block, ((1,), (1,)))


def both(scratch, pair, block):
    odd = lane_bit(block.shape, 1)
    zero = jnp.zeros_like(block)
    scratch[pl.ds(pair * LANES, block.shape[0], stride=2), :] = jnp.where(odd, zero, block)
    scratch[pl.ds(pair * LANES + 1, block.shape[0], stride=2), :] = jnp.where(odd, block, zero)
    return scratch[pair * LANES : (pair + 1) * LANES, :]


def multiply(scratch, pair, earlier, later, exact):
    later = both(scratch, pair, later)
    if exact:
        return dot(earlier.astype(BF16), later.astype(BF16))
    earlier_high, earlier_low = halves(earlier)
    high, low = halves(later)
    return dot(earlier_high, high) + (dot(earlier_low, high) + dot(earlier_high, low))


STEP = 8


def diagonals(load, out, first, scratch, pairs):
    count = LANES // 2
    shape = (pairs, LANES)
    giants = count // STEP

    def slid(tiles, shift, mask):
        here = lane_bit(shape, mask)
        return [jnp.where(here, b, a) for a, b in zip(tiles, tiles[shift:] + tiles[:shift])]

    for small in range(STEP):
        tiles = [load(small + STEP * giant) for giant in range(giants)]
        shift = 1
        while shift < giants:
            tiles = slid(tiles, shift, 2 * STEP * shift)
            shift *= 2
        for giant, tile in enumerate(tiles):
            at = (small + STEP * giant) * pairs
            scratch[at : at + pairs, :] = tile
    for giant in range(giants):
        tiles = []
        for j in range(2 * STEP - 1):
            at = (giant * STEP + j) % count * pairs
            tiles.append(scratch[at : at + pairs, :])
        shift = 1
        while shift < STEP:
            tiles = slid(tiles, shift, 2 * shift)[:-shift]
            shift *= 2
        for j, tile in enumerate(tiles):
            at = first + (giant * STEP + j) * pairs
            turn_by = 2 * STEP * giant
            out[at : at + pairs, :] = pltpu.roll(tile, turn_by, 1) if giant else tile


def whole_tiles(ref, first, pairs):
    return lambda b: ref[first + b * pairs : first + (b + 1) * pairs, :]


def part_tiles(mine, other, pairs):
    first_core = lax.axis_index("gx") & 1 == 0

    def load(b):
        low, at = b < LANES // 4, b % (LANES // 4) * pairs
        own, far = mine[at : at + pairs, :], other[at : at + pairs, :]
        return jnp.where(first_core, own if low else far, far if low else own)

    return load


def mapped(ref, vector, first=0):
    pairs = vector.shape[0]
    turns = [vector] + [pltpu.roll(vector, LANES - 2 * j, 1) for j in range(1, STEP)]
    total = None
    for giant in range(LANES // 2 // STEP):
        terms = []
        for j in range(STEP):
            at = first + (giant * STEP + j) * pairs
            terms.append(ref[at : at + pairs, :] * turns[j])
        while len(terms) > 1:
            terms = [a + b for a, b in zip(terms[::2], terms[1::2])]
        part = pltpu.roll(terms[0], LANES - 2 * STEP * giant, 1) if giant else terms[0]
        total = part if total is None else total + part
    return total


def prep_kernel(reverse, blocks, *refs):
    if reverse:
        start, _, passed, *refs = refs
        for p in range(start.shape[0]):
            passed[p] = woven(start[p])
    steps, products, own, maps, native, rows_scratch = refs
    planes, _, rows, width = blocks.shape
    species = LANES // 2
    pairs = rows // 2
    size = species * pairs
    order = list(range(planes))[::-1] if reverse else list(range(planes))
    for step, plane in enumerate(order):
        at = pl.ds(plane * size, size)
        to_rows(rows_scratch, native, reader(blocks, plane, 0), rows, species)
        turn(rows_scratch, maps, 0, pairs, species)
        if step == 0:
            products[at, :] = -maps[...]
            continue
        steps[pl.ds((step - 1) * size, size), :] = maps[...]
        for pair in range(pairs):
            here = pl.ds(plane * size + pair, species, stride=pairs)
            before = pl.ds(order[step - 1] * size + pair, species, stride=pairs)
            later = -maps[pl.ds(pair, species, stride=pairs), :]
            products[here, :] = multiply(rows_scratch, pair, products[before, :], later, step == 1)
    own[...] = products[pl.ds(order[-1] * size, size), :]


def join_kernel(level, reverse, full, pairs, own, *refs):
    here = (lax.axis_index("gx") >> level) & 1
    core = lax.axis_index("gx") & 1
    species = LANES // 2
    *refs, scratch = refs
    outs = refs[-2:] if full else refs[-1:]
    partner = refs[: len(refs) - len(outs)]
    later_is_own = here == (0 if reverse else 1)
    for pair in range(pairs):
        mine = own[pl.ds(pair, species, stride=pairs), :]
        if len(partner) == 1:
            theirs = partner[0][pl.ds(pair, species, stride=pairs), :]
        else:
            close = partner[0][pl.ds(pair, species // 2, stride=pairs), :]
            far = partner[1][pl.ds(pair, species // 2, stride=pairs), :]
            theirs = jnp.where(
                core == 0, jnp.concatenate([close, far], 0), jnp.concatenate([far, close], 0)
            )
        earlier = jnp.where(later_is_own, theirs, mine)
        later = jnp.where(later_is_own, mine, theirs)
        if full:
            kept = multiply(scratch, pair, earlier, later, False)
            outs[0][pl.ds(pair, species, stride=pairs), :] = kept
            kept = jnp.where(core == 0, kept[: species // 2], kept[species // 2 :])
        else:
            kept = jnp.where(core == 0, earlier[: species // 2], earlier[species // 2 :])
            kept = multiply(scratch, pair, kept, later, False)
        outs[-1][pl.ds(pair, species // 2, stride=pairs), :] = kept


def base_kernel(start, source, diag, upper, side, rhs, base):
    planes = start.shape[0]
    vectors = [spread(start[p]) for p in range(planes)]
    for p in range(planes):
        own = apply([(reader(diag, p, 0), spread_raw(source[p]))])
        terms = [
            (reader(side, 2, p, 0), shifted(vectors[p], True)),
            (reader(side, 3, p, 0), shifted(vectors[p], False)),
        ]
        if p + 1 < planes:
            terms.append((reader(upper, p, 0), vectors[p + 1]))
        around = apply(terms)
        rhs[p] = gather_pairs(own)
        base[p] = gather_pairs(own - around)


def convert(pairs, sources, outs, scratch):
    size = pairs * LANES // 2
    for source, out in zip(sources, outs):
        for first in range(0, source.shape[0], size):
            diagonals(whole_tiles(source, first, pairs), out, first, scratch, pairs)


def near_kernel(pairs, *refs):
    *refs, scratch = refs
    convert(pairs, refs[: len(refs) // 2], refs[len(refs) // 2 :], scratch)


def far_kernel(pairs, mine, other, out, scratch):
    diagonals(part_tiles(mine, other, pairs), out, 0, scratch, pairs)


def outgoing(offset, partners, here, slots):
    vectors = [offset]
    for level, ref in enumerate(partners):
        passed = mapped(ref, vectors[-1])
        vectors.append(jnp.where((here >> level) & 1 == 0, passed, vectors[-1]))
    place = lax.axis_index("gx")
    for target in range(slots.shape[0]):
        apart = place ^ target
        value = vectors[0]
        for level in range(1, len(vectors)):
            value = jnp.where(apart >= 1 << level, vectors[level], value)
        slots[target] = value


def incoming(got, partners, here, reverse):
    count = got.shape[0]
    entering = None
    for level in range(len(partners) + 1)[::-1]:
        total = None
        for source in range(count):
            place = count - 1 - source if reverse else source
            term = jnp.where((place >> level) == (here >> level) - 1, got[source], 0.0)
            total = term if total is None else total + term
        if entering is not None:
            total = total + mapped(partners[level], entering)
        before = jnp.zeros_like(total) if entering is None else entering
        entering = jnp.where((here >> level) & 1 == 1, total, before)
    return entering


def beside(axis, paired, other):
    place, count = lax.axis_index(axis), lax.axis_size(axis)
    odd = place & 1 == 1
    low = jnp.where(odd, paired, other)
    high = jnp.where(odd, other, paired)
    return jnp.where(place == 0, 0.0, low), jnp.where(place == count - 1, 0.0, high)


def forward_offset_kernel(base, paired, other, ahead, side, upper, step_maps, *rest):
    *partners, drive, offsets, slots = rest
    planes, pairs = base.shape[:2]
    size = pairs * LANES // 2
    here = lax.axis_index("gx")
    last = here == lax.axis_size("gx") - 1
    previous = None
    for p in range(planes):
        low, high = beside("gy", paired[p], other[p])
        terms = [(reader(side, 0, p, 0), spread(low)), (reader(side, 1, p, 0), spread(high))]
        if p + 1 == planes:
            beyond = jnp.where(last, 0.0, ahead[0])
            terms.append((reader(upper, p, 0), spread(beyond)))
        fresh = base[p] - gather_pairs(apply(terms))
        drive[p] = fresh
        if previous is not None:
            fresh = fresh - mapped(step_maps, previous, (p - 1) * size)
        offsets[p] = fresh
        previous = fresh
    outgoing(previous, partners, here, slots)


def forward_kernel(got, drive, offsets, rhs, entry_maps, *rest):
    *partners, out, copy, base = rest
    planes = drive.shape[0]
    size = drive.shape[1] * LANES // 2
    entering = incoming(got, partners, lax.axis_index("gx"), False)
    for p in range(planes):
        value = offsets[p] + mapped(entry_maps, entering, p * size)
        base[p] = rhs[p] - (drive[p] - value)
        out[p] = unwoven(value)
        copy[p] = value


def side_kernel(levels, base, vectors, side, steps, products, partner, *rest):
    parts = rest[: 2 * (levels - 2)]
    out, step_maps, entry_maps, near, *far, scratch = rest[2 * (levels - 2) :]
    planes, pairs = base.shape[:2]
    for p in range(planes):
        vector = spread(vectors[p])
        around = apply(
            [
                (reader(side, 2, p, 0), shifted(vector, True)),
                (reader(side, 3, p, 0), shifted(vector, False)),
            ]
        )
        out[p] = base[p] - gather_pairs(around)
    convert(pairs, (steps, products, partner), (step_maps, entry_maps, near), scratch.at[0])
    for level, ref in enumerate(far):
        diagonals(part_tiles(*parts[2 * level : 2 * level + 2], pairs), ref, 0, scratch.at[1], pairs)


def backward_offset_kernel(base, paired, other, side, step_maps, *rest):
    *partners, offsets, slots = rest
    planes = base.shape[0]
    size = base.shape[1] * LANES // 2
    here = lax.axis_size("gx") - 1 - lax.axis_index("gx")
    previous = None
    for p in range(planes)[::-1]:
        low, high = beside("gy", paired[p], other[p])
        around = apply([(reader(side, 0, p, 0), spread(low)), (reader(side, 1, p, 0), spread(high))])
        fresh = base[p] - gather_pairs(around)
        if previous is not None:
            fresh = fresh - mapped(step_maps, previous, (planes - 2 - p) * size)
        offsets[p] = fresh
        previous = fresh
    outgoing(previous, partners, here, slots)


def backward_kernel(got, offsets, entry_maps, *rest):
    *partners, out = rest
    size = offsets.shape[1] * LANES // 2
    here = lax.axis_size("gx") - 1 - lax.axis_index("gx")
    entering = incoming(got, partners, here, True)
    for p in range(offsets.shape[0]):
        out[p] = unwoven(offsets[p] + mapped(entry_maps, entering, p * size))


def call(kernel, operands, outs, scratch, micros):
    arrays = [o[0] if isinstance(o, tuple) else o for o in operands]
    held = [i for i, o in enumerate(operands) if isinstance(o, tuple)]
    outs = [jax.ShapeDtypeStruct(shape, F32) for shape in outs]
    moved = sum(a.size * a.dtype.itemsize for a in arrays)
    return pl.pallas_call(
        kernel,
        out_shape=outs,
        in_specs=[
            pl.BlockSpec(memory_space=pl.ANY if i in held else pltpu.VMEM) for i in range(len(arrays))
        ],
        out_specs=[pl.BlockSpec(memory_space=pltpu.VMEM) for _ in outs],
        scratch_shapes=[pltpu.VMEM(shape, F32) for shape in scratch],
        compiler_params=pltpu.CompilerParams(vmem_limit_bytes=12 << 20),
        cost_estimate=pl.CostEstimate(
            flops=int(micros * 1.15e9), bytes_accessed=moved, transcendentals=0
        ),
    )(*arrays)


def swaps(block):
    count, rows = lax.axis_size("gx"), lax.axis_size("gy")
    route = []
    for place in range(count):
        for row in range(rows):
            target = row + 1 if row & 1 else row - 1
            to = place * rows + target if 0 <= target < rows else (place ^ 1) * rows + row
            route.append((place * rows + row, to))
    return crossed(block, "gy", 1), lax.ppermute(block, ("gx", "gy"), route)


def crossed(block, axis, distance):
    return lax.ppermute(block, axis, [(i, i ^ distance) for i in range(lax.axis_size(axis))])


def exchange(slots, axis):
    return lax.all_to_all(slots, axis, 0, 0)


def local(start, source, diag_inverse, x_lower, x_upper, side_blocks):
    planes, _, depth, width = x_lower.shape
    species = start.shape[2] // depth
    pairs = depth // 2
    count = lax.axis_size("gx")
    levels = count.bit_length() - 1
    size = species * pairs
    one = (pairs, LANES)
    vec = (planes,) + one
    maps, steps = (planes * size, LANES), ((planes - 1) * size, LANES)
    whole, half = (size, LANES), (size // 2, LANES)
    slots = (count,) + one
    start = start.reshape(vec)
    source = source.reshape(vec)

    def prepare(reverse, blocks, after=None):
        *passed, step_maps, products, own = call(
            functools.partial(prep_kernel, reverse),
            [blocks] + ([start, (after, None)] if reverse else []),
            ([vec] if reverse else []) + [steps, maps, whole],
            [whole, (depth * species // 2, LANES), (depth * species, LANES)],
            1.0,
        )
        partners, kept = [], None
        for level in range(levels - 1):
            if level == 0:
                got = [crossed(own, "gx", 1)]
            else:
                mine = crossed(kept, "gx", 1 << level)
                got = [mine, crossed(mine, "gx", 1)]
            partners += got
            if level + 2 < levels:
                full = level + 3 < levels
                outs = call(
                    functools.partial(join_kernel, level, reverse, full, pairs),
                    [own] + got,
                    [whole, half] if full else [half],
                    [(depth * species, LANES)],
                    0.4,
                )
                own, kept = outs[0], outs[-1]
        return [step_maps, products, *partners], passed

    lower, _ = prepare(False, x_lower)
    upper, (start,) = prepare(True, x_upper, lower[1])
    paired, other = swaps(start)
    ahead = lax.ppermute(start[:1], "gx", [(i, (i - 1) % count) for i in range(count)])

    rhs, base = call(
        base_kernel, [start, source, diag_inverse, x_upper, side_blocks], [vec, vec], [], 5.0
    )
    step_maps, entry_maps, near = call(
        functools.partial(near_kernel, pairs), lower[:3], [steps, maps, whole], [whole], 0.5
    )
    partners = [near]
    for level in range(levels - 2):
        partners += call(
            functools.partial(far_kernel, pairs),
            lower[3 + 2 * level : 5 + 2 * level],
            [whole],
            [whole],
            0.3,
        )
    drive, offsets, sent = call(
        forward_offset_kernel,
        [base, paired, other, ahead, side_blocks, x_upper, step_maps] + partners,
        [vec, vec, slots],
        [],
        1.5,
    )
    forward, copy, base = call(
        forward_kernel,
        [exchange(sent, "gx"), drive, offsets, rhs, entry_maps] + partners,
        [vec, vec, vec],
        [],
        1.0,
    )
    paired, other = swaps(copy)
    base, step_maps, entry_maps, *partners = call(
        functools.partial(side_kernel, levels),
        [base, copy, side_blocks] + upper,
        [vec, steps, maps, whole] + [whole] * (levels - 2),
        [(2,) + whole],
        0.7,
    )
    offsets, sent = call(
        backward_offset_kernel,
        [base, paired, other, side_blocks, step_maps] + partners,
        [vec, slots],
        [],
        1.5,
    )
    (result,) = call(
        backward_kernel, [exchange(sent, "gx"), offsets, entry_maps] + partners, [vec], [], 1.0
    )
    shape = (planes, 1, depth * species)
    return forward.reshape(shape), result.reshape(shape)


def solution(mesh):
    return jax.shard_map(
        local,
        mesh=mesh,
        in_specs=(
            P("gx", "gy", None),
            P("gx", "gy", None),
            P("gx", "gy", None, None),
            P("gx", "gy", None, None),
            P("gx", "gy", None, None),
            P(None, "gx", "gy", None, None),
        ),
        out_specs=(P("gx", "gy", None), P("gx", "gy", None)),
        check_vma=False,
    )
```

```python
import functools

import jax
import jax.numpy as jnp
from jax import lax
from jax.experimental import pallas as pl
from jax.experimental.pallas import tpu as pltpu
from jax.sharding import PartitionSpec as P

LANES = 128
F32 = jnp.float32
BF16 = jnp.bfloat16


def lane_bit(shape, shift):
    return (lax.broadcasted_iota(jnp.int32, shape, len(shape) - 1) & shift) != 0


def segment_sums(leaf, tiles, rows):
    shape = (rows, LANES)

    def node(base, stride, shift):
        if stride == tiles:
            return leaf(base)
        low = node(base, stride * 2, shift * 2)
        high = node(base + stride, stride * 2, shift * 2)
        low = low + pltpu.roll(low, LANES - shift, 1)
        high = high + pltpu.roll(high, shift, 1)
        return jnp.where(lane_bit(shape, shift), high, low)

    part = node(0, 1, 2)
    odd = lane_bit(shape, 1)
    part = part + jnp.where(odd, pltpu.roll(part, 1, 1), pltpu.roll(part, LANES - 1, 1))
    upper = lane_bit(shape, LANES // 2)
    return jnp.where(upper == odd, part, pltpu.roll(part, LANES // 2, 1))


def apply(terms):
    rows = terms[0][1].shape[0]
    tiles = LANES // 4

    def leaf(t):
        return sum(read(t).astype(F32) * vector for read, vector in terms)

    return segment_sums(leaf, tiles, rows)


def reader(ref, *index):
    return lambda t: ref[(*index, slice(None), slice(t * LANES, (t + 1) * LANES))]


def lanes(shape):
    return lax.broadcasted_iota(jnp.int32, shape, 1)


def woven(raw):
    lane = lanes(raw.shape)
    return jnp.take_along_axis(raw, (lane >> 1) + (lane & 1) * (LANES // 2), 1)


def unwoven(vector):
    lane = lanes(vector.shape)
    return jnp.take_along_axis(vector, (lane & LANES // 2 - 1) * 2 + lane // (LANES // 2), 1)


def spread(vector):
    half = vector.shape[0]
    row = lax.broadcasted_iota(jnp.int32, vector.shape, 0)
    place = (lanes(vector.shape) & LANES // 2 - 1) * 2 + (row & 1)
    parts = []
    for first in (0, half // 2):
        block = jnp.take_along_axis(vector, first + row // 2, 0)
        parts.append(jnp.take_along_axis(block, place, 1))
    return jnp.concatenate(parts, 0)


def spread_raw(raw):
    half = raw.shape[0]
    row = lax.broadcasted_iota(jnp.int32, raw.shape, 0)
    same = (row & 1 == 1) == lane_bit(raw.shape, LANES // 2)
    parts = []
    for first in (0, half // 2):
        block = jnp.take_along_axis(raw, first + row // 2, 0)
        parts.append(jnp.where(same, block, pltpu.roll(block, LANES // 2, 1)))
    return jnp.concatenate(parts, 0)


def gather_pairs(vector):
    half = vector.shape[0] // 2
    shape = (half, LANES)
    row = lax.broadcasted_iota(jnp.int32, shape, 0)
    odd = lane_bit(shape, 1)
    parts = []
    for block in (vector[:half], vector[half:]):
        block = jnp.take_along_axis(block, lanes(shape) >> 1, 1)
        block = jnp.where(odd, pltpu.roll(block, half - 1, 0), block)
        parts.append(jnp.take_along_axis(block, 2 * row & half - 1, 0))
    return jnp.where(row < half // 2, parts[0], parts[1])


def shifted(vector, down):
    rows = vector.shape[0]
    row = lax.broadcasted_iota(jnp.int32, vector.shape, 0)
    if down:
        return jnp.where(row == 0, 0.0, pltpu.roll(vector, 1, 0))
    return jnp.where(row == rows - 1, 0.0, pltpu.roll(vector, rows - 1, 0))


def to_rows(scratch, native, read, rows, species):
    pairs = rows // 2
    for t in range(species // 2):
        native[t * rows : (t + 1) * rows, :] = read(t).astype(F32)
    for t in range(species // 2):
        for inner in (0, 1):
            tile = native[pl.ds(t * rows + inner, pairs, stride=2), :]
            other = pltpu.roll(tile, LANES // 2, 1)
            scratch[pl.ds(4 * t + inner, pairs, stride=LANES), :] = tile
            scratch[pl.ds(4 * t + 2 + inner, pairs, stride=LANES), :] = other


def halves(a):
    high = a.astype(BF16)
    return high, (a - high.astype(F32)).astype(BF16)


def dot(a, b, dims=((1,), (0,))):
    return lax.dot_general(a, b, (dims, ((), ())), preferred_element_type=F32)


def turn(scratch, out, first, pairs, species):
    unit = (
        lax.broadcasted_iota(jnp.int32, (species, species), 0)
        == lax.broadcasted_iota(jnp.int32, (species, species), 1)
    ).astype(F32).astype(BF16)
    for pair in range(pairs):
        block = scratch[pair * LANES : (pair + 1) * LANES, :species].astype(BF16)
        out[pl.ds(first + pair, species, stride=pairs), :] = dot(unit, block, ((1,), (1,)))


def both(scratch, pair, block):
    odd = lane_bit(block.shape, 1)
    zero = jnp.zeros_like(block)
    scratch[pl.ds(pair * LANES, block.shape[0], stride=2), :] = jnp.where(odd, zero, block)
    scratch[pl.ds(pair * LANES + 1, block.shape[0], stride=2), :] = jnp.where(odd, block, zero)
    return scratch[pair * LANES : (pair + 1) * LANES, :]


def multiply(scratch, pair, earlier, later, exact):
    later = both(scratch, pair, later)
    if exact:
        return dot(earlier.astype(BF16), later.astype(BF16))
    earlier_high, earlier_low = halves(earlier)
    high, low = halves(later)
    return dot(earlier_high, high) + (dot(earlier_low, high) + dot(earlier_high, low))


STEP = 8


def diagonals(load, out, first, scratch, pairs):
    count = LANES // 2
    shape = (pairs, LANES)
    giants = count // STEP

    def slid(tiles, shift, mask):
        here = lane_bit(shape, mask)
        return [jnp.where(here, b, a) for a, b in zip(tiles, tiles[shift:] + tiles[:shift])]

    for small in range(STEP):
        tiles = [load(small + STEP * giant) for giant in range(giants)]
        shift = 1
        while shift < giants:
            tiles = slid(tiles, shift, 2 * STEP * shift)
            shift *= 2
        for giant, tile in enumerate(tiles):
            at = (small + STEP * giant) * pairs
            scratch[at : at + pairs, :] = tile
    for giant in range(giants):
        tiles = []
        for j in range(2 * STEP - 1):
            at = (giant * STEP + j) % count * pairs
            tiles.append(scratch[at : at + pairs, :])
        shift = 1
        while shift < STEP:
            tiles = slid(tiles, shift, 2 * shift)[:-shift]
            shift *= 2
        for j, tile in enumerate(tiles):
            at = first + (giant * STEP + j) * pairs
            turn_by = 2 * STEP * giant
            out[at : at + pairs, :] = pltpu.roll(tile, turn_by, 1) if giant else tile


def whole_tiles(ref, first, pairs):
    return lambda b: ref[first + b * pairs : first + (b + 1) * pairs, :]


def part_tiles(mine, other, pairs):
    first_core = lax.axis_index("gx") & 1 == 0

    def load(b):
        low, at = b < LANES // 4, b % (LANES // 4) * pairs
        own, far = mine[at : at + pairs, :], other[at : at + pairs, :]
        return jnp.where(first_core, own if low else far, far if low else own)

    return load


def mapped(ref, vector, first=0):
    pairs = vector.shape[0]
    turns = [vector] + [pltpu.roll(vector, LANES - 2 * j, 1) for j in range(1, STEP)]
    total = None
    for giant in range(LANES // 2 // STEP):
        terms = []
        for j in range(STEP):
            at = first + (giant * STEP + j) * pairs
            terms.append(ref[at : at + pairs, :] * turns[j])
        while len(terms) > 1:
            terms = [a + b for a, b in zip(terms[::2], terms[1::2])]
        part = pltpu.roll(terms[0], LANES - 2 * STEP * giant, 1) if giant else terms[0]
        total = part if total is None else total + part
    return total


def prep_kernel(reverse, blocks, *refs):
    if reverse:
        start, _, passed, *refs = refs
        for p in range(start.shape[0]):
            passed[p] = woven(start[p])
    steps, products, own, maps, native, rows_scratch = refs
    planes, _, rows, width = blocks.shape
    species = LANES // 2
    pairs = rows // 2
    size = species * pairs
    order = list(range(planes))[::-1] if reverse else list(range(planes))
    for step, plane in enumerate(order):
        at = pl.ds(plane * size, size)
        to_rows(rows_scratch, native, reader(blocks, plane, 0), rows, species)
        turn(rows_scratch, maps, 0, pairs, species)
        if step == 0:
            products[at, :] = -maps[...]
            continue
        steps[pl.ds((step - 1) * size, size), :] = maps[...]
        for pair in range(pairs):
            here = pl.ds(plane * size + pair, species, stride=pairs)
            before = pl.ds(order[step - 1] * size + pair, species, stride=pairs)
            later = -maps[pl.ds(pair, species, stride=pairs), :]
            products[here, :] = multiply(rows_scratch, pair, products[before, :], later, step == 1)
    own[...] = products[pl.ds(order[-1] * size, size), :]


def join_kernel(level, reverse, full, pairs, own, *refs):
    here = (lax.axis_index("gx") >> level) & 1
    core = lax.axis_index("gx") & 1
    species = LANES // 2
    _, *refs, scratch = refs
    outs = refs[-2:] if full else refs[-1:]
    partner = refs[: len(refs) - len(outs)]
    later_is_own = here == (0 if reverse else 1)
    for pair in range(pairs):
        mine = own[pl.ds(pair, species, stride=pairs), :]
        if len(partner) == 1:
            theirs = partner[0][pl.ds(pair, species, stride=pairs), :]
        else:
            close = partner[0][pl.ds(pair, species // 2, stride=pairs), :]
            far = partner[1][pl.ds(pair, species // 2, stride=pairs), :]
            theirs = jnp.where(
                core == 0, jnp.concatenate([close, far], 0), jnp.concatenate([far, close], 0)
            )
        earlier = jnp.where(later_is_own, theirs, mine)
        later = jnp.where(later_is_own, mine, theirs)
        if full:
            kept = multiply(scratch, pair, earlier, later, False)
            outs[0][pl.ds(pair, species, stride=pairs), :] = kept
            kept = jnp.where(core == 0, kept[: species // 2], kept[species // 2 :])
        else:
            kept = jnp.where(core == 0, earlier[: species // 2], earlier[species // 2 :])
            kept = multiply(scratch, pair, kept, later, False)
        outs[-1][pl.ds(pair, species // 2, stride=pairs), :] = kept


def base_kernel(start, source, diag, upper, side, rhs, base):
    planes = start.shape[0]
    vectors = [spread(start[p]) for p in range(planes)]
    for p in range(planes):
        own = apply([(reader(diag, p, 0), spread_raw(source[p]))])
        terms = [
            (reader(side, 2, p, 0), shifted(vectors[p], True)),
            (reader(side, 3, p, 0), shifted(vectors[p], False)),
        ]
        if p + 1 < planes:
            terms.append((reader(upper, p, 0), vectors[p + 1]))
        around = apply(terms)
        rhs[p] = gather_pairs(own)
        base[p] = gather_pairs(own - around)


def convert(pairs, sources, outs, scratch):
    size = pairs * LANES // 2
    for source, out in zip(sources, outs):
        for first in range(0, source.shape[0], size):
            diagonals(whole_tiles(source, first, pairs), out, first, scratch, pairs)


def near_kernel(pairs, *refs):
    *refs, scratch = refs
    convert(pairs, refs[: len(refs) // 2], refs[len(refs) // 2 :], scratch)


def far_kernel(pairs, mine, other, out, scratch):
    diagonals(part_tiles(mine, other, pairs), out, 0, scratch, pairs)


def outgoing(offset, partners, here, slots):
    vectors = [offset]
    for level, ref in enumerate(partners):
        passed = mapped(ref, vectors[-1])
        vectors.append(jnp.where((here >> level) & 1 == 0, passed, vectors[-1]))
    place = lax.axis_index("gx")
    for apart in range(slots.shape[0]):
        slots[place ^ apart] = vectors[max(apart.bit_length() - 1, 0)]


def incoming(got, partners, here, reverse):
    count = got.shape[0]
    entering = None
    for level in range(len(partners) + 1)[::-1]:
        total = None
        first = jnp.maximum((here >> level) - 1, 0) << level
        for e in range(1 << level):
            place = first + e
            term = got[count - 1 - place if reverse else place]
            total = term if total is None else total + term
        if entering is not None:
            total = total + mapped(partners[level], entering)
        before = jnp.zeros_like(total) if entering is None else entering
        entering = jnp.where((here >> level) & 1 == 1, total, before)
    return entering


def beside(axis, paired, other):
    place, count = lax.axis_index(axis), lax.axis_size(axis)
    odd = place & 1 == 1
    low = jnp.where(odd, paired, other)
    high = jnp.where(odd, other, paired)
    return jnp.where(place == 0, 0.0, low), jnp.where(place == count - 1, 0.0, high)


def forward_offset_kernel(base, paired, other, ahead, side, upper, step_maps, *rest):
    *partners, drive, offsets, slots = rest
    planes, pairs = base.shape[:2]
    size = pairs * LANES // 2
    here = lax.axis_index("gx")
    last = here == lax.axis_size("gx") - 1
    previous = None
    for p in range(planes):
        low, high = beside("gy", paired[p], other[p])
        terms = [(reader(side, 0, p, 0), spread(low)), (reader(side, 1, p, 0), spread(high))]
        if p + 1 == planes:
            beyond = jnp.where(last, 0.0, ahead[0])
            terms.append((reader(upper, p, 0), spread(beyond)))
        fresh = base[p] - gather_pairs(apply(terms))
        drive[p] = fresh
        if previous is not None:
            fresh = fresh - mapped(step_maps, previous, (p - 1) * size)
        offsets[p] = fresh
        previous = fresh
    outgoing(previous, partners, here, slots)


def forward_kernel(got, drive, offsets, rhs, entry_maps, *rest):
    *partners, out, copy, base = rest
    planes = drive.shape[0]
    size = drive.shape[1] * LANES // 2
    entering = incoming(got, partners, lax.axis_index("gx"), False)
    for p in range(planes):
        value = offsets[p] + mapped(entry_maps, entering, p * size)
        base[p] = rhs[p] - (drive[p] - value)
        out[p] = unwoven(value)
        copy[p] = value


def side_kernel(levels, base, vectors, side, steps, products, partner, *rest):
    parts = rest[: 2 * (levels - 2)]
    out, step_maps, entry_maps, near, *far, scratch = rest[2 * (levels - 2) :]
    planes, pairs = base.shape[:2]
    for p in range(planes):
        vector = spread(vectors[p])
        around = apply(
            [
                (reader(side, 2, p, 0), shifted(vector, True)),
                (reader(side, 3, p, 0), shifted(vector, False)),
            ]
        )
        out[p] = base[p] - gather_pairs(around)
    convert(pairs, (steps, products, partner), (step_maps, entry_maps, near), scratch.at[0])
    for level, ref in enumerate(far):
        diagonals(part_tiles(*parts[2 * level : 2 * level + 2], pairs), ref, 0, scratch.at[1], pairs)


def backward_offset_kernel(base, paired, other, side, step_maps, *rest):
    *partners, offsets, slots = rest
    planes = base.shape[0]
    size = base.shape[1] * LANES // 2
    here = lax.axis_size("gx") - 1 - lax.axis_index("gx")
    previous = None
    for p in range(planes)[::-1]:
        low, high = beside("gy", paired[p], other[p])
        around = apply([(reader(side, 0, p, 0), spread(low)), (reader(side, 1, p, 0), spread(high))])
        fresh = base[p] - gather_pairs(around)
        if previous is not None:
            fresh = fresh - mapped(step_maps, previous, (planes - 2 - p) * size)
        offsets[p] = fresh
        previous = fresh
    outgoing(previous, partners, here, slots)


def backward_kernel(got, offsets, entry_maps, *rest):
    *partners, out = rest
    size = offsets.shape[1] * LANES // 2
    here = lax.axis_size("gx") - 1 - lax.axis_index("gx")
    entering = incoming(got, partners, here, True)
    for p in range(offsets.shape[0]):
        out[p] = unwoven(offsets[p] + mapped(entry_maps, entering, p * size))


def call(kernel, operands, outs, scratch, micros):
    arrays = [o[0] if isinstance(o, tuple) else o for o in operands]
    held = [i for i, o in enumerate(operands) if isinstance(o, tuple)]
    outs = [jax.ShapeDtypeStruct(shape, F32) for shape in outs]
    moved = sum(a.size * a.dtype.itemsize for a in arrays)
    return pl.pallas_call(
        kernel,
        out_shape=outs,
        in_specs=[
            pl.BlockSpec(memory_space=pl.ANY if i in held else pltpu.VMEM) for i in range(len(arrays))
        ],
        out_specs=[pl.BlockSpec(memory_space=pltpu.VMEM) for _ in outs],
        scratch_shapes=[pltpu.VMEM(shape, F32) for shape in scratch],
        compiler_params=pltpu.CompilerParams(vmem_limit_bytes=12 << 20),
        cost_estimate=pl.CostEstimate(
            flops=int(micros * 1.15e9), bytes_accessed=moved, transcendentals=0
        ),
    )(*arrays)


def swaps(block):
    count, rows = lax.axis_size("gx"), lax.axis_size("gy")
    route = []
    for place in range(count):
        for row in range(rows):
            target = row + 1 if row & 1 else row - 1
            to = place * rows + target if 0 <= target < rows else (place ^ 1) * rows + row
            route.append((place * rows + row, to))
    return crossed(block, "gy", 1), lax.ppermute(block, ("gx", "gy"), route)


def crossed(block, axis, distance):
    return lax.ppermute(block, axis, [(i, i ^ distance) for i in range(lax.axis_size(axis))])


def exchange(slots, axis):
    return lax.all_to_all(slots, axis, 0, 0)


def local(start, source, diag_inverse, x_lower, x_upper, side_blocks):
    planes, _, depth, width = x_lower.shape
    species = start.shape[2] // depth
    pairs = depth // 2
    count = lax.axis_size("gx")
    levels = count.bit_length() - 1
    size = species * pairs
    one = (pairs, LANES)
    vec = (planes,) + one
    maps, steps = (planes * size, LANES), ((planes - 1) * size, LANES)
    whole, half = (size, LANES), (size // 2, LANES)
    slots = (count,) + one
    start = start.reshape(vec)
    source = source.reshape(vec)

    def prepare(reverse, blocks, after=None):
        return call(
            functools.partial(prep_kernel, reverse),
            [blocks] + ([start, (after, None)] if reverse else []),
            ([vec] if reverse else []) + [steps, maps, whole],
            [whole, (depth * species // 2, LANES), (depth * species, LANES)],
            1.0,
        )

    def partner_maps(reverse, own, after):
        partners, kept = [], None
        for level in range(levels - 1):
            if level == 0:
                got = [crossed(own, "gx", 1)]
            else:
                mine = crossed(kept, "gx", 1 << level)
                got = [mine, crossed(mine, "gx", 1)]
            partners += got
            if level + 2 < levels:
                full = level + 3 < levels
                outs = call(
                    functools.partial(join_kernel, level, reverse, full, pairs),
                    [own, (after, None)] + got,
                    [whole, half] if full else [half],
                    [(depth * species, LANES)],
                    0.4,
                )
                own, kept = outs[0], outs[-1]
        return partners

    step_maps, products, own = prepare(False, x_lower)
    start, upper_steps, upper_products, upper_own = prepare(True, x_upper, products)
    lower = [step_maps, products, *partner_maps(False, own, start)]
    upper = [upper_steps, upper_products, *partner_maps(True, upper_own, start)]
    paired, other = swaps(start)
    ahead = lax.ppermute(start[:1], "gx", [(i, (i - 1) % count) for i in range(count)])

    rhs, base = call(
        base_kernel, [start, source, diag_inverse, x_upper, side_blocks], [vec, vec], [], 5.0
    )
    step_maps, entry_maps, near = call(
        functools.partial(near_kernel, pairs), lower[:3], [steps, maps, whole], [whole], 0.5
    )
    partners = [near]
    for level in range(levels - 2):
        partners += call(
            functools.partial(far_kernel, pairs),
            lower[3 + 2 * level : 5 + 2 * level],
            [whole],
            [whole],
            0.3,
        )
    drive, offsets, sent = call(
        forward_offset_kernel,
        [base, paired, other, ahead, side_blocks, x_upper, step_maps] + partners,
        [vec, vec, slots],
        [],
        1.5,
    )
    forward, copy, base = call(
        forward_kernel,
        [exchange(sent, "gx"), drive, offsets, rhs, entry_maps] + partners,
        [vec, vec, vec],
        [],
        1.0,
    )
    paired, other = swaps(copy)
    base, step_maps, entry_maps, *partners = call(
        functools.partial(side_kernel, levels),
        [base, copy, side_blocks] + upper,
        [vec, steps, maps, whole] + [whole] * (levels - 2),
        [(2,) + whole],
        0.7,
    )
    offsets, sent = call(
        backward_offset_kernel,
        [base, paired, other, side_blocks, step_maps] + partners,
        [vec, slots],
        [],
        1.5,
    )
    (result,) = call(
        backward_kernel, [exchange(sent, "gx"), offsets, entry_maps] + partners, [vec], [], 1.0
    )
    shape = (planes, 1, depth * species)
    return forward.reshape(shape), result.reshape(shape)


def solution(mesh):
    return jax.shard_map(
        local,
        mesh=mesh,
        in_specs=(
            P("gx", "gy", None),
            P("gx", "gy", None),
            P("gx", "gy", None, None),
            P("gx", "gy", None, None),
            P("gx", "gy", None, None),
            P(None, "gx", "gy", None, None),
        ),
        out_specs=(P("gx", "gy", None), P("gx", "gy", None)),
        check_vma=False,
    )
```

```python
import functools

import jax
import jax.numpy as jnp
from jax import lax
from jax.experimental import pallas as pl
from jax.experimental.pallas import tpu as pltpu
from jax.sharding import PartitionSpec as P

LANES = 128
F32 = jnp.float32
BF16 = jnp.bfloat16


def lane_bit(shape, shift):
    return (lax.broadcasted_iota(jnp.int32, shape, len(shape) - 1) & shift) != 0


def segment_sums(leaf, tiles, rows):
    shape = (rows, LANES)

    def node(base, stride, shift):
        if stride == tiles:
            return leaf(base)
        low = node(base, stride * 2, shift * 2)
        high = node(base + stride, stride * 2, shift * 2)
        low = low + pltpu.roll(low, LANES - shift, 1)
        high = high + pltpu.roll(high, shift, 1)
        return jnp.where(lane_bit(shape, shift), high, low)

    part = node(0, 1, 2)
    odd = lane_bit(shape, 1)
    part = part + jnp.where(odd, pltpu.roll(part, 1, 1), pltpu.roll(part, LANES - 1, 1))
    upper = lane_bit(shape, LANES // 2)
    return jnp.where(upper == odd, part, pltpu.roll(part, LANES // 2, 1))


def apply(terms):
    rows = terms[0][1].shape[0]
    tiles = LANES // 4

    def leaf(t):
        return sum(read(t).astype(F32) * vector for read, vector in terms)

    return segment_sums(leaf, tiles, rows)


def reader(ref, *index):
    return lambda t: ref[(*index, slice(None), slice(t * LANES, (t + 1) * LANES))]


def lanes(shape):
    return lax.broadcasted_iota(jnp.int32, shape, 1)


def woven(raw):
    lane = lanes(raw.shape)
    return jnp.take_along_axis(raw, (lane >> 1) + (lane & 1) * (LANES // 2), 1)


def unwoven(vector):
    lane = lanes(vector.shape)
    return jnp.take_along_axis(vector, (lane & LANES // 2 - 1) * 2 + lane // (LANES // 2), 1)


def spread(vector):
    half = vector.shape[0]
    row = lax.broadcasted_iota(jnp.int32, vector.shape, 0)
    place = (lanes(vector.shape) & LANES // 2 - 1) * 2 + (row & 1)
    parts = []
    for first in (0, half // 2):
        block = jnp.take_along_axis(vector, first + row // 2, 0)
        parts.append(jnp.take_along_axis(block, place, 1))
    return jnp.concatenate(parts, 0)


def spread_raw(raw):
    half = raw.shape[0]
    row = lax.broadcasted_iota(jnp.int32, raw.shape, 0)
    same = (row & 1 == 1) == lane_bit(raw.shape, LANES // 2)
    parts = []
    for first in (0, half // 2):
        block = jnp.take_along_axis(raw, first + row // 2, 0)
        parts.append(jnp.where(same, block, pltpu.roll(block, LANES // 2, 1)))
    return jnp.concatenate(parts, 0)


def gather_pairs(vector):
    half = vector.shape[0] // 2
    shape = (half, LANES)
    row = lax.broadcasted_iota(jnp.int32, shape, 0)
    odd = lane_bit(shape, 1)
    parts = []
    for block in (vector[:half], vector[half:]):
        block = jnp.take_along_axis(block, lanes(shape) >> 1, 1)
        block = jnp.where(odd, pltpu.roll(block, half - 1, 0), block)
        parts.append(jnp.take_along_axis(block, 2 * row & half - 1, 0))
    return jnp.where(row < half // 2, parts[0], parts[1])


def shifted(vector, down):
    rows = vector.shape[0]
    row = lax.broadcasted_iota(jnp.int32, vector.shape, 0)
    if down:
        return jnp.where(row == 0, 0.0, pltpu.roll(vector, 1, 0))
    return jnp.where(row == rows - 1, 0.0, pltpu.roll(vector, rows - 1, 0))


def to_rows(scratch, native, read, rows, species):
    pairs = rows // 2
    for t in range(species // 2):
        native[t * rows : (t + 1) * rows, :] = read(t).astype(F32)
    for t in range(species // 2):
        for inner in (0, 1):
            tile = native[pl.ds(t * rows + inner, pairs, stride=2), :]
            other = pltpu.roll(tile, LANES // 2, 1)
            scratch[pl.ds(4 * t + inner, pairs, stride=LANES), :] = tile
            scratch[pl.ds(4 * t + 2 + inner, pairs, stride=LANES), :] = other


def halves(a):
    high = a.astype(BF16)
    return high, (a - high.astype(F32)).astype(BF16)


def dot(a, b, dims=((1,), (0,))):
    return lax.dot_general(a, b, (dims, ((), ())), preferred_element_type=F32)


def turn(scratch, out, first, pairs, species):
    unit = (
        lax.broadcasted_iota(jnp.int32, (species, species), 0)
        == lax.broadcasted_iota(jnp.int32, (species, species), 1)
    ).astype(F32).astype(BF16)
    for pair in range(pairs):
        block = scratch[pair * LANES : (pair + 1) * LANES, :species].astype(BF16)
        out[pl.ds(first + pair, species, stride=pairs), :] = dot(unit, block, ((1,), (1,)))


def both(scratch, pair, block):
    odd = lane_bit(block.shape, 1)
    zero = jnp.zeros_like(block)
    scratch[pl.ds(pair * LANES, block.shape[0], stride=2), :] = jnp.where(odd, zero, block)
    scratch[pl.ds(pair * LANES + 1, block.shape[0], stride=2), :] = jnp.where(odd, block, zero)
    return scratch[pair * LANES : (pair + 1) * LANES, :]


def multiply(scratch, pair, earlier, later, exact):
    later = both(scratch, pair, later)
    if exact:
        return dot(earlier.astype(BF16), later.astype(BF16))
    earlier_high, earlier_low = halves(earlier)
    high, low = halves(later)
    return dot(earlier_high, high) + (dot(earlier_low, high) + dot(earlier_high, low))


STEP = 8


def diagonals(load, out, first, scratch, pairs):
    count = LANES // 2
    shape = (pairs, LANES)
    giants = count // STEP

    def slid(tiles, shift, mask):
        here = lane_bit(shape, mask)
        return [jnp.where(here, b, a) for a, b in zip(tiles, tiles[shift:] + tiles[:shift])]

    for small in range(STEP):
        tiles = [load(small + STEP * giant) for giant in range(giants)]
        shift = 1
        while shift < giants:
            tiles = slid(tiles, shift, 2 * STEP * shift)
            shift *= 2
        for giant, tile in enumerate(tiles):
            at = (small + STEP * giant) * pairs
            scratch[at : at + pairs, :] = tile
    for giant in range(giants):
        tiles = []
        for j in range(2 * STEP - 1):
            at = (giant * STEP + j) % count * pairs
            tiles.append(scratch[at : at + pairs, :])
        shift = 1
        while shift < STEP:
            tiles = slid(tiles, shift, 2 * shift)[:-shift]
            shift *= 2
        for j, tile in enumerate(tiles):
            at = first + (giant * STEP + j) * pairs
            turn_by = 2 * STEP * giant
            out[at : at + pairs, :] = pltpu.roll(tile, turn_by, 1) if giant else tile


def whole_tiles(ref, first, pairs):
    return lambda b: ref[first + b * pairs : first + (b + 1) * pairs, :]


def part_tiles(mine, other, pairs):
    first_core = lax.axis_index("gx") & 1 == 0

    def load(b):
        low, at = b < LANES // 4, b % (LANES // 4) * pairs
        own, far = mine[at : at + pairs, :], other[at : at + pairs, :]
        return jnp.where(first_core, own if low else far, far if low else own)

    return load


def mapped(ref, vector, first=0):
    pairs = vector.shape[0]
    turns = [vector] + [pltpu.roll(vector, LANES - 2 * j, 1) for j in range(1, STEP)]
    total = None
    for giant in range(LANES // 2 // STEP):
        terms = []
        for j in range(STEP):
            at = first + (giant * STEP + j) * pairs
            terms.append(ref[at : at + pairs, :] * turns[j])
        while len(terms) > 1:
            terms = [a + b for a, b in zip(terms[::2], terms[1::2])]
        part = pltpu.roll(terms[0], LANES - 2 * STEP * giant, 1) if giant else terms[0]
        total = part if total is None else total + part
    return total


def prep_kernel(reverse, blocks, *refs):
    if reverse:
        start, _, passed, *refs = refs
        for p in range(start.shape[0]):
            passed[p] = woven(start[p])
    steps, products, own, maps, native, rows_scratch = refs
    planes, _, rows, width = blocks.shape
    species = LANES // 2
    pairs = rows // 2
    size = species * pairs
    order = list(range(planes))[::-1] if reverse else list(range(planes))
    for step, plane in enumerate(order):
        at = pl.ds(plane * size, size)
        to_rows(rows_scratch, native, reader(blocks, plane, 0), rows, species)
        turn(rows_scratch, maps, 0, pairs, species)
        if step == 0:
            products[at, :] = -maps[...]
            continue
        steps[pl.ds((step - 1) * size, size), :] = maps[...]
        for pair in range(pairs):
            here = pl.ds(plane * size + pair, species, stride=pairs)
            before = pl.ds(order[step - 1] * size + pair, species, stride=pairs)
            later = -maps[pl.ds(pair, species, stride=pairs), :]
            products[here, :] = multiply(rows_scratch, pair, products[before, :], later, step == 1)
    own[...] = products[pl.ds(order[-1] * size, size), :]


def join_kernel(level, reverse, full, pairs, own, *refs):
    here = (lax.axis_index("gx") >> level) & 1
    core = lax.axis_index("gx") & 1
    species = LANES // 2
    _, *refs, scratch = refs
    outs = refs[-2:] if full and not reverse else refs[-1:]
    partner = refs[: len(refs) - len(outs)]
    later_is_own = here == (0 if reverse else 1)
    for pair in range(pairs):
        mine = own[pl.ds(pair, species, stride=pairs), :]
        if len(partner) == 1:
            theirs = partner[0][pl.ds(pair, species, stride=pairs), :]
        else:
            close = partner[0][pl.ds(pair, species // 2, stride=pairs), :]
            far = partner[1][pl.ds(pair, species // 2, stride=pairs), :]
            theirs = jnp.where(
                core == 0, jnp.concatenate([close, far], 0), jnp.concatenate([far, close], 0)
            )
        earlier = jnp.where(later_is_own, theirs, mine)
        later = jnp.where(later_is_own, mine, theirs)
        if full:
            kept = multiply(scratch, pair, earlier, later, False)
            outs[0][pl.ds(pair, species, stride=pairs), :] = kept
            if reverse:
                continue
            kept = jnp.where(core == 0, kept[: species // 2], kept[species // 2 :])
        else:
            kept = jnp.where(core == 0, earlier[: species // 2], earlier[species // 2 :])
            kept = multiply(scratch, pair, kept, later, False)
        outs[-1][pl.ds(pair, species // 2, stride=pairs), :] = kept


def base_kernel(start, source, diag, upper, side, rhs, base):
    planes = start.shape[0]
    vectors = [spread(start[p]) for p in range(planes)]
    for p in range(planes):
        own = apply([(reader(diag, p, 0), spread_raw(source[p]))])
        terms = [
            (reader(side, 2, p, 0), shifted(vectors[p], True)),
            (reader(side, 3, p, 0), shifted(vectors[p], False)),
        ]
        if p + 1 < planes:
            terms.append((reader(upper, p, 0), vectors[p + 1]))
        around = apply(terms)
        rhs[p] = gather_pairs(own)
        base[p] = gather_pairs(own - around)


def convert(pairs, sources, outs, scratch):
    size = pairs * LANES // 2
    for source, out in zip(sources, outs):
        for first in range(0, source.shape[0], size):
            diagonals(whole_tiles(source, first, pairs), out, first, scratch, pairs)


def near_kernel(pairs, *refs):
    *refs, scratch = refs
    convert(pairs, refs[: len(refs) // 2], refs[len(refs) // 2 :], scratch)


def far_kernel(pairs, mine, other, out, scratch):
    diagonals(part_tiles(mine, other, pairs), out, 0, scratch, pairs)


def outgoing(offset, partners, here, slots):
    vectors = [offset]
    for level, ref in enumerate(partners):
        passed = mapped(ref, vectors[-1])
        vectors.append(jnp.where((here >> level) & 1 == 0, passed, vectors[-1]))
    place = lax.axis_index("gx")
    for apart in range(slots.shape[0]):
        slots[place ^ apart] = vectors[max(apart.bit_length() - 1, 0)]


def incoming(got, partners, here, reverse):
    count = got.shape[0]
    entering = None
    for level in range(len(partners) + 1)[::-1]:
        total = None
        first = jnp.maximum((here >> level) - 1, 0) << level
        for e in range(1 << level):
            place = first + e
            term = got[count - 1 - place if reverse else place]
            total = term if total is None else total + term
        if entering is not None:
            total = total + mapped(partners[level], entering)
        before = jnp.zeros_like(total) if entering is None else entering
        entering = jnp.where((here >> level) & 1 == 1, total, before)
    return entering


def beside(axis, paired, other):
    place, count = lax.axis_index(axis), lax.axis_size(axis)
    odd = place & 1 == 1
    low = jnp.where(odd, paired, other)
    high = jnp.where(odd, other, paired)
    return jnp.where(place == 0, 0.0, low), jnp.where(place == count - 1, 0.0, high)


def forward_offset_kernel(base, paired, other, ahead, side, upper, step_maps, *rest):
    *partners, drive, offsets, slots = rest
    planes, pairs = base.shape[:2]
    size = pairs * LANES // 2
    here = lax.axis_index("gx")
    last = here == lax.axis_size("gx") - 1
    previous = None
    for p in range(planes):
        low, high = beside("gy", paired[p], other[p])
        terms = [(reader(side, 0, p, 0), spread(low)), (reader(side, 1, p, 0), spread(high))]
        if p + 1 == planes:
            beyond = jnp.where(last, 0.0, ahead[0])
            terms.append((reader(upper, p, 0), spread(beyond)))
        fresh = base[p] - gather_pairs(apply(terms))
        drive[p] = fresh
        if previous is not None:
            fresh = fresh - mapped(step_maps, previous, (p - 1) * size)
        offsets[p] = fresh
        previous = fresh
    outgoing(previous, partners, here, slots)


def forward_kernel(got, drive, offsets, rhs, entry_maps, *rest):
    *partners, out, copy, base = rest
    planes = drive.shape[0]
    size = drive.shape[1] * LANES // 2
    entering = incoming(got, partners, lax.axis_index("gx"), False)
    for p in range(planes):
        value = offsets[p] + mapped(entry_maps, entering, p * size)
        base[p] = rhs[p] - (drive[p] - value)
        out[p] = unwoven(value)
        copy[p] = value


def side_kernel(base, vectors, side, *rest):
    *rest, scratch = rest
    sources, (out, *converted) = rest[: len(rest) // 2], rest[len(rest) // 2 :]
    planes, pairs = base.shape[:2]
    for p in range(planes):
        vector = spread(vectors[p])
        around = apply(
            [
                (reader(side, 2, p, 0), shifted(vector, True)),
                (reader(side, 3, p, 0), shifted(vector, False)),
            ]
        )
        out[p] = base[p] - gather_pairs(around)
    convert(pairs, sources, converted, scratch)


def backward_offset_kernel(base, paired, other, side, step_maps, *rest):
    *partners, offsets, slots = rest
    planes = base.shape[0]
    size = base.shape[1] * LANES // 2
    here = lax.axis_size("gx") - 1 - lax.axis_index("gx")
    previous = None
    for p in range(planes)[::-1]:
        low, high = beside("gy", paired[p], other[p])
        around = apply([(reader(side, 0, p, 0), spread(low)), (reader(side, 1, p, 0), spread(high))])
        fresh = base[p] - gather_pairs(around)
        if previous is not None:
            fresh = fresh - mapped(step_maps, previous, (planes - 2 - p) * size)
        offsets[p] = fresh
        previous = fresh
    outgoing(previous, partners, here, slots)


def backward_kernel(got, offsets, entry_maps, *rest):
    *partners, out = rest
    size = offsets.shape[1] * LANES // 2
    here = lax.axis_size("gx") - 1 - lax.axis_index("gx")
    entering = incoming(got, partners, here, True)
    for p in range(offsets.shape[0]):
        out[p] = unwoven(offsets[p] + mapped(entry_maps, entering, p * size))


def call(kernel, operands, outs, scratch, micros):
    arrays = [o[0] if isinstance(o, tuple) else o for o in operands]
    held = [i for i, o in enumerate(operands) if isinstance(o, tuple)]
    outs = [jax.ShapeDtypeStruct(shape, F32) for shape in outs]
    moved = sum(a.size * a.dtype.itemsize for a in arrays)
    return pl.pallas_call(
        kernel,
        out_shape=outs,
        in_specs=[
            pl.BlockSpec(memory_space=pl.ANY if i in held else pltpu.VMEM) for i in range(len(arrays))
        ],
        out_specs=[pl.BlockSpec(memory_space=pltpu.VMEM) for _ in outs],
        scratch_shapes=[pltpu.VMEM(shape, F32) for shape in scratch],
        compiler_params=pltpu.CompilerParams(vmem_limit_bytes=12 << 20),
        cost_estimate=pl.CostEstimate(
            flops=int(micros * 1.15e9), bytes_accessed=moved, transcendentals=0
        ),
    )(*arrays)


def swaps(block):
    count, rows = lax.axis_size("gx"), lax.axis_size("gy")
    route = []
    for place in range(count):
        for row in range(rows):
            target = row + 1 if row & 1 else row - 1
            to = place * rows + target if 0 <= target < rows else (place ^ 1) * rows + row
            route.append((place * rows + row, to))
    return crossed(block, "gy", 1), lax.ppermute(block, ("gx", "gy"), route)


def crossed(block, axis, distance):
    return lax.ppermute(block, axis, [(i, i ^ distance) for i in range(lax.axis_size(axis))])


def exchange(slots, axis):
    return lax.all_to_all(slots, axis, 0, 0)


def local(start, source, diag_inverse, x_lower, x_upper, side_blocks):
    planes, _, depth, width = x_lower.shape
    species = start.shape[2] // depth
    pairs = depth // 2
    count = lax.axis_size("gx")
    levels = count.bit_length() - 1
    size = species * pairs
    one = (pairs, LANES)
    vec = (planes,) + one
    maps, steps = (planes * size, LANES), ((planes - 1) * size, LANES)
    whole, half = (size, LANES), (size // 2, LANES)
    slots = (count,) + one
    start = start.reshape(vec)
    source = source.reshape(vec)

    def prepare(reverse, blocks, after=None):
        return call(
            functools.partial(prep_kernel, reverse),
            [blocks] + ([start, (after, None)] if reverse else []),
            ([vec] if reverse else []) + [steps, maps, whole],
            [whole, (depth * species // 2, LANES), (depth * species, LANES)],
            1.0,
        )

    def partner_maps(reverse, own, after):
        partners, kept = [], None
        for level in range(levels - 1):
            if level == 0 or reverse:
                got = [crossed(own, "gx", 1 << level)]
            else:
                mine = crossed(kept, "gx", 1 << level)
                got = [mine, crossed(mine, "gx", 1)]
            partners += got
            if level + 2 < levels:
                full = reverse or level + 3 < levels
                outs = call(
                    functools.partial(join_kernel, level, reverse, full, pairs),
                    [own, (after, None)] + got,
                    [whole] if reverse else [whole, half] if full else [half],
                    [(depth * species, LANES)],
                    0.4,
                )
                own, kept = outs[0], outs[-1]
        return partners

    step_maps, products, own = prepare(False, x_lower)
    start, upper_steps, upper_products, upper_own = prepare(True, x_upper, products)
    rhs, base = call(
        base_kernel, [start, source, diag_inverse, x_upper, side_blocks], [vec, vec], [], 5.0
    )
    lower = [step_maps, products, *partner_maps(False, own, start)]
    upper = [upper_steps, upper_products, *partner_maps(True, upper_own, start)]
    paired, other = swaps(start)
    ahead = lax.ppermute(start[:1], "gx", [(i, (i - 1) % count) for i in range(count)])

    step_maps, entry_maps, near = call(
        functools.partial(near_kernel, pairs), lower[:3], [steps, maps, whole], [whole], 0.5
    )
    partners = [near]
    for level in range(levels - 2):
        partners += call(
            functools.partial(far_kernel, pairs),
            lower[3 + 2 * level : 5 + 2 * level],
            [whole],
            [whole],
            0.3,
        )
    drive, offsets, sent = call(
        forward_offset_kernel,
        [base, paired, other, ahead, side_blocks, x_upper, step_maps] + partners,
        [vec, vec, slots],
        [],
        1.5,
    )
    forward, copy, base = call(
        forward_kernel,
        [exchange(sent, "gx"), drive, offsets, rhs, entry_maps] + partners,
        [vec, vec, vec],
        [],
        1.0,
    )
    paired, other = swaps(copy)
    base, step_maps, entry_maps, *partners = call(
        side_kernel,
        [base, copy, side_blocks] + upper,
        [vec, steps, maps] + [whole] * (levels - 1),
        [whole],
        0.7,
    )
    offsets, sent = call(
        backward_offset_kernel,
        [base, paired, other, side_blocks, step_maps] + partners,
        [vec, slots],
        [],
        1.5,
    )
    (result,) = call(
        backward_kernel, [exchange(sent, "gx"), offsets, entry_maps] + partners, [vec], [], 1.0
    )
    shape = (planes, 1, depth * species)
    return forward.reshape(shape), result.reshape(shape)


def solution(mesh):
    return jax.shard_map(
        local,
        mesh=mesh,
        in_specs=(
            P("gx", "gy", None),
            P("gx", "gy", None),
            P("gx", "gy", None, None),
            P("gx", "gy", None, None),
            P("gx", "gy", None, None),
            P(None, "gx", "gy", None, None),
        ),
        out_specs=(P("gx", "gy", None), P("gx", "gy", None)),
        check_vma=False,
    )
```

```python
import functools

import jax
import jax.numpy as jnp
from jax import lax
from jax.experimental import pallas as pl
from jax.experimental.pallas import tpu as pltpu
from jax.sharding import PartitionSpec as P

LANES = 128
F32 = jnp.float32
BF16 = jnp.bfloat16


def lane_bit(shape, shift):
    return (lax.broadcasted_iota(jnp.int32, shape, len(shape) - 1) & shift) != 0


def segment_sums(leaf, tiles, rows):
    shape = (rows, LANES)

    def node(base, stride, shift):
        if stride == tiles:
            return leaf(base)
        low = node(base, stride * 2, shift * 2)
        high = node(base + stride, stride * 2, shift * 2)
        low = low + pltpu.roll(low, LANES - shift, 1)
        high = high + pltpu.roll(high, shift, 1)
        return jnp.where(lane_bit(shape, shift), high, low)

    part = node(0, 1, 2)
    odd = lane_bit(shape, 1)
    part = part + jnp.where(odd, pltpu.roll(part, 1, 1), pltpu.roll(part, LANES - 1, 1))
    upper = lane_bit(shape, LANES // 2)
    return jnp.where(upper == odd, part, pltpu.roll(part, LANES // 2, 1))


def apply(terms):
    rows = terms[0][1].shape[0]
    tiles = LANES // 4

    def leaf(t):
        return sum(read(t).astype(F32) * vector for read, vector in terms)

    return segment_sums(leaf, tiles, rows)


def reader(ref, *index):
    return lambda t: ref[(*index, slice(None), slice(t * LANES, (t + 1) * LANES))]


def lanes(shape):
    return lax.broadcasted_iota(jnp.int32, shape, 1)


def woven(raw):
    lane = lanes(raw.shape)
    return jnp.take_along_axis(raw, (lane >> 1) + (lane & 1) * (LANES // 2), 1)


def unwoven(vector):
    lane = lanes(vector.shape)
    return jnp.take_along_axis(vector, (lane & LANES // 2 - 1) * 2 + lane // (LANES // 2), 1)


def spread(vector):
    half = vector.shape[0]
    row = lax.broadcasted_iota(jnp.int32, vector.shape, 0)
    place = (lanes(vector.shape) & LANES // 2 - 1) * 2 + (row & 1)
    parts = []
    for first in (0, half // 2):
        block = jnp.take_along_axis(vector, first + row // 2, 0)
        parts.append(jnp.take_along_axis(block, place, 1))
    return jnp.concatenate(parts, 0)


def spread_raw(raw):
    half = raw.shape[0]
    row = lax.broadcasted_iota(jnp.int32, raw.shape, 0)
    same = (row & 1 == 1) == lane_bit(raw.shape, LANES // 2)
    parts = []
    for first in (0, half // 2):
        block = jnp.take_along_axis(raw, first + row // 2, 0)
        parts.append(jnp.where(same, block, pltpu.roll(block, LANES // 2, 1)))
    return jnp.concatenate(parts, 0)


def gather_pairs(vector):
    half = vector.shape[0] // 2
    shape = (half, LANES)
    row = lax.broadcasted_iota(jnp.int32, shape, 0)
    odd = lane_bit(shape, 1)
    parts = []
    for block in (vector[:half], vector[half:]):
        block = jnp.take_along_axis(block, lanes(shape) >> 1, 1)
        block = jnp.where(odd, pltpu.roll(block, half - 1, 0), block)
        parts.append(jnp.take_along_axis(block, 2 * row & half - 1, 0))
    return jnp.where(row < half // 2, parts[0], parts[1])


def shifted(vector, down):
    rows = vector.shape[0]
    row = lax.broadcasted_iota(jnp.int32, vector.shape, 0)
    if down:
        return jnp.where(row == 0, 0.0, pltpu.roll(vector, 1, 0))
    return jnp.where(row == rows - 1, 0.0, pltpu.roll(vector, rows - 1, 0))


def to_rows(scratch, native, read, rows, species):
    pairs = rows // 2
    for t in range(species // 2):
        native[t * rows : (t + 1) * rows, :] = read(t).astype(F32)
    for t in range(species // 2):
        for inner in (0, 1):
            tile = native[pl.ds(t * rows + inner, pairs, stride=2), :]
            other = pltpu.roll(tile, LANES // 2, 1)
            scratch[pl.ds(4 * t + inner, pairs, stride=LANES), :] = tile
            scratch[pl.ds(4 * t + 2 + inner, pairs, stride=LANES), :] = other


def halves(a):
    high = a.astype(BF16)
    return high, (a - high.astype(F32)).astype(BF16)


def dot(a, b, dims=((1,), (0,))):
    return lax.dot_general(a, b, (dims, ((), ())), preferred_element_type=F32)


def turn(scratch, out, first, pairs, species):
    unit = (
        lax.broadcasted_iota(jnp.int32, (species, species), 0)
        == lax.broadcasted_iota(jnp.int32, (species, species), 1)
    ).astype(F32).astype(BF16)
    for pair in range(pairs):
        block = scratch[pair * LANES : (pair + 1) * LANES, :species].astype(BF16)
        out[pl.ds(first + pair, species, stride=pairs), :] = dot(unit, block, ((1,), (1,)))


def both(scratch, pair, block):
    odd = lane_bit(block.shape, 1)
    zero = jnp.zeros_like(block)
    scratch[pl.ds(pair * LANES, block.shape[0], stride=2), :] = jnp.where(odd, zero, block)
    scratch[pl.ds(pair * LANES + 1, block.shape[0], stride=2), :] = jnp.where(odd, block, zero)
    return scratch[pair * LANES : (pair + 1) * LANES, :]


def multiply(scratch, pair, earlier, later, exact):
    later = both(scratch, pair, later)
    if exact:
        return dot(earlier.astype(BF16), later.astype(BF16))
    earlier_high, earlier_low = halves(earlier)
    high, low = halves(later)
    return dot(earlier_high, high) + (dot(earlier_low, high) + dot(earlier_high, low))


STEP = 8


def diagonals(load, out, first, scratch, pairs):
    count = LANES // 2
    shape = (pairs, LANES)
    giants = count // STEP

    def slid(tiles, shift, mask):
        here = lane_bit(shape, mask)
        return [jnp.where(here, b, a) for a, b in zip(tiles, tiles[shift:] + tiles[:shift])]

    for small in range(STEP):
        tiles = [load(small + STEP * giant) for giant in range(giants)]
        shift = 1
        while shift < giants:
            tiles = slid(tiles, shift, 2 * STEP * shift)
            shift *= 2
        for giant, tile in enumerate(tiles):
            at = (small + STEP * giant) * pairs
            scratch[at : at + pairs, :] = tile
    for giant in range(giants):
        tiles = []
        for j in range(2 * STEP - 1):
            at = (giant * STEP + j) % count * pairs
            tiles.append(scratch[at : at + pairs, :])
        shift = 1
        while shift < STEP:
            tiles = slid(tiles, shift, 2 * shift)[:-shift]
            shift *= 2
        for j, tile in enumerate(tiles):
            at = first + (giant * STEP + j) * pairs
            turn_by = 2 * STEP * giant
            out[at : at + pairs, :] = pltpu.roll(tile, turn_by, 1) if giant else tile


def whole_tiles(ref, first, pairs):
    return lambda b: ref[first + b * pairs : first + (b + 1) * pairs, :]


def part_tiles(mine, other, pairs):
    first_core = lax.axis_index("gx") & 1 == 0

    def load(b):
        low, at = b < LANES // 4, b % (LANES // 4) * pairs
        own, far = mine[at : at + pairs, :], other[at : at + pairs, :]
        return jnp.where(first_core, own if low else far, far if low else own)

    return load


def mapped(ref, vector, first=0):
    pairs = vector.shape[0]
    turns = [vector] + [pltpu.roll(vector, LANES - 2 * j, 1) for j in range(1, STEP)]
    total = None
    for giant in range(LANES // 2 // STEP):
        terms = []
        for j in range(STEP):
            at = first + (giant * STEP + j) * pairs
            terms.append(ref[at : at + pairs, :] * turns[j])
        while len(terms) > 1:
            terms = [a + b for a, b in zip(terms[::2], terms[1::2])]
        part = pltpu.roll(terms[0], LANES - 2 * STEP * giant, 1) if giant else terms[0]
        total = part if total is None else total + part
    return total


def prep_kernel(reverse, blocks, *refs):
    steps, products, own, maps, native, rows_scratch = refs[1:] if reverse else refs
    planes, _, rows, width = blocks.shape
    species = LANES // 2
    pairs = rows // 2
    size = species * pairs
    order = list(range(planes))[::-1] if reverse else list(range(planes))
    for step, plane in enumerate(order):
        at = pl.ds(plane * size, size)
        to_rows(rows_scratch, native, reader(blocks, plane, 0), rows, species)
        turn(rows_scratch, maps, 0, pairs, species)
        if step == 0:
            products[at, :] = -maps[...]
            continue
        steps[pl.ds((step - 1) * size, size), :] = maps[...]
        for pair in range(pairs):
            here = pl.ds(plane * size + pair, species, stride=pairs)
            before = pl.ds(order[step - 1] * size + pair, species, stride=pairs)
            later = -maps[pl.ds(pair, species, stride=pairs), :]
            products[here, :] = multiply(rows_scratch, pair, products[before, :], later, step == 1)
    own[...] = products[pl.ds(order[-1] * size, size), :]


def weave_kernel(start, passed):
    for p in range(start.shape[0]):
        passed[p] = woven(start[p])


def join_kernel(level, reverse, full, pairs, own, *refs):
    here = (lax.axis_index("gx") >> level) & 1
    core = lax.axis_index("gx") & 1
    species = LANES // 2
    _, *refs, scratch = refs
    if level == 0 and not reverse:
        start, *refs, passed = refs
        weave_kernel(start, passed)
    outs = refs[-2:] if full and not reverse else refs[-1:]
    partner = refs[: len(refs) - len(outs)]
    later_is_own = here == (0 if reverse else 1)
    for pair in range(pairs):
        mine = own[pl.ds(pair, species, stride=pairs), :]
        if len(partner) == 1:
            theirs = partner[0][pl.ds(pair, species, stride=pairs), :]
        else:
            close = partner[0][pl.ds(pair, species // 2, stride=pairs), :]
            far = partner[1][pl.ds(pair, species // 2, stride=pairs), :]
            theirs = jnp.where(
                core == 0, jnp.concatenate([close, far], 0), jnp.concatenate([far, close], 0)
            )
        earlier = jnp.where(later_is_own, theirs, mine)
        later = jnp.where(later_is_own, mine, theirs)
        if full:
            kept = multiply(scratch, pair, earlier, later, False)
            outs[0][pl.ds(pair, species, stride=pairs), :] = kept
            if reverse:
                continue
            kept = jnp.where(core == 0, kept[: species // 2], kept[species // 2 :])
        else:
            kept = jnp.where(core == 0, earlier[: species // 2], earlier[species // 2 :])
            kept = multiply(scratch, pair, kept, later, False)
        outs[-1][pl.ds(pair, species // 2, stride=pairs), :] = kept


def base_kernel(start, source, diag, upper, side, base):
    planes = start.shape[0]
    vectors = [spread(-start[p]) for p in range(planes)]
    for p in range(planes):
        terms = [
            (reader(diag, p, 0), spread_raw(source[p])),
            (reader(side, 2, p, 0), shifted(vectors[p], True)),
            (reader(side, 3, p, 0), shifted(vectors[p], False)),
        ]
        if p + 1 < planes:
            terms.append((reader(upper, p, 0), vectors[p + 1]))
        base[p] = gather_pairs(apply(terms))


def convert(pairs, sources, outs, scratch):
    size = pairs * LANES // 2
    for source, out in zip(sources, outs):
        for first in range(0, source.shape[0], size):
            diagonals(whole_tiles(source, first, pairs), out, first, scratch, pairs)


def near_kernel(pairs, *refs):
    *refs, scratch = refs
    convert(pairs, refs[: len(refs) // 2], refs[len(refs) // 2 :], scratch)


def far_kernel(pairs, mine, other, out, scratch):
    diagonals(part_tiles(mine, other, pairs), out, 0, scratch, pairs)


def outgoing(offset, partners, here, slots):
    vectors = [offset]
    for level, ref in enumerate(partners):
        passed = mapped(ref, vectors[-1])
        vectors.append(jnp.where((here >> level) & 1 == 0, passed, vectors[-1]))
    place = lax.axis_index("gx")
    for apart in range(slots.shape[0]):
        slots[place ^ apart] = vectors[max(apart.bit_length() - 1, 0)]


def incoming(got, partners, here, reverse):
    count = got.shape[0]
    entering = None
    for level in range(len(partners) + 1)[::-1]:
        total = None
        first = jnp.maximum((here >> level) - 1, 0) << level
        for e in range(1 << level):
            place = first + e
            term = got[count - 1 - place if reverse else place]
            total = term if total is None else total + term
        if entering is not None:
            total = total + mapped(partners[level], entering)
        before = jnp.zeros_like(total) if entering is None else entering
        entering = jnp.where((here >> level) & 1 == 1, total, before)
    return entering


def beside(axis, paired, other):
    place, count = lax.axis_index(axis), lax.axis_size(axis)
    odd = place & 1 == 1
    low = jnp.where(odd, paired, other)
    high = jnp.where(odd, other, paired)
    return jnp.where(place == 0, 0.0, low), jnp.where(place == count - 1, 0.0, high)


def drive_kernel(base, paired, other, ahead, side, upper, drive):
    planes = base.shape[0]
    last = lax.axis_index("gx") == lax.axis_size("gx") - 1
    for p in range(planes):
        low, high = beside("gy", paired[p], other[p])
        terms = [(reader(side, 0, p, 0), spread(low)), (reader(side, 1, p, 0), spread(high))]
        if p + 1 == planes:
            beyond = jnp.where(last, 0.0, ahead[0])
            terms.append((reader(upper, p, 0), spread(beyond)))
        drive[p] = base[p] - gather_pairs(apply(terms))


def forward_offset_kernel(drive, step_maps, *rest):
    *partners, offsets, slots = rest
    planes = drive.shape[0]
    size = drive.shape[1] * LANES // 2
    previous = None
    for p in range(planes):
        fresh = drive[p]
        if previous is not None:
            fresh = fresh - mapped(step_maps, previous, (p - 1) * size)
        offsets[p] = fresh
        previous = fresh
    outgoing(previous, partners, lax.axis_index("gx"), slots)


def forward_kernel(got, drive, offsets, entry_maps, *rest):
    *partners, out, copy, base = rest
    planes = drive.shape[0]
    size = drive.shape[1] * LANES // 2
    entering = incoming(got, partners, lax.axis_index("gx"), False)
    for p in range(planes):
        value = offsets[p] + mapped(entry_maps, entering, p * size)
        base[p] = value - drive[p]
        out[p] = unwoven(value)
        copy[p] = value


def side_kernel(base, vectors, source, diag, side, *rest):
    *rest, scratch = rest
    sources, (out, *converted) = rest[: len(rest) // 2], rest[len(rest) // 2 :]
    planes, pairs = base.shape[:2]
    for p in range(planes):
        vector = spread(-vectors[p])
        around = apply(
            [
                (reader(diag, p, 0), spread_raw(source[p])),
                (reader(side, 2, p, 0), shifted(vector, True)),
                (reader(side, 3, p, 0), shifted(vector, False)),
            ]
        )
        out[p] = base[p] + gather_pairs(around)
    convert(pairs, sources, converted, scratch)


def backward_offset_kernel(base, paired, other, side, step_maps, *rest):
    *partners, offsets, slots = rest
    planes = base.shape[0]
    size = base.shape[1] * LANES // 2
    here = lax.axis_size("gx") - 1 - lax.axis_index("gx")
    previous = None
    for p in range(planes)[::-1]:
        low, high = beside("gy", paired[p], other[p])
        around = apply([(reader(side, 0, p, 0), spread(low)), (reader(side, 1, p, 0), spread(high))])
        fresh = base[p] - gather_pairs(around)
        if previous is not None:
            fresh = fresh - mapped(step_maps, previous, (planes - 2 - p) * size)
        offsets[p] = fresh
        previous = fresh
    outgoing(previous, partners, here, slots)


def backward_kernel(got, offsets, entry_maps, *rest):
    *partners, out = rest
    size = offsets.shape[1] * LANES // 2
    here = lax.axis_size("gx") - 1 - lax.axis_index("gx")
    entering = incoming(got, partners, here, True)
    for p in range(offsets.shape[0]):
        out[p] = unwoven(offsets[p] + mapped(entry_maps, entering, p * size))


def call(kernel, operands, outs, scratch, micros):
    arrays = [o[0] if isinstance(o, tuple) else o for o in operands]
    held = [i for i, o in enumerate(operands) if isinstance(o, tuple)]
    outs = [jax.ShapeDtypeStruct(shape, F32) for shape in outs]
    moved = sum(a.size * a.dtype.itemsize for a in arrays)
    return pl.pallas_call(
        kernel,
        out_shape=outs,
        in_specs=[
            pl.BlockSpec(memory_space=pl.ANY if i in held else pltpu.VMEM) for i in range(len(arrays))
        ],
        out_specs=[pl.BlockSpec(memory_space=pltpu.VMEM) for _ in outs],
        scratch_shapes=[pltpu.VMEM(shape, F32) for shape in scratch],
        compiler_params=pltpu.CompilerParams(vmem_limit_bytes=12 << 20),
        cost_estimate=pl.CostEstimate(
            flops=int(micros * 1.15e9), bytes_accessed=moved, transcendentals=0
        ),
    )(*arrays)


def swaps(block):
    count, rows = lax.axis_size("gx"), lax.axis_size("gy")
    route = []
    for place in range(count):
        for row in range(rows):
            target = row + 1 if row & 1 else row - 1
            to = place * rows + target if 0 <= target < rows else (place ^ 1) * rows + row
            route.append((place * rows + row, to))
    return crossed(block, "gy", 1), lax.ppermute(block, ("gx", "gy"), route)


def crossed(block, axis, distance):
    return lax.ppermute(block, axis, [(i, i ^ distance) for i in range(lax.axis_size(axis))])


def exchange(slots, axis):
    return lax.all_to_all(slots, axis, 0, 0)


def local(start, source, diag_inverse, x_lower, x_upper, side_blocks):
    planes, _, depth, width = x_lower.shape
    species = start.shape[2] // depth
    pairs = depth // 2
    count = lax.axis_size("gx")
    levels = count.bit_length() - 1
    size = species * pairs
    one = (pairs, LANES)
    vec = (planes,) + one
    maps, steps = (planes * size, LANES), ((planes - 1) * size, LANES)
    whole, half = (size, LANES), (size // 2, LANES)
    slots = (count,) + one
    start = start.reshape(vec)
    source = source.reshape(vec)

    def prepare(reverse, blocks, after=None):
        return call(
            functools.partial(prep_kernel, reverse),
            [blocks] + ([(after, None)] if reverse else []),
            [steps, maps, whole],
            [whole, (depth * species // 2, LANES), (depth * species, LANES)],
            1.0,
        )

    def partner_maps(reverse, own, after):
        partners, kept = [], None
        for level in range(levels - 1):
            if level == 0 or reverse:
                got = [crossed(own, "gx", 1 << level)]
            else:
                mine = crossed(kept, "gx", 1 << level)
                got = [mine, crossed(mine, "gx", 1)]
            partners += got
            if level + 2 < levels:
                full = reverse or level + 3 < levels
                weave = level == 0 and not reverse
                outs = call(
                    functools.partial(join_kernel, level, reverse, full, pairs),
                    [own, (after, None)] + ([start] if weave else []) + got,
                    ([whole] if reverse else [whole, half] if full else [half]) + [vec] * weave,
                    [(depth * species, LANES)],
                    0.02,
                )
                if weave:
                    *outs, woven_start = outs
                    partners.append(woven_start)
                own, kept = outs[0], outs[-1]
        return partners

    step_maps, products, own = prepare(False, x_lower)
    upper_steps, upper_products, upper_own = prepare(True, x_upper, products)
    lower = [step_maps, products, *partner_maps(False, own, upper_products)]
    if levels > 2:
        start = lower.pop(3)
    else:
        (start,) = call(weave_kernel, [start], [vec], [], 0.1)
    (base,) = call(
        base_kernel, [start, source, diag_inverse, x_upper, side_blocks], [vec], [], 0.05
    )
    upper = [upper_steps, upper_products, *partner_maps(True, upper_own, upper_products)]
    paired, other = swaps(start)
    ahead = lax.ppermute(start[:1], "gx", [(i, (i - 1) % count) for i in range(count)])

    step_maps, entry_maps, near = call(
        functools.partial(near_kernel, pairs), lower[:3], [steps, maps, whole], [whole], 0.5
    )
    partners = [near]
    for level in range(levels - 2):
        partners += call(
            functools.partial(far_kernel, pairs),
            lower[3 + 2 * level : 5 + 2 * level],
            [whole],
            [whole],
            0.3,
        )
    (drive,) = call(
        drive_kernel, [base, paired, other, ahead, side_blocks, x_upper], [vec], [], 1.0
    )
    offsets, sent = call(
        forward_offset_kernel, [drive, step_maps] + partners, [vec, slots], [], 1.0
    )
    forward, copy, base = call(
        forward_kernel,
        [exchange(sent, "gx"), drive, offsets, entry_maps] + partners,
        [vec, vec, vec],
        [],
        1.0,
    )
    paired, other = swaps(copy)
    base, step_maps, entry_maps, *partners = call(
        side_kernel,
        [base, copy, source, diag_inverse, side_blocks] + upper,
        [vec, steps, maps] + [whole] * (levels - 1),
        [whole],
        0.7,
    )
    offsets, sent = call(
        backward_offset_kernel,
        [base, paired, other, side_blocks, step_maps] + partners,
        [vec, slots],
        [],
        1.5,
    )
    (result,) = call(
        backward_kernel, [exchange(sent, "gx"), offsets, entry_maps] + partners, [vec], [], 1.0
    )
    shape = (planes, 1, depth * species)
    return forward.reshape(shape), result.reshape(shape)


def solution(mesh):
    return jax.shard_map(
        local,
        mesh=mesh,
        in_specs=(
            P("gx", "gy", None),
            P("gx", "gy", None),
            P("gx", "gy", None, None),
            P("gx", "gy", None, None),
            P("gx", "gy", None, None),
            P(None, "gx", "gy", None, None),
        ),
        out_specs=(P("gx", "gy", None), P("gx", "gy", None)),
        check_vma=False,
    )
```

```python
import functools

import jax
import jax.numpy as jnp
from jax import lax
from jax.experimental import pallas as pl
from jax.experimental.pallas import tpu as pltpu
from jax.sharding import PartitionSpec as P

LANES = 128
F32 = jnp.float32
BF16 = jnp.bfloat16


def lane_bit(shape, shift):
    return (lax.broadcasted_iota(jnp.int32, shape, len(shape) - 1) & shift) != 0


def segment_sums(leaf, tiles, rows):
    shape = (rows, LANES)

    def node(base, stride, shift):
        if stride == tiles:
            return leaf(base)
        low = node(base, stride * 2, shift * 2)
        high = node(base + stride, stride * 2, shift * 2)
        low = low + pltpu.roll(low, LANES - shift, 1)
        high = high + pltpu.roll(high, shift, 1)
        return jnp.where(lane_bit(shape, shift), high, low)

    part = node(0, 1, 2)
    odd = lane_bit(shape, 1)
    part = part + jnp.where(odd, pltpu.roll(part, 1, 1), pltpu.roll(part, LANES - 1, 1))
    upper = lane_bit(shape, LANES // 2)
    return jnp.where(upper == odd, part, pltpu.roll(part, LANES // 2, 1))


def apply(terms):
    rows = terms[0][1].shape[0]
    tiles = LANES // 4

    def leaf(t):
        return sum(read(t).astype(F32) * vector for read, vector in terms)

    return segment_sums(leaf, tiles, rows)


def reader(ref, *index):
    return lambda t: ref[(*index, slice(None), slice(t * LANES, (t + 1) * LANES))]


def lanes(shape):
    return lax.broadcasted_iota(jnp.int32, shape, 1)


def woven(raw):
    lane = lanes(raw.shape)
    return jnp.take_along_axis(raw, (lane >> 1) + (lane & 1) * (LANES // 2), 1)


def unwoven(vector):
    lane = lanes(vector.shape)
    return jnp.take_along_axis(vector, (lane & LANES // 2 - 1) * 2 + lane // (LANES // 2), 1)


def spread(vector):
    half = vector.shape[0]
    row = lax.broadcasted_iota(jnp.int32, vector.shape, 0)
    place = (lanes(vector.shape) & LANES // 2 - 1) * 2 + (row & 1)
    parts = []
    for first in (0, half // 2):
        block = jnp.take_along_axis(vector, first + row // 2, 0)
        parts.append(jnp.take_along_axis(block, place, 1))
    return jnp.concatenate(parts, 0)


def spread_raw(raw):
    half = raw.shape[0]
    row = lax.broadcasted_iota(jnp.int32, raw.shape, 0)
    same = (row & 1 == 1) == lane_bit(raw.shape, LANES // 2)
    parts = []
    for first in (0, half // 2):
        block = jnp.take_along_axis(raw, first + row // 2, 0)
        parts.append(jnp.where(same, block, pltpu.roll(block, LANES // 2, 1)))
    return jnp.concatenate(parts, 0)


def gather_pairs(vector):
    half = vector.shape[0] // 2
    shape = (half, LANES)
    row = lax.broadcasted_iota(jnp.int32, shape, 0)
    odd = lane_bit(shape, 1)
    parts = []
    for block in (vector[:half], vector[half:]):
        block = jnp.take_along_axis(block, lanes(shape) >> 1, 1)
        block = jnp.where(odd, pltpu.roll(block, half - 1, 0), block)
        parts.append(jnp.take_along_axis(block, 2 * row & half - 1, 0))
    return jnp.where(row < half // 2, parts[0], parts[1])


def shifted(vector, down):
    rows = vector.shape[0]
    row = lax.broadcasted_iota(jnp.int32, vector.shape, 0)
    if down:
        return jnp.where(row == 0, 0.0, pltpu.roll(vector, 1, 0))
    return jnp.where(row == rows - 1, 0.0, pltpu.roll(vector, rows - 1, 0))


def to_rows(scratch, native, read, rows, species):
    pairs = rows // 2
    for t in range(species // 2):
        native[t * rows : (t + 1) * rows, :] = read(t).astype(F32)
    for t in range(species // 2):
        for inner in (0, 1):
            tile = native[pl.ds(t * rows + inner, pairs, stride=2), :]
            other = pltpu.roll(tile, LANES // 2, 1)
            scratch[pl.ds(4 * t + inner, pairs, stride=LANES), :] = tile
            scratch[pl.ds(4 * t + 2 + inner, pairs, stride=LANES), :] = other


def halves(a):
    high = a.astype(BF16)
    return high, (a - high.astype(F32)).astype(BF16)


def dot(a, b, dims=((1,), (0,))):
    return lax.dot_general(a, b, (dims, ((), ())), preferred_element_type=F32)


def turn(scratch, out, first, pairs, species):
    unit = (
        lax.broadcasted_iota(jnp.int32, (species, species), 0)
        == lax.broadcasted_iota(jnp.int32, (species, species), 1)
    ).astype(F32).astype(BF16)
    for pair in range(pairs):
        block = scratch[pair * LANES : (pair + 1) * LANES, :species].astype(BF16)
        out[pl.ds(first + pair, species, stride=pairs), :] = dot(unit, block, ((1,), (1,)))


def both(scratch, pair, block):
    odd = lane_bit(block.shape, 1)
    zero = jnp.zeros_like(block)
    scratch[pl.ds(pair * LANES, block.shape[0], stride=2), :] = jnp.where(odd, zero, block)
    scratch[pl.ds(pair * LANES + 1, block.shape[0], stride=2), :] = jnp.where(odd, block, zero)
    return scratch[pair * LANES : (pair + 1) * LANES, :]


def multiply(scratch, pair, earlier, later, exact):
    later = both(scratch, pair, later)
    if exact:
        return dot(earlier.astype(BF16), later.astype(BF16))
    earlier_high, earlier_low = halves(earlier)
    high, low = halves(later)
    return dot(earlier_high, high) + (dot(earlier_low, high) + dot(earlier_high, low))


STEP = 8


def diagonals(load, out, first, scratch, pairs):
    count = LANES // 2
    shape = (pairs, LANES)
    giants = count // STEP

    def slid(tiles, shift, mask):
        here = lane_bit(shape, mask)
        return [jnp.where(here, b, a) for a, b in zip(tiles, tiles[shift:] + tiles[:shift])]

    for small in range(STEP):
        tiles = [load(small + STEP * giant) for giant in range(giants)]
        shift = 1
        while shift < giants:
            tiles = slid(tiles, shift, 2 * STEP * shift)
            shift *= 2
        for giant, tile in enumerate(tiles):
            at = (small + STEP * giant) * pairs
            scratch[at : at + pairs, :] = tile
    for giant in range(giants):
        tiles = []
        for j in range(2 * STEP - 1):
            at = (giant * STEP + j) % count * pairs
            tiles.append(scratch[at : at + pairs, :])
        shift = 1
        while shift < STEP:
            tiles = slid(tiles, shift, 2 * shift)[:-shift]
            shift *= 2
        for j, tile in enumerate(tiles):
            at = first + (giant * STEP + j) * pairs
            turn_by = 2 * STEP * giant
            out[at : at + pairs, :] = pltpu.roll(tile, turn_by, 1) if giant else tile


def whole_tiles(ref, first, pairs):
    return lambda b: ref[first + b * pairs : first + (b + 1) * pairs, :]


def part_tiles(mine, other, pairs):
    first_core = lax.axis_index("gx") & 1 == 0

    def load(b):
        low, at = b < LANES // 4, b % (LANES // 4) * pairs
        own, far = mine[at : at + pairs, :], other[at : at + pairs, :]
        return jnp.where(first_core, own if low else far, far if low else own)

    return load


def mapped(ref, vector, first=0):
    pairs = vector.shape[0]
    turns = [vector] + [pltpu.roll(vector, LANES - 2 * j, 1) for j in range(1, STEP)]
    total = None
    for giant in range(LANES // 2 // STEP):
        terms = []
        for j in range(STEP):
            at = first + (giant * STEP + j) * pairs
            terms.append(ref[at : at + pairs, :] * turns[j])
        while len(terms) > 1:
            terms = [a + b for a, b in zip(terms[::2], terms[1::2])]
        part = pltpu.roll(terms[0], LANES - 2 * STEP * giant, 1) if giant else terms[0]
        total = part if total is None else total + part
    return total


def prep_kernel(reverse, blocks, *refs):
    steps, products, own, maps, native, rows_scratch = refs[1:] if reverse else refs
    planes, _, rows, width = blocks.shape
    species = LANES // 2
    pairs = rows // 2
    size = species * pairs
    order = list(range(planes))[::-1] if reverse else list(range(planes))
    for step, plane in enumerate(order):
        at = pl.ds(plane * size, size)
        to_rows(rows_scratch, native, reader(blocks, plane, 0), rows, species)
        turn(rows_scratch, maps, 0, pairs, species)
        if step == 0:
            products[at, :] = -maps[...]
            continue
        steps[pl.ds((step - 1) * size, size), :] = maps[...]
        for pair in range(pairs):
            here = pl.ds(plane * size + pair, species, stride=pairs)
            before = pl.ds(order[step - 1] * size + pair, species, stride=pairs)
            later = -maps[pl.ds(pair, species, stride=pairs), :]
            products[here, :] = multiply(rows_scratch, pair, products[before, :], later, step == 1)
    own[...] = products[pl.ds(order[-1] * size, size), :]


def weave_kernel(start, passed):
    for p in range(start.shape[0]):
        passed[p] = woven(start[p])


def join_kernel(level, reverse, full, pairs, own, *refs):
    here = (lax.axis_index("gx") >> level) & 1
    core = lax.axis_index("gx") & 1
    species = LANES // 2
    _, *refs, scratch = refs
    if level == 0 and not reverse:
        start, *refs, passed = refs
        weave_kernel(start, passed)
    outs = refs[-2:] if full and not reverse else refs[-1:]
    partner = refs[: len(refs) - len(outs)]
    later_is_own = here == (0 if reverse else 1)
    for pair in range(pairs):
        mine = own[pl.ds(pair, species, stride=pairs), :]
        if len(partner) == 1:
            theirs = partner[0][pl.ds(pair, species, stride=pairs), :]
        else:
            close = partner[0][pl.ds(pair, species // 2, stride=pairs), :]
            far = partner[1][pl.ds(pair, species // 2, stride=pairs), :]
            theirs = jnp.where(
                core == 0, jnp.concatenate([close, far], 0), jnp.concatenate([far, close], 0)
            )
        earlier = jnp.where(later_is_own, theirs, mine)
        later = jnp.where(later_is_own, mine, theirs)
        if full:
            kept = multiply(scratch, pair, earlier, later, False)
            outs[0][pl.ds(pair, species, stride=pairs), :] = kept
            if reverse:
                continue
            kept = jnp.where(core == 0, kept[: species // 2], kept[species // 2 :])
        else:
            kept = jnp.where(core == 0, earlier[: species // 2], earlier[species // 2 :])
            kept = multiply(scratch, pair, kept, later, False)
        outs[-1][pl.ds(pair, species // 2, stride=pairs), :] = kept


def base_kernel(start, source, diag, upper, side, base):
    planes = start.shape[0]
    vectors = [spread(-start[p]) for p in range(planes)]
    for p in range(planes):
        terms = [
            (reader(diag, p, 0), spread_raw(source[p])),
            (reader(side, 2, p, 0), shifted(vectors[p], True)),
            (reader(side, 3, p, 0), shifted(vectors[p], False)),
        ]
        if p + 1 < planes:
            terms.append((reader(upper, p, 0), vectors[p + 1]))
        base[p] = gather_pairs(apply(terms))


def convert(pairs, sources, outs, scratch):
    size = pairs * LANES // 2
    for source, out in zip(sources, outs):
        for first in range(0, source.shape[0], size):
            diagonals(whole_tiles(source, first, pairs), out, first, scratch, pairs)


def near_kernel(pairs, *refs):
    *refs, scratch = refs
    convert(pairs, refs[: len(refs) // 2], refs[len(refs) // 2 :], scratch)


def far_kernel(pairs, mine, other, out, scratch):
    diagonals(part_tiles(mine, other, pairs), out, 0, scratch, pairs)


def outgoing(offset, partners, here, slots):
    vectors = [offset]
    for level, ref in enumerate(partners):
        passed = mapped(ref, vectors[-1])
        vectors.append(jnp.where((here >> level) & 1 == 0, passed, vectors[-1]))
    place = lax.axis_index("gx")
    for apart in range(slots.shape[0]):
        slots[place ^ apart] = vectors[max(apart.bit_length() - 1, 0)]


def incoming(got, partners, here, reverse):
    count = got.shape[0]
    entering = None
    for level in range(len(partners) + 1)[::-1]:
        total = None
        first = jnp.maximum((here >> level) - 1, 0) << level
        for e in range(1 << level):
            place = first + e
            term = got[count - 1 - place if reverse else place]
            total = term if total is None else total + term
        if entering is not None:
            total = total + mapped(partners[level], entering)
        before = jnp.zeros_like(total) if entering is None else entering
        entering = jnp.where((here >> level) & 1 == 1, total, before)
    return entering


def beside(axis, paired, other):
    place, count = lax.axis_index(axis), lax.axis_size(axis)
    odd = place & 1 == 1
    low = jnp.where(odd, paired, other)
    high = jnp.where(odd, other, paired)
    return jnp.where(place == 0, 0.0, low), jnp.where(place == count - 1, 0.0, high)


def drive_kernel(base, paired, other, ahead, side, upper, drive):
    planes = base.shape[0]
    last = lax.axis_index("gx") == lax.axis_size("gx") - 1
    for p in range(planes):
        low, high = beside("gy", paired[p], other[p])
        terms = [(reader(side, 0, p, 0), spread(low)), (reader(side, 1, p, 0), spread(high))]
        if p + 1 == planes:
            beyond = jnp.where(last, 0.0, ahead[0])
            terms.append((reader(upper, p, 0), spread(beyond)))
        drive[p] = base[p] - gather_pairs(apply(terms))


def forward_offset_kernel(drive, step_maps, *rest):
    *partners, offsets, slots = rest
    planes = drive.shape[0]
    size = drive.shape[1] * LANES // 2
    previous = None
    for p in range(planes):
        fresh = drive[p]
        if previous is not None:
            fresh = fresh - mapped(step_maps, previous, (p - 1) * size)
        offsets[p] = fresh
        previous = fresh
    outgoing(previous, partners, lax.axis_index("gx"), slots)


def forward_kernel(got, drive, offsets, entry_maps, *rest):
    *partners, out, copy, base = rest
    planes = drive.shape[0]
    size = drive.shape[1] * LANES // 2
    entering = incoming(got, partners, lax.axis_index("gx"), False)
    for p in range(planes):
        value = offsets[p] + mapped(entry_maps, entering, p * size)
        base[p] = value - drive[p]
        out[p] = unwoven(value)
        copy[p] = value


def side_kernel(base, vectors, source, diag, side, *rest):
    *rest, scratch = rest
    sources, (out, *converted) = rest[: len(rest) // 2], rest[len(rest) // 2 :]
    planes, pairs = base.shape[:2]
    for p in range(planes):
        vector = spread(-vectors[p])
        around = apply(
            [
                (reader(diag, p, 0), spread_raw(source[p])),
                (reader(side, 2, p, 0), shifted(vector, True)),
                (reader(side, 3, p, 0), shifted(vector, False)),
            ]
        )
        out[p] = base[p] + gather_pairs(around)
    convert(pairs, sources, converted, scratch)


def backward_offset_kernel(base, paired, other, side, step_maps, *rest):
    *partners, offsets, slots = rest
    planes = base.shape[0]
    size = base.shape[1] * LANES // 2
    here = lax.axis_size("gx") - 1 - lax.axis_index("gx")
    previous = None
    for p in range(planes)[::-1]:
        low, high = beside("gy", paired[p], other[p])
        around = apply([(reader(side, 0, p, 0), spread(low)), (reader(side, 1, p, 0), spread(high))])
        fresh = base[p] - gather_pairs(around)
        if previous is not None:
            fresh = fresh - mapped(step_maps, previous, (planes - 2 - p) * size)
        offsets[p] = fresh
        previous = fresh
    outgoing(previous, partners, here, slots)


def backward_kernel(got, offsets, entry_maps, *rest):
    *partners, out = rest
    size = offsets.shape[1] * LANES // 2
    here = lax.axis_size("gx") - 1 - lax.axis_index("gx")
    entering = incoming(got, partners, here, True)
    for p in range(offsets.shape[0]):
        out[p] = unwoven(offsets[p] + mapped(entry_maps, entering, p * size))


def call(kernel, operands, outs, scratch, micros):
    arrays = [o[0] if isinstance(o, tuple) else o for o in operands]
    held = [i for i, o in enumerate(operands) if isinstance(o, tuple)]
    outs = [jax.ShapeDtypeStruct(shape, F32) for shape in outs]
    moved = sum(a.size * a.dtype.itemsize for a in arrays)
    return pl.pallas_call(
        kernel,
        out_shape=outs,
        in_specs=[
            pl.BlockSpec(memory_space=pl.ANY if i in held else pltpu.VMEM) for i in range(len(arrays))
        ],
        out_specs=[pl.BlockSpec(memory_space=pltpu.VMEM) for _ in outs],
        scratch_shapes=[pltpu.VMEM(shape, F32) for shape in scratch],
        compiler_params=pltpu.CompilerParams(vmem_limit_bytes=12 << 20),
        cost_estimate=pl.CostEstimate(
            flops=int(micros * 1.15e9), bytes_accessed=moved, transcendentals=0
        ),
    )(*arrays)


def swaps(block):
    count, rows = lax.axis_size("gx"), lax.axis_size("gy")
    route = []
    for place in range(count):
        for row in range(rows):
            target = row + 1 if row & 1 else row - 1
            to = place * rows + target if 0 <= target < rows else (place ^ 1) * rows + row
            route.append((place * rows + row, to))
    return crossed(block, "gy", 1), lax.ppermute(block, ("gx", "gy"), route)


def crossed(block, axis, distance):
    return lax.ppermute(block, axis, [(i, i ^ distance) for i in range(lax.axis_size(axis))])


def exchange(slots, axis):
    return lax.all_to_all(slots, axis, 0, 0)


def local(start, source, diag_inverse, x_lower, x_upper, side_blocks):
    planes, _, depth, width = x_lower.shape
    species = start.shape[2] // depth
    pairs = depth // 2
    count = lax.axis_size("gx")
    levels = count.bit_length() - 1
    size = species * pairs
    one = (pairs, LANES)
    vec = (planes,) + one
    maps, steps = (planes * size, LANES), ((planes - 1) * size, LANES)
    whole, half = (size, LANES), (size // 2, LANES)
    slots = (count,) + one
    start = start.reshape(vec)
    source = source.reshape(vec)

    def prepare(reverse, blocks, after=None):
        return call(
            functools.partial(prep_kernel, reverse),
            [blocks] + ([(after, None)] if reverse else []),
            [steps, maps, whole],
            [whole, (depth * species // 2, LANES), (depth * species, LANES)],
            1.0,
        )

    def partner_maps(reverse, own, after):
        partners, kept = [], None
        for level in range(levels - 1):
            if level == 0 or reverse:
                got = [crossed(own, "gx", 1 << level)]
            else:
                mine = crossed(kept, "gx", 1 << level)
                got = [mine, crossed(mine, "gx", 1)]
            partners += got
            if level + 2 < levels:
                full = reverse or level + 3 < levels
                weave = level == 0 and not reverse
                outs = call(
                    functools.partial(join_kernel, level, reverse, full, pairs),
                    [own, (after, None)] + ([start] if weave else []) + got,
                    ([whole] if reverse else [whole, half] if full else [half]) + [vec] * weave,
                    [(depth * species, LANES)],
                    0.02,
                )
                if weave:
                    *outs, woven_start = outs
                    partners.append(woven_start)
                own, kept = outs[0], outs[-1]
        return partners

    step_maps, products, own = prepare(False, x_lower)
    upper_steps, upper_products, upper_own = prepare(True, x_upper, products)
    lower = [step_maps, products, *partner_maps(False, own, upper_products)]
    if levels > 2:
        start = lower.pop(3)
    else:
        (start,) = call(weave_kernel, [start], [vec], [], 0.1)
    (base,) = call(
        base_kernel, [start, source, diag_inverse, x_upper, side_blocks], [vec], [], 0.02
    )
    upper = [upper_steps, upper_products, *partner_maps(True, upper_own, upper_products)]
    paired, other = swaps(start)
    ahead = lax.ppermute(start[:1], "gx", [(i, (i - 1) % count) for i in range(count)])

    step_maps, entry_maps, near = call(
        functools.partial(near_kernel, pairs), lower[:3], [steps, maps, whole], [whole], 0.1
    )
    partners = [near]
    for level in range(levels - 2):
        partners += call(
            functools.partial(far_kernel, pairs),
            lower[3 + 2 * level : 5 + 2 * level],
            [whole],
            [whole],
            0.1,
        )
    (drive,) = call(
        drive_kernel, [base, paired, other, ahead, side_blocks, x_upper], [vec], [], 1.2
    )
    offsets, sent = call(
        forward_offset_kernel, [drive, step_maps] + partners, [vec, slots], [], 1.0
    )
    forward, copy, base = call(
        forward_kernel,
        [exchange(sent, "gx"), drive, offsets, entry_maps] + partners,
        [vec, vec, vec],
        [],
        1.0,
    )
    paired, other = swaps(copy)
    base, step_maps, entry_maps, *partners = call(
        side_kernel,
        [base, copy, source, diag_inverse, side_blocks] + upper,
        [vec, steps, maps] + [whole] * (levels - 1),
        [whole],
        0.7,
    )
    offsets, sent = call(
        backward_offset_kernel,
        [base, paired, other, side_blocks, step_maps] + partners,
        [vec, slots],
        [],
        1.5,
    )
    (result,) = call(
        backward_kernel, [exchange(sent, "gx"), offsets, entry_maps] + partners, [vec], [], 1.0
    )
    shape = (planes, 1, depth * species)
    return forward.reshape(shape), result.reshape(shape)


def solution(mesh):
    return jax.shard_map(
        local,
        mesh=mesh,
        in_specs=(
            P("gx", "gy", None),
            P("gx", "gy", None),
            P("gx", "gy", None, None),
            P("gx", "gy", None, None),
            P("gx", "gy", None, None),
            P(None, "gx", "gy", None, None),
        ),
        out_specs=(P("gx", "gy", None), P("gx", "gy", None)),
        check_vma=False,
    )
```

```python
import functools

import jax
import jax.numpy as jnp
from jax import lax
from jax.experimental import pallas as pl
from jax.experimental.pallas import tpu as pltpu
from jax.sharding import PartitionSpec as P

LANES = 128
F32 = jnp.float32
BF16 = jnp.bfloat16


def lane_bit(shape, shift):
    return (lax.broadcasted_iota(jnp.int32, shape, len(shape) - 1) & shift) != 0


def segment_sums(leaf, tiles, rows):
    shape = (rows, LANES)

    def node(base, stride, shift):
        if stride == tiles:
            return leaf(base)
        low = node(base, stride * 2, shift * 2)
        high = node(base + stride, stride * 2, shift * 2)
        low = low + pltpu.roll(low, LANES - shift, 1)
        high = high + pltpu.roll(high, shift, 1)
        return jnp.where(lane_bit(shape, shift), high, low)

    part = node(0, 1, 2)
    odd = lane_bit(shape, 1)
    part = part + jnp.where(odd, pltpu.roll(part, 1, 1), pltpu.roll(part, LANES - 1, 1))
    upper = lane_bit(shape, LANES // 2)
    return jnp.where(upper == odd, part, pltpu.roll(part, LANES // 2, 1))


def apply(terms):
    rows = terms[0][1].shape[0]
    tiles = LANES // 4

    def leaf(t):
        return sum(read(t).astype(F32) * vector for read, vector in terms)

    return segment_sums(leaf, tiles, rows)


def reader(ref, *index):
    return lambda t: ref[(*index, slice(None), slice(t * LANES, (t + 1) * LANES))]


def lanes(shape):
    return lax.broadcasted_iota(jnp.int32, shape, 1)


def woven(raw):
    lane = lanes(raw.shape)
    return jnp.take_along_axis(raw, (lane >> 1) + (lane & 1) * (LANES // 2), 1)


def unwoven(vector):
    lane = lanes(vector.shape)
    return jnp.take_along_axis(vector, (lane & LANES // 2 - 1) * 2 + lane // (LANES // 2), 1)


def spread(vector):
    half = vector.shape[0]
    row = lax.broadcasted_iota(jnp.int32, vector.shape, 0)
    place = (lanes(vector.shape) & LANES // 2 - 1) * 2 + (row & 1)
    parts = []
    for first in (0, half // 2):
        block = jnp.take_along_axis(vector, first + row // 2, 0)
        parts.append(jnp.take_along_axis(block, place, 1))
    return jnp.concatenate(parts, 0)


def spread_raw(raw):
    half = raw.shape[0]
    row = lax.broadcasted_iota(jnp.int32, raw.shape, 0)
    same = (row & 1 == 1) == lane_bit(raw.shape, LANES // 2)
    parts = []
    for first in (0, half // 2):
        block = jnp.take_along_axis(raw, first + row // 2, 0)
        parts.append(jnp.where(same, block, pltpu.roll(block, LANES // 2, 1)))
    return jnp.concatenate(parts, 0)


def gather_pairs(vector):
    half = vector.shape[0] // 2
    shape = (half, LANES)
    row = lax.broadcasted_iota(jnp.int32, shape, 0)
    odd = lane_bit(shape, 1)
    parts = []
    for block in (vector[:half], vector[half:]):
        block = jnp.take_along_axis(block, lanes(shape) >> 1, 1)
        block = jnp.where(odd, pltpu.roll(block, half - 1, 0), block)
        parts.append(jnp.take_along_axis(block, 2 * row & half - 1, 0))
    return jnp.where(row < half // 2, parts[0], parts[1])


def shifted(vector, down):
    rows = vector.shape[0]
    row = lax.broadcasted_iota(jnp.int32, vector.shape, 0)
    if down:
        return jnp.where(row == 0, 0.0, pltpu.roll(vector, 1, 0))
    return jnp.where(row == rows - 1, 0.0, pltpu.roll(vector, rows - 1, 0))


def to_rows(scratch, native, read, rows, species):
    pairs = rows // 2
    for t in range(species // 2):
        native[t * rows : (t + 1) * rows, :] = read(t).astype(F32)
    for t in range(species // 2):
        for inner in (0, 1):
            tile = native[pl.ds(t * rows + inner, pairs, stride=2), :]
            other = pltpu.roll(tile, LANES // 2, 1)
            scratch[pl.ds(4 * t + inner, pairs, stride=LANES), :] = tile
            scratch[pl.ds(4 * t + 2 + inner, pairs, stride=LANES), :] = other


def halves(a):
    high = a.astype(BF16)
    return high, (a - high.astype(F32)).astype(BF16)


def dot(a, b, dims=((1,), (0,))):
    return lax.dot_general(a, b, (dims, ((), ())), preferred_element_type=F32)


def turn(scratch, out, first, pairs, species):
    unit = (
        lax.broadcasted_iota(jnp.int32, (species, species), 0)
        == lax.broadcasted_iota(jnp.int32, (species, species), 1)
    ).astype(F32).astype(BF16)
    for pair in range(pairs):
        block = scratch[pair * LANES : (pair + 1) * LANES, :species].astype(BF16)
        out[pl.ds(first + pair, species, stride=pairs), :] = dot(unit, block, ((1,), (1,)))


def both(scratch, pair, block):
    odd = lane_bit(block.shape, 1)
    zero = jnp.zeros_like(block)
    scratch[pl.ds(pair * LANES, block.shape[0], stride=2), :] = jnp.where(odd, zero, block)
    scratch[pl.ds(pair * LANES + 1, block.shape[0], stride=2), :] = jnp.where(odd, block, zero)
    return scratch[pair * LANES : (pair + 1) * LANES, :]


def multiply(scratch, pair, earlier, later, exact):
    later = both(scratch, pair, later)
    if exact:
        return dot(earlier.astype(BF16), later.astype(BF16))
    earlier_high, earlier_low = halves(earlier)
    high, low = halves(later)
    return dot(earlier_high, high) + (dot(earlier_low, high) + dot(earlier_high, low))


STEP = 8


def diagonals(load, out, first, scratch, pairs):
    count = LANES // 2
    shape = (pairs, LANES)
    giants = count // STEP

    def slid(tiles, shift, mask):
        here = lane_bit(shape, mask)
        return [jnp.where(here, b, a) for a, b in zip(tiles, tiles[shift:] + tiles[:shift])]

    for small in range(STEP):
        tiles = [load(small + STEP * giant) for giant in range(giants)]
        shift = 1
        while shift < giants:
            tiles = slid(tiles, shift, 2 * STEP * shift)
            shift *= 2
        for giant, tile in enumerate(tiles):
            at = (small + STEP * giant) * pairs
            scratch[at : at + pairs, :] = tile
    for giant in range(giants):
        tiles = []
        for j in range(2 * STEP - 1):
            at = (giant * STEP + j) % count * pairs
            tiles.append(scratch[at : at + pairs, :])
        shift = 1
        while shift < STEP:
            tiles = slid(tiles, shift, 2 * shift)[:-shift]
            shift *= 2
        for j, tile in enumerate(tiles):
            at = first + (giant * STEP + j) * pairs
            turn_by = 2 * STEP * giant
            out[at : at + pairs, :] = pltpu.roll(tile, turn_by, 1) if giant else tile


def whole_tiles(ref, first, pairs):
    return lambda b: ref[first + b * pairs : first + (b + 1) * pairs, :]


def part_tiles(mine, other, pairs):
    first_core = lax.axis_index("gx") & 1 == 0

    def load(b):
        low, at = b < LANES // 4, b % (LANES // 4) * pairs
        own, far = mine[at : at + pairs, :], other[at : at + pairs, :]
        return jnp.where(first_core, own if low else far, far if low else own)

    return load


def mapped(ref, vector, first=0):
    pairs = vector.shape[0]
    turns = [vector] + [pltpu.roll(vector, LANES - 2 * j, 1) for j in range(1, STEP)]
    total = None
    for giant in range(LANES // 2 // STEP):
        terms = []
        for j in range(STEP):
            at = first + (giant * STEP + j) * pairs
            terms.append(ref[at : at + pairs, :] * turns[j])
        while len(terms) > 1:
            terms = [a + b for a, b in zip(terms[::2], terms[1::2])]
        part = pltpu.roll(terms[0], LANES - 2 * STEP * giant, 1) if giant else terms[0]
        total = part if total is None else total + part
    return total


def prep_kernel(reverse, blocks, *refs):
    steps, products, own, maps, native, rows_scratch = refs[1:] if reverse else refs
    planes, _, rows, width = blocks.shape
    species = LANES // 2
    pairs = rows // 2
    size = species * pairs
    order = list(range(planes))[::-1] if reverse else list(range(planes))
    for step, plane in enumerate(order):
        at = pl.ds(plane * size, size)
        to_rows(rows_scratch, native, reader(blocks, plane, 0), rows, species)
        turn(rows_scratch, maps, 0, pairs, species)
        if step == 0:
            products[at, :] = -maps[...]
            continue
        steps[pl.ds((step - 1) * size, size), :] = maps[...]
        for pair in range(pairs):
            here = pl.ds(plane * size + pair, species, stride=pairs)
            before = pl.ds(order[step - 1] * size + pair, species, stride=pairs)
            later = -maps[pl.ds(pair, species, stride=pairs), :]
            products[here, :] = multiply(rows_scratch, pair, products[before, :], later, step == 1)
    own[...] = products[pl.ds(order[-1] * size, size), :]


def weave_kernel(start, passed):
    for p in range(start.shape[0]):
        passed[p] = woven(start[p])


def join_kernel(level, reverse, full, pairs, own, *refs):
    here = (lax.axis_index("gx") >> level) & 1
    core = lax.axis_index("gx") & 1
    species = LANES // 2
    _, *refs, scratch = refs
    if level == 0 and not reverse:
        start, *refs, passed = refs
        weave_kernel(start, passed)
    outs = refs[-2:] if full and not reverse else refs[-1:]
    partner = refs[: len(refs) - len(outs)]
    later_is_own = here == (0 if reverse else 1)
    for pair in range(pairs):
        mine = own[pl.ds(pair, species, stride=pairs), :]
        if len(partner) == 1:
            theirs = partner[0][pl.ds(pair, species, stride=pairs), :]
        else:
            close = partner[0][pl.ds(pair, species // 2, stride=pairs), :]
            far = partner[1][pl.ds(pair, species // 2, stride=pairs), :]
            theirs = jnp.where(
                core == 0, jnp.concatenate([close, far], 0), jnp.concatenate([far, close], 0)
            )
        earlier = jnp.where(later_is_own, theirs, mine)
        later = jnp.where(later_is_own, mine, theirs)
        if full:
            kept = multiply(scratch, pair, earlier, later, False)
            outs[0][pl.ds(pair, species, stride=pairs), :] = kept
            if reverse:
                continue
            kept = jnp.where(core == 0, kept[: species // 2], kept[species // 2 :])
        else:
            kept = jnp.where(core == 0, earlier[: species // 2], earlier[species // 2 :])
            kept = multiply(scratch, pair, kept, later, False)
        outs[-1][pl.ds(pair, species // 2, stride=pairs), :] = kept


def base_kernel(start, source, diag, upper, side, base):
    planes = start.shape[0]
    vectors = [spread(-start[p]) for p in range(planes)]
    for p in range(planes):
        terms = [
            (reader(diag, p, 0), spread_raw(source[p])),
            (reader(side, 2, p, 0), shifted(vectors[p], True)),
            (reader(side, 3, p, 0), shifted(vectors[p], False)),
        ]
        if p + 1 < planes:
            terms.append((reader(upper, p, 0), vectors[p + 1]))
        base[p] = gather_pairs(apply(terms))


def convert(pairs, sources, outs, scratch):
    size = pairs * LANES // 2
    for source, out in zip(sources, outs):
        for first in range(0, source.shape[0], size):
            diagonals(whole_tiles(source, first, pairs), out, first, scratch, pairs)


def near_kernel(pairs, *refs):
    *refs, scratch = refs
    convert(pairs, refs[: len(refs) // 2], refs[len(refs) // 2 :], scratch)


def outgoing(offset, partners, here, slots):
    vectors = [offset]
    for level, ref in enumerate(partners):
        passed = mapped(ref, vectors[-1])
        vectors.append(jnp.where((here >> level) & 1 == 0, passed, vectors[-1]))
    place = lax.axis_index("gx")
    for apart in range(slots.shape[0]):
        slots[place ^ apart] = vectors[max(apart.bit_length() - 1, 0)]


def incoming(got, partners, here, reverse):
    count = got.shape[0]
    entering = None
    for level in range(len(partners) + 1)[::-1]:
        total = None
        first = jnp.maximum((here >> level) - 1, 0) << level
        for e in range(1 << level):
            place = first + e
            term = got[count - 1 - place if reverse else place]
            total = term if total is None else total + term
        if entering is not None:
            total = total + mapped(partners[level], entering)
        before = jnp.zeros_like(total) if entering is None else entering
        entering = jnp.where((here >> level) & 1 == 1, total, before)
    return entering


def beside(axis, paired, other):
    place, count = lax.axis_index(axis), lax.axis_size(axis)
    odd = place & 1 == 1
    low = jnp.where(odd, paired, other)
    high = jnp.where(odd, other, paired)
    return jnp.where(place == 0, 0.0, low), jnp.where(place == count - 1, 0.0, high)


def drive_kernel(base, paired, other, ahead, side, upper, drive):
    planes = base.shape[0]
    last = lax.axis_index("gx") == lax.axis_size("gx") - 1
    for p in range(planes):
        low, high = beside("gy", paired[p], other[p])
        terms = [(reader(side, 0, p, 0), spread(low)), (reader(side, 1, p, 0), spread(high))]
        if p + 1 == planes:
            beyond = jnp.where(last, 0.0, ahead[0])
            terms.append((reader(upper, p, 0), spread(beyond)))
        drive[p] = base[p] - gather_pairs(apply(terms))


def forward_offset_kernel(levels, drive, step_maps, near, *rest):
    parts, (offsets, slots, *far, scratch) = rest[: 2 * (levels - 2)], rest[2 * (levels - 2) :]
    planes, pairs = drive.shape[:2]
    size = pairs * LANES // 2
    for level, ref in enumerate(far):
        diagonals(part_tiles(*parts[2 * level : 2 * level + 2], pairs), ref, 0, scratch, pairs)
    previous = None
    for p in range(planes):
        fresh = drive[p]
        if previous is not None:
            fresh = fresh - mapped(step_maps, previous, (p - 1) * size)
        offsets[p] = fresh
        previous = fresh
    outgoing(previous, [near, *far], lax.axis_index("gx"), slots)


def forward_kernel(got, drive, offsets, entry_maps, *rest):
    *partners, out, copy, base = rest
    planes = drive.shape[0]
    size = drive.shape[1] * LANES // 2
    entering = incoming(got, partners, lax.axis_index("gx"), False)
    for p in range(planes):
        value = offsets[p] + mapped(entry_maps, entering, p * size)
        base[p] = value - drive[p]
        out[p] = unwoven(value)
        copy[p] = value


def side_kernel(base, vectors, source, diag, side, *rest):
    *rest, scratch = rest
    sources, (out, *converted) = rest[: len(rest) // 2], rest[len(rest) // 2 :]
    planes, pairs = base.shape[:2]
    for p in range(planes):
        vector = spread(-vectors[p])
        around = apply(
            [
                (reader(diag, p, 0), spread_raw(source[p])),
                (reader(side, 2, p, 0), shifted(vector, True)),
                (reader(side, 3, p, 0), shifted(vector, False)),
            ]
        )
        out[p] = base[p] + gather_pairs(around)
    convert(pairs, sources, converted, scratch)


def backward_offset_kernel(base, paired, other, side, step_maps, *rest):
    *partners, offsets, slots = rest
    planes = base.shape[0]
    size = base.shape[1] * LANES // 2
    here = lax.axis_size("gx") - 1 - lax.axis_index("gx")
    previous = None
    for p in range(planes)[::-1]:
        low, high = beside("gy", paired[p], other[p])
        around = apply([(reader(side, 0, p, 0), spread(low)), (reader(side, 1, p, 0), spread(high))])
        fresh = base[p] - gather_pairs(around)
        if previous is not None:
            fresh = fresh - mapped(step_maps, previous, (planes - 2 - p) * size)
        offsets[p] = fresh
        previous = fresh
    outgoing(previous, partners, here, slots)


def backward_kernel(got, offsets, entry_maps, *rest):
    *partners, out = rest
    size = offsets.shape[1] * LANES // 2
    here = lax.axis_size("gx") - 1 - lax.axis_index("gx")
    entering = incoming(got, partners, here, True)
    for p in range(offsets.shape[0]):
        out[p] = unwoven(offsets[p] + mapped(entry_maps, entering, p * size))


def call(kernel, operands, outs, scratch, micros):
    arrays = [o[0] if isinstance(o, tuple) else o for o in operands]
    held = [i for i, o in enumerate(operands) if isinstance(o, tuple)]
    outs = [jax.ShapeDtypeStruct(shape, F32) for shape in outs]
    moved = sum(a.size * a.dtype.itemsize for a in arrays)
    return pl.pallas_call(
        kernel,
        out_shape=outs,
        in_specs=[
            pl.BlockSpec(memory_space=pl.ANY if i in held else pltpu.VMEM) for i in range(len(arrays))
        ],
        out_specs=[pl.BlockSpec(memory_space=pltpu.VMEM) for _ in outs],
        scratch_shapes=[pltpu.VMEM(shape, F32) for shape in scratch],
        compiler_params=pltpu.CompilerParams(vmem_limit_bytes=12 << 20),
        cost_estimate=pl.CostEstimate(
            flops=int(micros * 1.15e9), bytes_accessed=moved, transcendentals=0
        ),
    )(*arrays)


def swaps(block):
    count, rows = lax.axis_size("gx"), lax.axis_size("gy")
    route = []
    for place in range(count):
        for row in range(rows):
            target = row + 1 if row & 1 else row - 1
            to = place * rows + target if 0 <= target < rows else (place ^ 1) * rows + row
            route.append((place * rows + row, to))
    return crossed(block, "gy", 1), lax.ppermute(block, ("gx", "gy"), route)


def crossed(block, axis, distance):
    return lax.ppermute(block, axis, [(i, i ^ distance) for i in range(lax.axis_size(axis))])


def exchange(slots, axis):
    return lax.all_to_all(slots, axis, 0, 0)


def local(start, source, diag_inverse, x_lower, x_upper, side_blocks):
    planes, _, depth, width = x_lower.shape
    species = start.shape[2] // depth
    pairs = depth // 2
    count = lax.axis_size("gx")
    levels = count.bit_length() - 1
    size = species * pairs
    one = (pairs, LANES)
    vec = (planes,) + one
    maps, steps = (planes * size, LANES), ((planes - 1) * size, LANES)
    whole, half = (size, LANES), (size // 2, LANES)
    slots = (count,) + one
    start = start.reshape(vec)
    source = source.reshape(vec)

    def prepare(reverse, blocks, after=None):
        return call(
            functools.partial(prep_kernel, reverse),
            [blocks] + ([(after, None)] if reverse else []),
            [steps, maps, whole],
            [whole, (depth * species // 2, LANES), (depth * species, LANES)],
            1.0,
        )

    def partner_maps(reverse, own, after):
        partners, kept = [], None
        for level in range(levels - 1):
            if level == 0 or reverse:
                got = [crossed(own, "gx", 1 << level)]
            else:
                mine = crossed(kept, "gx", 1 << level)
                got = [mine, crossed(mine, "gx", 1)]
            partners += got
            if level + 2 < levels:
                full = reverse or level + 3 < levels
                weave = level == 0 and not reverse
                outs = call(
                    functools.partial(join_kernel, level, reverse, full, pairs),
                    [own, (after, None)] + ([start] if weave else []) + got,
                    ([whole] if reverse else [whole, half] if full else [half]) + [vec] * weave,
                    [(depth * species, LANES)],
                    0.02,
                )
                if weave:
                    *outs, woven_start = outs
                    partners.append(woven_start)
                own, kept = outs[0], outs[-1]
        return partners

    step_maps, products, own = prepare(False, x_lower)
    upper_steps, upper_products, upper_own = prepare(True, x_upper, products)
    lower = [step_maps, products, *partner_maps(False, own, upper_products)]
    if levels > 2:
        start = lower.pop(3)
    else:
        (start,) = call(weave_kernel, [start], [vec], [], 0.1)
    (base,) = call(
        base_kernel, [start, source, diag_inverse, x_upper, side_blocks], [vec], [], 0.02
    )
    upper = [upper_steps, upper_products, *partner_maps(True, upper_own, upper_products)]
    paired, other = swaps(start)
    ahead = lax.ppermute(start[:1], "gx", [(i, (i - 1) % count) for i in range(count)])

    step_maps, entry_maps, near = call(
        functools.partial(near_kernel, pairs), lower[:3], [steps, maps, whole], [whole], 0.1
    )
    (drive,) = call(
        drive_kernel, [base, paired, other, ahead, side_blocks, x_upper], [vec], [], 1.2
    )
    offsets, sent, *far = call(
        functools.partial(forward_offset_kernel, levels),
        [drive, step_maps, near] + lower[3:],
        [vec, slots] + [whole] * (levels - 2),
        [whole],
        1.0,
    )
    partners = [near, *far]
    forward, copy, base = call(
        forward_kernel,
        [exchange(sent, "gx"), drive, offsets, entry_maps] + partners,
        [vec, vec, vec],
        [],
        1.0,
    )
    paired, other = swaps(copy)
    base, step_maps, entry_maps, *partners = call(
        side_kernel,
        [base, copy, source, diag_inverse, side_blocks] + upper,
        [vec, steps, maps] + [whole] * (levels - 1),
        [whole],
        0.7,
    )
    offsets, sent = call(
        backward_offset_kernel,
        [base, paired, other, side_blocks, step_maps] + partners,
        [vec, slots],
        [],
        1.5,
    )
    (result,) = call(
        backward_kernel, [exchange(sent, "gx"), offsets, entry_maps] + partners, [vec], [], 1.0
    )
    shape = (planes, 1, depth * species)
    return forward.reshape(shape), result.reshape(shape)


def solution(mesh):
    return jax.shard_map(
        local,
        mesh=mesh,
        in_specs=(
            P("gx", "gy", None),
            P("gx", "gy", None),
            P("gx", "gy", None, None),
            P("gx", "gy", None, None),
            P("gx", "gy", None, None),
            P(None, "gx", "gy", None, None),
        ),
        out_specs=(P("gx", "gy", None), P("gx", "gy", None)),
        check_vma=False,
    )
```
